32 devices in a mesh: tiles: 32 (over z, y, x, core).
Axes of the slice: x: 2, y: 2, z: 4, core: 2. Of those that a mesh axis runs over, the one named last changes fastest.
Arguments:
- fields: bfloat16 [32, 64, 64, 128], P('tiles')
- cotangent: bfloat16 [32, 64, 64, 128], P('tiles'), may hold values from -6 to 6
- ocean_mask: int32 [32, 64, 64], P('tiles'), may hold values from 0 to 1
- neighbours: int32 [32, 8], P('tiles'), may hold values from -1 to 31, as said below
- kernel: float32 [7, 7, 128], replicated, may hold values from -0.875 to 0.875
- conv_bias: float32 [128], replicated, may hold values from -0.5 to 0.5
- ln_gain: float32 [128], replicated, may hold values from 0.5 to 1.5
- ln_bias: float32 [128], replicated, may hold values from -1.5 to 1.5
- weight_in: bfloat16 [128, 512], replicated, may hold values from -0.5 to 0.5
- bias_in: float32 [512], replicated, may hold values from -1.5 to 1.5
- weight_out: bfloat16 [512, 128], replicated, may hold values from -0.25 to 0.25
- bias_out: float32 [128], replicated, may hold values from -1.5 to 1.5
- layer_scale: float32 [128], replicated, may hold values from 0.3 to 1.5
Outputs:
- updated: bfloat16 [32, 64, 64, 128], P('tiles')
- d_fields: float32 [32, 64, 64, 128], P('tiles')
- d_kernel: float32 [7, 7, 128], replicated
- d_conv_bias: float32 [128], replicated
- d_ln_gain: float32 [128], replicated
- d_ln_bias: float32 [128], replicated
- d_weight_in: float32 [128, 512], replicated
- d_bias_in: float32 [512], replicated
- d_weight_out: float32 [512, 128], replicated
- d_bias_out: float32 [128], replicated
- d_layer_scale: float32 [128], replicated
The draws below stay inside these ranges and needn't reach their ends.
Inputs may be any that keep to these rules, and one draw needn't show every extreme that they name: `neighbours`: entries name tiles across the north, south, west, east, north-west, north-east, south-west and south-east sides; the lists are mutual (a tile lists its neighbour on one side and is listed on the opposite one) and follow one grid of tiles (where a tile and its listed neighbour both list a tile, it is the one the grid places there; a tile listed by nobody around it holds no ocean). Every listed tile is held by a device at most 7 indices away along tiles, and some listed tile is exactly 7 away; the index offset of a given side is not the same for all tiles.
All inputs are finite; a program needn't handle non-finite values.
Results may differ from the reference program's by a relative error of at most 0.0062.
Values may be sent and summed in bfloat16 or wider, within the bound.
No kernel may reach another device: no remote copies, remote signals or barrier semaphores. Data moves between devices by JAX's collectives and lax.ppermute only.
A program may use at most 448 MiB of HBM per device.

```python
import math
import jax
import jax.numpy as jnp
from jax import lax

TPD = 1
TILE = 64
C = 128
F = 512
KSIZE = 7
BAND = 4
TILES = 32


def tile_layout(key):
    live_key, order_key = jax.random.split(jax.random.fold_in(key, 7))
    position = jnp.arange(TILES, dtype=jnp.int32)
    grid_row = position // BAND
    grid_col = position % BAND
    grid_rows = TILES // BAND
    first_row = max(TPD // BAND - 1, 0)
    live_tile = jax.random.randint(live_key, (TILES,), 0, 4) > 0
    live_tile = live_tile | (grid_row < 2) | (grid_row >= grid_rows - 2)
    live_tile = live_tile | (grid_row == first_row) | (grid_row == first_row + 1)
    live_tile = live_tile | (position // TPD == TILES // TPD // 2)
    scores = jax.random.randint(order_key, (grid_rows, BAND), 0, 1 << 20) * BAND + jnp.arange(BAND, dtype=jnp.int32)[None, :]
    scores = scores.at[first_row, 0].set(-1)
    scores = scores.at[first_row + 1, 1].set(1 << 23)
    ordering = jnp.argsort(scores, axis=1)
    ranking = jnp.argsort(ordering, axis=1).astype(jnp.int32)
    tile_slot = grid_row * BAND + ranking.reshape(-1)
    return (live_tile, grid_row, grid_col, tile_slot)


def draw_neighbours(key, part):
    live_tile, grid_row, grid_col, tile_slot = tile_layout(key)
    step_row = jnp.array([-1, 1, 0, 0, -1, -1, 1, 1], jnp.int32)
    step_col = jnp.array([0, 0, -1, 1, -1, 1, -1, 1], jnp.int32)
    target_row = grid_row[:, None] + step_row[None, :]
    target_col = grid_col[:, None] + step_col[None, :]
    inside = (target_row >= 0) & (target_row < TILES // BAND) & (target_col >= 0) & (target_col < BAND)
    target = jnp.where(inside, target_row * BAND + target_col, 0)
    usable = inside & live_tile[target] & live_tile[:, None]
    listing = jnp.where(usable, tile_slot[target], -1).astype(jnp.int32)
    return jnp.zeros((TILES, 8), jnp.int32).at[tile_slot].set(listing)


def draw_ocean_mask(key, part):
    live_tile, grid_row, grid_col, tile_slot = tile_layout(key)
    pixels = jax.random.randint(jax.random.fold_in(key, 11), (TILES, TILE, TILE), 0, 20) < 17
    by_position = (pixels & live_tile[:, None, None]).astype(jnp.int32)
    return jnp.zeros((TILES, TILE, TILE), jnp.int32).at[tile_slot].set(by_position)


def draw_fields(key, part):
    base_key, chan_key, pixel_key = jax.random.split(key, 3)
    base = jnp.clip(jax.random.normal(base_key, (TILES, TILE, TILE, C), jnp.float32), -6.0, 6.0)
    chan_scale = jnp.exp(jax.random.uniform(chan_key, (TILES, 1, 1, C), jnp.float32, -1.15, 1.15))
    pixel_scale = jnp.exp(jax.random.uniform(pixel_key, (TILES, TILE, TILE, 1), jnp.float32, -0.7, 0.7))
    return (base * chan_scale * pixel_scale).astype(jnp.bfloat16)


def block_scale(own_key, dims, cuts, low, largest):
    def one(axis_at, blocks):
        steps = jax.random.uniform(jax.random.fold_in(jax.random.fold_in(own_key, 6), axis_at), (blocks,), jnp.float32, low / len(cuts), largest / len(cuts))
        return jnp.repeat(jnp.exp(steps), dims[axis_at] // blocks).reshape((-1,) + (1,) * (len(dims) - axis_at - 1))

    factor_of = one(*cuts[0])
    for cut in cuts[1:]:
        factor_of = factor_of * one(*cut)
    return factor_of


def bell_draw(own_key, shape, scale, most, pieces=(), held_as=jnp.bfloat16):
    values = jax.random.normal(own_key, shape, jnp.float32) * scale
    if len(pieces) > 0:
        values = block_scale(own_key, shape, pieces, -0.22, 0.18) * values
    return jnp.clip(values, min=-most, max=most).astype(held_as)


def setup_inputs(seed: int = 0) -> dict:
    keys = jax.random.split(jax.random.key(seed), 14)
    return {
        "fields": draw_fields(jax.random.fold_in(keys[13], 71), 0),
        "cotangent": bell_draw(keys[1], (TILES, TILE, TILE, C), 1.0, 6.0, ((0, 32),)),
        "ocean_mask": draw_ocean_mask(jax.random.fold_in(keys[13], 71), 0),
        "neighbours": draw_neighbours(jax.random.fold_in(keys[13], 71), 0),
        "kernel": bell_draw(keys[4], (KSIZE, KSIZE, C), (KSIZE * KSIZE) ** -0.5, 0.875, (), jnp.float32),
        "conv_bias": jnp.clip(jax.random.uniform(keys[5], (C,), jnp.float32, -0.5, 0.5), -0.5, 0.5),
        "ln_gain": jnp.clip(1.0 + 0.1 * jax.random.normal(keys[6], (C,), jnp.float32), 0.5, 1.5),
        "ln_bias": bell_draw(keys[7], (C,), 0.3, 1.5, (), jnp.float32),
        "weight_in": bell_draw(keys[8], (C, F), C ** -0.5, 0.5),
        "bias_in": bell_draw(keys[9], (F,), 0.3, 1.5, (), jnp.float32),
        "weight_out": bell_draw(keys[10], (F, C), F ** -0.5, 0.25),
        "bias_out": bell_draw(keys[11], (C,), 0.3, 1.5, (), jnp.float32),
        "layer_scale": jnp.clip(jnp.exp(jax.random.uniform(keys[12], (C,), jnp.float32, math.log(0.3), math.log(1.5))), 0.3, 1.5),
    }


EPS = 1e-06
GELU_K = 0.7978845608028654
GELU_C = 0.044715
CONTRACT_LAST = (((1,), (1,)), ((), ()))
CONTRACT_ROWS = (((0,), (0,)), ((), ()))

def gelu_parts(hidden):
    cube = hidden * hidden * hidden
    tanh_part = jnp.tanh(GELU_K * (hidden + GELU_C * cube))
    gelu_value = 0.5 * hidden * (1.0 + tanh_part)
    gelu_slope = 0.5 * (1.0 + tanh_part) + 0.5 * hidden * (1.0 - tanh_part * tanh_part) * GELU_K * (1.0 + 3.0 * GELU_C * hidden * hidden)
    return (gelu_value, gelu_slope)

def block_core(conv, signal, ln_gain, ln_bias, weight_in, bias_in, weight_out, bias_out, layer_scale):
    mean_part = lax.optimization_barrier(jnp.mean(conv, axis=-1, keepdims=True))
    centred = conv - mean_part
    inv_std = lax.rsqrt(lax.optimization_barrier(jnp.mean(centred * centred, axis=-1, keepdims=True)) + EPS)
    normed = centred * inv_std
    lifted = (normed * ln_gain + ln_bias).astype(jnp.bfloat16)
    hidden = jnp.dot(lifted, weight_in, preferred_element_type=jnp.float32) + bias_in
    gelu_value, gelu_slope = gelu_parts(hidden)
    activated = gelu_value.astype(jnp.bfloat16)
    branch = jnp.dot(activated, weight_out, preferred_element_type=jnp.float32) + bias_out
    d_branch = signal * layer_scale
    branch_low = d_branch.astype(jnp.bfloat16)
    d_activated = lax.dot_general(branch_low, weight_out, CONTRACT_LAST, preferred_element_type=jnp.float32)
    d_hidden = d_activated * gelu_slope
    hidden_low = d_hidden.astype(jnp.bfloat16)
    d_lifted = lax.dot_general(hidden_low, weight_in, CONTRACT_LAST, preferred_element_type=jnp.float32)
    d_normed = d_lifted * ln_gain
    d_conv = inv_std * (d_normed - lax.optimization_barrier(jnp.mean(d_normed, axis=-1, keepdims=True)) - normed * lax.optimization_barrier(jnp.mean(d_normed * normed, axis=-1, keepdims=True)))
    partials = (lax.optimization_barrier(jnp.sum(signal * branch, axis=0)), lax.optimization_barrier(jnp.sum(d_branch, axis=0)), lax.dot_general(activated, branch_low, CONTRACT_ROWS, preferred_element_type=jnp.float32), lax.optimization_barrier(jnp.sum(d_hidden, axis=0)), lax.dot_general(lifted, hidden_low, CONTRACT_ROWS, preferred_element_type=jnp.float32), lax.optimization_barrier(jnp.sum(d_lifted * normed, axis=0)), lax.optimization_barrier(jnp.sum(d_lifted, axis=0)))
    return (branch, d_conv, partials)

def frame_strips(stack, radius):
    extent = stack.shape[1]
    top_rows = stack[:, :radius]
    bottom_rows = stack[:, extent - radius:]
    left_cols = jnp.swapaxes(stack[:, :, :radius], 1, 2)
    right_cols = jnp.swapaxes(stack[:, :, extent - radius:], 1, 2)
    return jnp.stack([top_rows, bottom_rows, left_cols, right_cols], axis=1)

def assemble(middle, picked, radius):
    extent = middle.shape[1]
    top_mid = picked[:, 0, 1]
    bottom_mid = picked[:, 1, 0]
    left_mid = jnp.swapaxes(picked[:, 2, 3], 1, 2)
    right_mid = jnp.swapaxes(picked[:, 3, 2], 1, 2)
    north_west = picked[:, 4, 1, :, extent - radius:]
    north_east = picked[:, 5, 1, :, :radius]
    south_west = picked[:, 6, 0, :, extent - radius:]
    south_east = picked[:, 7, 0, :, :radius]
    upper = jnp.concatenate([north_west, top_mid, north_east], axis=2)
    centre_band = jnp.concatenate([left_mid, middle, right_mid], axis=2)
    lower = jnp.concatenate([south_west, bottom_mid, south_east], axis=2)
    return jnp.concatenate([upper, centre_band, lower], axis=1)

def depthwise(padded, kernel):
    ksize = kernel.shape[0]
    out_size = padded.shape[1] - ksize + 1
    total = jnp.zeros((padded.shape[0], out_size, out_size, padded.shape[3]), jnp.float32)
    for row_tap in range(ksize):
        for col_tap in range(ksize):
            total = total + padded[:, row_tap:row_tap + out_size, col_tap:col_tap + out_size, :] * kernel[row_tap, col_tap]
    return total

def kernel_grad(padded, d_conv, ksize):
    out_size = d_conv.shape[1]
    rows_list = []
    for row_tap in range(ksize):
        cols_list = []
        for col_tap in range(ksize):
            window = padded[:, row_tap:row_tap + out_size, col_tap:col_tap + out_size, :]
            cols_list.append(lax.optimization_barrier(jnp.sum(window * d_conv, axis=(0, 1, 2))))
        rows_list.append(jnp.stack(cols_list))
    return jnp.stack(rows_list)

def reference(fields, cotangent, ocean_mask, neighbours, kernel, conv_bias, ln_gain, ln_bias, weight_in, bias_in, weight_out, bias_out, layer_scale):
    radius = KSIZE // 2
    mask_float = ocean_mask.astype(jnp.float32)[..., None]
    masked = (fields.astype(jnp.float32) * mask_float).astype(jnp.bfloat16)
    listed = neighbours >= 0
    safe_ids = jnp.where(listed, neighbours, 0).astype(jnp.int32)
    strips = frame_strips(masked, radius)

    def pick(table, tile_index):
        chosen = jnp.take(table, safe_ids[tile_index], axis=0)
        keep = listed[tile_index][:, None, None, None, None]
        return jnp.where(keep, chosen, jnp.zeros_like(chosen))[None]

    def one_tile(table, tile_index):
        return lax.dynamic_slice_in_dim(table, tile_index, 1, 0)

    def forward_tile(carry, tile_index):
        middle = one_tile(masked, tile_index)
        padded = assemble(middle, pick(strips, tile_index), radius).astype(jnp.float32)
        conv = depthwise(padded, kernel) + conv_bias
        tile_mask = one_tile(mask_float, tile_index)
        signal = one_tile(cotangent, tile_index).astype(jnp.float32) * tile_mask
        branch, d_conv, partials = block_core(conv.reshape(-1, C), signal.reshape(-1, C), ln_gain, ln_bias, weight_in, bias_in, weight_out, bias_out, layer_scale)
        branch = branch.reshape(conv.shape)
        d_conv = d_conv.reshape(conv.shape)
        updated = (tile_mask * (middle.astype(jnp.float32) + layer_scale * branch)).astype(jnp.bfloat16)
        partials = partials + (kernel_grad(padded, d_conv, KSIZE), lax.optimization_barrier(jnp.sum(d_conv, axis=(0, 1, 2))))
        carry = tuple((running + piece_sum for running, piece_sum in zip(carry, partials)))
        return (carry, (updated[0], d_conv[0]))
    start = (jnp.zeros((C,), jnp.float32), jnp.zeros((C,), jnp.float32), jnp.zeros((F, C), jnp.float32), jnp.zeros((F,), jnp.float32), jnp.zeros((C, F), jnp.float32), jnp.zeros((C,), jnp.float32), jnp.zeros((C,), jnp.float32), jnp.zeros((KSIZE, KSIZE, C), jnp.float32), jnp.zeros((C,), jnp.float32))
    tile_order = jnp.arange(TILES, dtype=jnp.int32)
    totals, outputs = lax.scan(forward_tile, start, tile_order)
    updated, d_conv_all = outputs
    d_strips = frame_strips(d_conv_all, radius)
    flipped = kernel[::-1, ::-1]

    def backward_tile(tile_index):
        padded = assemble(one_tile(d_conv_all, tile_index), pick(d_strips, tile_index), radius)
        back = depthwise(padded, flipped)
        tile_mask = one_tile(mask_float, tile_index)
        signal = one_tile(cotangent, tile_index).astype(jnp.float32) * tile_mask
        return (tile_mask * (signal + back))[0]
    d_fields = lax.map(backward_tile, tile_order)
    grad_scale = 1.0 / math.sqrt(TILES * TILE * TILE)
    scaled = [running * grad_scale for running in totals]
    return (updated, d_fields, scaled[7], scaled[8], scaled[5], scaled[6], scaled[4], scaled[3], scaled[2], scaled[1], scaled[0])
```

```python
import math

import jax
import jax.numpy as jnp
from jax import lax
from jax.sharding import PartitionSpec as P

EPS = 1e-06
GELU_K = 0.7978845608028654
GELU_C = 0.044715
CONTRACT_LAST = (((1,), (1,)), ((), ()))
CONTRACT_ROWS = (((0,), (0,)), ((), ()))


def gelu_parts(hidden):
    cube = hidden * hidden * hidden
    tanh_part = jnp.tanh(GELU_K * (hidden + GELU_C * cube))
    gelu_value = 0.5 * hidden * (1.0 + tanh_part)
    gelu_slope = 0.5 * (1.0 + tanh_part) + 0.5 * hidden * (1.0 - tanh_part * tanh_part) * GELU_K * (
        1.0 + 3.0 * GELU_C * hidden * hidden
    )
    return (gelu_value, gelu_slope)


def block_core(
    conv, signal, ln_gain, ln_bias, weight_in, bias_in, weight_out, bias_out, layer_scale
):
    mean_part = jnp.mean(conv, axis=-1, keepdims=True)
    centred = conv - mean_part
    inv_std = lax.rsqrt(jnp.mean(centred * centred, axis=-1, keepdims=True) + EPS)
    normed = centred * inv_std
    lifted = (normed * ln_gain + ln_bias).astype(jnp.bfloat16)
    hidden = jnp.dot(lifted, weight_in, preferred_element_type=jnp.float32) + bias_in
    gelu_value, gelu_slope = gelu_parts(hidden)
    activated = gelu_value.astype(jnp.bfloat16)
    branch = jnp.dot(activated, weight_out, preferred_element_type=jnp.float32) + bias_out
    d_branch = signal * layer_scale
    branch_low = d_branch.astype(jnp.bfloat16)
    d_activated = lax.dot_general(
        branch_low, weight_out, CONTRACT_LAST, preferred_element_type=jnp.float32
    )
    d_hidden = d_activated * gelu_slope
    hidden_low = d_hidden.astype(jnp.bfloat16)
    d_lifted = lax.dot_general(
        hidden_low, weight_in, CONTRACT_LAST, preferred_element_type=jnp.float32
    )
    d_normed = d_lifted * ln_gain
    d_conv = inv_std * (
        d_normed
        - jnp.mean(d_normed, axis=-1, keepdims=True)
        - normed * jnp.mean(d_normed * normed, axis=-1, keepdims=True)
    )
    partials = (
        jnp.sum(signal * branch, axis=0),
        jnp.sum(d_branch, axis=0),
        lax.dot_general(activated, branch_low, CONTRACT_ROWS, preferred_element_type=jnp.float32),
        jnp.sum(d_hidden, axis=0),
        lax.dot_general(lifted, hidden_low, CONTRACT_ROWS, preferred_element_type=jnp.float32),
        jnp.sum(d_lifted * normed, axis=0),
        jnp.sum(d_lifted, axis=0),
    )
    return (branch, d_conv, partials)


def frame_strips(stack, radius):
    extent = stack.shape[1]
    top_rows = stack[:, :radius]
    bottom_rows = stack[:, extent - radius :]
    left_cols = jnp.swapaxes(stack[:, :, :radius], 1, 2)
    right_cols = jnp.swapaxes(stack[:, :, extent - radius :], 1, 2)
    return jnp.stack([top_rows, bottom_rows, left_cols, right_cols], axis=1)


def assemble(middle, picked, radius):
    extent = middle.shape[1]
    top_mid = picked[:, 0]
    bottom_mid = picked[:, 1]
    left_mid = jnp.swapaxes(picked[:, 2], 1, 2)
    right_mid = jnp.swapaxes(picked[:, 3], 1, 2)
    north_west = picked[:, 4, :, extent - radius :]
    north_east = picked[:, 5, :, :radius]
    south_west = picked[:, 6, :, extent - radius :]
    south_east = picked[:, 7, :, :radius]
    upper = jnp.concatenate([north_west, top_mid, north_east], axis=2)
    centre_band = jnp.concatenate([left_mid, middle, right_mid], axis=2)
    lower = jnp.concatenate([south_west, bottom_mid, south_east], axis=2)
    return jnp.concatenate([upper, centre_band, lower], axis=1)


def depthwise(padded, kernel):
    ksize = kernel.shape[0]
    out_size = padded.shape[1] - ksize + 1
    total = jnp.zeros((padded.shape[0], out_size, out_size, padded.shape[3]), jnp.float32)
    for row_tap in range(ksize):
        for col_tap in range(ksize):
            total = (
                total
                + padded[:, row_tap : row_tap + out_size, col_tap : col_tap + out_size, :]
                * kernel[row_tap, col_tap]
            )
    return total


def kernel_grad(padded, d_conv, ksize):
    out_size = d_conv.shape[1]
    rows_list = []
    for row_tap in range(ksize):
        cols_list = []
        for col_tap in range(ksize):
            window = padded[:, row_tap : row_tap + out_size, col_tap : col_tap + out_size, :]
            cols_list.append(jnp.sum(window * d_conv, axis=(0, 1, 2)))
        rows_list.append(jnp.stack(cols_list))
    return jnp.stack(rows_list)


GROUP = 8
STRIP_FOR = (1, 0, 3, 2, 1, 1, 0, 0)
OPPOSITE = (1, 0, 3, 2, 7, 6, 5, 4)


def halo_maps(neighbours):
    peers = lax.axis_size("tiles")
    device = lax.axis_index("tiles")
    group = device // GROUP
    place = device % GROUP
    mine = neighbours[0]
    below = lax.ppermute(mine, "tiles", [(i, i + GROUP) for i in range(peers - GROUP)])
    above = lax.ppermute(mine, "tiles", [(i + GROUP, i) for i in range(peers - GROUP)])
    dest = jnp.arange(GROUP, dtype=jnp.int32)
    strip_of_side = jnp.array([STRIP_FOR[OPPOSITE[side]] for side in range(8)], jnp.int32)

    def strip_to(listing):
        hit = listing[None, :] == (group * GROUP + dest)[:, None]
        return jnp.sum(jnp.where(hit, strip_of_side[None, :], 0), axis=1)

    own = strip_to(mine)
    relayed = jnp.where(dest < place, 4 + strip_to(below), 8 + strip_to(above))
    send_index = jnp.stack([own, relayed], axis=1).reshape(-1)
    listed = mine >= 0
    slot = jnp.where(listed, (mine % GROUP) * 2 + (mine // GROUP != group), 0)
    return send_index, slot, listed


def exchange(strips, maps):
    send_index, slot, listed = maps
    peers = lax.axis_size("tiles")
    below = lax.ppermute(strips, "tiles", [(i, i + GROUP) for i in range(peers - GROUP)])
    above = lax.ppermute(strips, "tiles", [(i + GROUP, i) for i in range(peers - GROUP)])
    table = jnp.concatenate([strips, below, above], axis=0)
    blocks = jnp.take(table, send_index, axis=0, mode="clip")
    blocks = blocks.reshape((GROUP, 2) + strips.shape[1:])
    groups = [list(range(g, g + GROUP)) for g in range(0, peers, GROUP)]
    arrived = lax.all_to_all(blocks, "tiles", 0, 0, axis_index_groups=groups)
    arrived = arrived.reshape((GROUP * 2,) + strips.shape[1:])
    chosen = jnp.take(arrived, slot, axis=0, mode="clip")
    return jnp.where(listed[:, None, None, None], chosen, jnp.zeros_like(chosen))


def sum_over_tiles(parts):
    peers = lax.axis_size("tiles")
    flat = jnp.concatenate([part.reshape(-1, 128) for part in parts], axis=0)
    rows = flat.shape[0]
    block = -(-rows // (peers * 8)) * 8
    flat = jnp.pad(flat, ((0, peers * block - rows), (0, 0))).reshape(peers, block, 128)
    summed = jnp.sum(lax.all_to_all(flat, "tiles", 0, 0), axis=0)
    shared = jnp.broadcast_to(summed.astype(jnp.bfloat16)[None], (peers, block, 128))
    total = lax.all_to_all(shared, "tiles", 0, 0).reshape(-1, 128).astype(jnp.float32)
    out = []
    at = 0
    for part in parts:
        size = part.size // 128
        out.append(total[at : at + size].reshape(part.shape))
        at += size
    return out


def per_device(
    fields,
    cotangent,
    ocean_mask,
    neighbours,
    kernel,
    conv_bias,
    ln_gain,
    ln_bias,
    weight_in,
    bias_in,
    weight_out,
    bias_out,
    layer_scale,
):
    tile_count = fields.shape[0]
    tile_side = fields.shape[1]
    channels = fields.shape[3]
    ksize = kernel.shape[0]
    radius = ksize // 2
    mask_float = ocean_mask.astype(jnp.float32)[..., None]
    masked = (fields.astype(jnp.float32) * mask_float).astype(jnp.bfloat16)
    maps = halo_maps(neighbours)
    signal = cotangent.astype(jnp.float32) * mask_float
    received = exchange(frame_strips(masked, radius)[0], maps)[None]
    padded = assemble(masked, received, radius).astype(jnp.float32)
    conv = depthwise(padded, kernel) + conv_bias
    branch, d_conv, partials = block_core(
        conv.reshape(-1, channels),
        signal.reshape(-1, channels),
        ln_gain,
        ln_bias,
        weight_in,
        bias_in,
        weight_out,
        bias_out,
        layer_scale,
    )
    branch = branch.reshape(conv.shape)
    d_conv = d_conv.reshape(conv.shape)
    updated = (mask_float * (masked.astype(jnp.float32) + layer_scale * branch)).astype(
        jnp.bfloat16
    )
    kernel_part = kernel_grad(padded, d_conv, ksize)
    bias_part = jnp.sum(d_conv, axis=(0, 1, 2))
    flipped = kernel[::-1, ::-1]
    outgoing = frame_strips(d_conv, radius)[0].astype(jnp.bfloat16)
    received = exchange(outgoing, maps)[None].astype(jnp.float32)
    back = depthwise(assemble(d_conv, received, radius), flipped)
    d_fields = mask_float * (signal + back)
    grad_scale = 1.0 / math.sqrt(lax.axis_size("tiles") * tile_count * tile_side * tile_side)
    scaled = [piece * grad_scale for piece in partials + (kernel_part, bias_part)]
    totals = sum_over_tiles(scaled)
    return (
        updated,
        d_fields,
        totals[7],
        totals[8],
        totals[5],
        totals[6],
        totals[4],
        totals[3],
        totals[2],
        totals[1],
        totals[0],
    )


def solution(mesh):
    placed = (
        P("tiles", None, None, None),
        P("tiles", None, None, None),
        P("tiles", None, None),
        P("tiles", None),
        P(),
        P(),
        P(),
        P(),
        P(),
        P(),
        P(),
        P(),
        P(),
    )
    return jax.shard_map(
        per_device,
        mesh=mesh,
        in_specs=placed,
        out_specs=(
            P("tiles", None, None, None),
            P("tiles", None, None, None),
            P(),
            P(),
            P(),
            P(),
            P(),
            P(),
            P(),
            P(),
            P(),
        ),
        check_vma=False,
    )
```

```python
import math

import jax
import jax.numpy as jnp
from jax import lax
from jax.experimental import pallas as pl
from jax.experimental.pallas import tpu as pltpu
from jax.sharding import PartitionSpec as P

EPS = 1e-06
GELU_K = 0.7978845608028654
GELU_C = 0.044715
CONTRACT_LAST = (((1,), (1,)), ((), ()))
CONTRACT_ROWS = (((0,), (0,)), ((), ()))


SIDE = 64
RADIUS = 3
TAPS = 7
PITCH = 72
ROWS = SIDE + 2 * RADIUS
PAIRS = ROWS // 2
BLOCK = 8
F32 = jnp.float32
BF16 = jnp.bfloat16


def tap_matrices(kernel):
    channels = kernel.shape[2]
    wide = jnp.pad(kernel, ((1, 1), (0, 0), (0, 0)))
    first = wide[1:9]
    second = wide[0:8]
    both = jnp.stack([first, second], axis=1).transpose(2, 0, 1, 3).astype(BF16)
    eye = jnp.eye(channels, dtype=BF16)
    spread = both[:, :, None, :, :] * eye[None, None, :, None, :]
    return spread.reshape(TAPS * 8 * channels, 2 * channels)


def place_strips(pick, padded, stage):
    for r in range(RADIUS):
        padded[r * PITCH + RADIUS : r * PITCH + RADIUS + SIDE, :] = pick(0, r)
        low = (RADIUS + SIDE + r) * PITCH
        padded[low + RADIUS : low + RADIUS + SIDE, :] = pick(1, r)
        padded[pl.ds(RADIUS * PITCH + r, SIDE, stride=PITCH), :] = pick(2, r)
        padded[pl.ds(RADIUS * PITCH + RADIUS + SIDE + r, SIDE, stride=PITCH), :] = pick(3, r)
        stage[0:SIDE, :] = pick(4, r)
        padded[r * PITCH : r * PITCH + RADIUS, :] = stage[SIDE - RADIUS : SIDE, :]
        stage[SIDE : 2 * SIDE, :] = pick(5, r)
        padded[r * PITCH + RADIUS + SIDE : r * PITCH + 2 * RADIUS + SIDE, :] = stage[SIDE : SIDE + RADIUS, :]
        stage[2 * SIDE : 3 * SIDE, :] = pick(6, r)
        padded[low : low + RADIUS, :] = stage[3 * SIDE - RADIUS : 3 * SIDE, :]
        stage[3 * SIDE : 4 * SIDE, :] = pick(7, r)
        padded[low + RADIUS + SIDE : low + 2 * RADIUS + SIDE, :] = stage[3 * SIDE : 3 * SIDE + RADIUS, :]


def shift_copies(padded, shifted):
    def body(pair, carry):
        for half in range(2):
            at = (2 * pair + half) * PITCH
            for tap in range(TAPS):
                row = padded[pl.ds(at + tap, SIDE), :].astype(BF16)
                shifted[tap, pair, :, half * 128 : (half + 1) * 128] = row
        return carry

    lax.fori_loop(0, PAIRS, body, 0)


def conv_block(shifted, taps, first, count):
    total = None
    for tap in range(TAPS):
        rows = [
            shifted[tap, pl.ds(first + move, count)].reshape(count * SIDE, 256) for move in range(4)
        ]
        part = jnp.dot(
            jnp.concatenate(rows, axis=1),
            taps[tap * 1024 : (tap + 1) * 1024, :],
            preferred_element_type=F32,
        )
        total = part if total is None else total + part
    return total


def picker(slot, listed, arrived):
    def pick(side, r):
        value = arrived[slot[side], r].astype(F32)
        return jnp.where(listed[side] > 0, value, 0.0)

    return pick


def core_body(
    slot, listed, fields, arrived, cotangent, mask, taps, conv_bias, ln_gain, ln_bias, weight_in,
    bias_in, weight_out, bias_out, layer_scale,
    updated, d_conv, strips, padded, d_weight_in, d_weight_out, d_bias_in, small,
    shifted, stage,
):
    place_strips(picker(slot, listed, arrived), padded, stage)

    def fill(i, carry):
        padded[pl.ds((i + RADIUS) * PITCH + RADIUS, SIDE), :] = fields[i].astype(F32) * mask[i].astype(F32)
        return carry

    lax.fori_loop(0, SIDE, fill, 0)
    shift_copies(padded, shifted)
    d_weight_in[...] = jnp.zeros_like(d_weight_in)
    d_weight_out[...] = jnp.zeros_like(d_weight_out)
    d_bias_in[...] = jnp.zeros_like(d_bias_in)
    small[...] = jnp.zeros_like(small)
    d_conv[0:6] = jnp.zeros((6, SIDE, 128), F32)
    d_conv[SIDE + 6 : SIDE + 12] = jnp.zeros((6, SIDE, 128), F32)
    count = BLOCK // 2
    points = BLOCK * SIDE

    def by_half(ref, at):
        part = ref[pl.ds(at, BLOCK)].astype(F32).reshape(count, 2, SIDE, 128)
        return jnp.concatenate([part[:, 0], part[:, 1]], axis=0).reshape(points, 128)

    def by_row(value):
        part = value.reshape(2, count, SIDE, 128)
        return jnp.stack([part[0], part[1]], axis=1).reshape(BLOCK, SIDE, 128)

    def fold(value):
        return jnp.sum(value.reshape(-1, 8, value.shape[-1]), axis=0)

    def step(index, carry):
        at = index * BLOCK
        both = conv_block(shifted, taps, index * count, count)
        conv = jnp.concatenate([both[:, :128], both[:, 128:]], axis=0) + conv_bias[...]
        live = by_half(mask, at)
        signal = by_half(cotangent, at) * live
        centred = conv - jnp.mean(conv, axis=-1, keepdims=True)
        inv_std = lax.rsqrt(jnp.mean(centred * centred, axis=-1, keepdims=True) + EPS)
        normed = centred * inv_std
        lifted = (normed * ln_gain[...] + ln_bias[...]).astype(BF16)
        hidden = jnp.dot(lifted, weight_in[...], preferred_element_type=F32) + bias_in[...]
        square = hidden * hidden
        tanh_part = jnp.tanh(hidden * (GELU_K + GELU_K * GELU_C * square))
        half = 0.5 * hidden
        activated = (half + half * tanh_part).astype(BF16)
        slope = (0.5 + 0.5 * tanh_part) + half * (1.0 - tanh_part * tanh_part) * (
            GELU_K + 3.0 * GELU_K * GELU_C * square
        )
        branch = jnp.dot(activated, weight_out[...], preferred_element_type=F32) + bias_out[...]
        d_branch = signal * layer_scale[...]
        branch_low = d_branch.astype(BF16)
        d_hidden = slope * lax.dot_general(
            branch_low, weight_out[...], CONTRACT_LAST, preferred_element_type=F32
        )
        hidden_low = d_hidden.astype(BF16)
        d_lifted = lax.dot_general(
            hidden_low, weight_in[...], CONTRACT_LAST, preferred_element_type=F32
        )
        d_normed = d_lifted * ln_gain[...]
        d_out = inv_std * (
            d_normed
            - jnp.mean(d_normed, axis=-1, keepdims=True)
            - normed * jnp.mean(d_normed * normed, axis=-1, keepdims=True)
        )
        masked = by_half(fields, at) * live
        updated[pl.ds(at, BLOCK)] = by_row(live * (masked + layer_scale[...] * branch)).astype(BF16)
        d_conv[pl.ds(at + 6, BLOCK)] = by_row(d_out)
        d_weight_out[...] += lax.dot_general(
            branch_low, activated, CONTRACT_ROWS, preferred_element_type=F32
        )
        d_weight_in[...] += lax.dot_general(
            lifted, hidden_low, CONTRACT_ROWS, preferred_element_type=F32
        )
        d_bias_in[...] += fold(d_hidden)
        small[0:8] += fold(signal * branch)
        small[8:16] += fold(d_branch)
        small[16:24] += fold(d_lifted * normed)
        small[24:32] += fold(d_lifted)
        small[32:40] += fold(d_out)
        return carry

    lax.fori_loop(0, SIDE // BLOCK, step, 0)
    for r in range(RADIUS):
        strips[0, r] = d_conv[6 + r].astype(BF16)
        strips[1, r] = d_conv[6 + SIDE - RADIUS + r].astype(BF16)
        flat = d_conv.reshape((SIDE + 12) * SIDE, 128)
        strips[2, r] = flat[pl.ds(6 * SIDE + r, SIDE, stride=SIDE), :].astype(BF16)
        strips[3, r] = flat[pl.ds(7 * SIDE - RADIUS + r, SIDE, stride=SIDE), :].astype(BF16)


def kernel_grad_body(padded, d_conv, out):
    flat = d_conv.reshape((SIDE + 12) * SIDE, 128)
    for low, high in ((0, 4), (4, 7)):
        taps_here = high - low

        def column(block, sums, low=low, taps_here=taps_here):
            left = block * 8

            def row(i, state):
                sums, recent = state
                newest = flat[pl.ds(pl.multiple_of((i + 6 - low) * SIDE + left, 8), 8), :]
                window = (newest,) + recent
                new = []
                at = i * PITCH + left
                pieces = [padded[pl.ds(at + b, 8), :] for b in range(TAPS)]
                for a in range(taps_here):
                    for b in range(TAPS):
                        new.append(sums[a * TAPS + b] + pieces[b] * window[a])
                return tuple(new), window[:-1]

            start = tuple(
                flat[pl.ds(pl.multiple_of((5 - low - a) * SIDE + left, 8), 8), :]
                for a in range(taps_here - 1)
            )
            sums, _ = lax.fori_loop(0, ROWS, row, (sums, start), unroll=2)
            return sums

        zero = tuple(jnp.zeros((8, 128), F32) for _ in range(taps_here * TAPS))
        sums = lax.fori_loop(0, SIDE // 8, column, zero)
        for a in range(taps_here):
            for b in range(TAPS):
                at = (low + a) * TAPS + b
                out[at : at + 1, :] = jnp.sum(sums[a * TAPS + b], axis=0, keepdims=True)


def back_body(slot, listed, d_conv, arrived, cotangent, mask, taps, d_fields, padded, shifted, stage):
    place_strips(picker(slot, listed, arrived), padded, stage)

    def fill(i, carry):
        padded[pl.ds((i + RADIUS) * PITCH + RADIUS, SIDE), :] = d_conv[i + 6]
        return carry

    lax.fori_loop(0, SIDE, fill, 0)
    shift_copies(padded, shifted)
    count = BLOCK // 2

    def step(index, carry):
        at = index * BLOCK
        both = conv_block(shifted, taps, index * count, count).reshape(count, SIDE, 256)
        back = jnp.stack([both[:, :, :128], both[:, :, 128:]], axis=1).reshape(BLOCK, SIDE, 128)
        live = mask[pl.ds(at, BLOCK)].astype(F32)
        d_fields[pl.ds(at, BLOCK)] = live * (live * cotangent[pl.ds(at, BLOCK)].astype(F32) + back)
        return carry

    lax.fori_loop(0, SIDE // BLOCK, step, 0)


VMEM_BYTES = 60 * 1024 * 1024
IN_VMEM = pl.BlockSpec(memory_space=pltpu.VMEM)
IN_SMEM = pl.BlockSpec(memory_space=pltpu.SMEM)


def run_core(slot, listed, fields, arrived, cotangent, mask, taps, vectors, weights):
    conv_bias, ln_gain, ln_bias, bias_in, bias_out, layer_scale = vectors
    weight_in, weight_out = weights
    shape = jax.ShapeDtypeStruct
    return pl.pallas_call(
        core_body,
        out_shape=(
            shape((SIDE, SIDE, 128), BF16),
            shape((SIDE + 12, SIDE, 128), F32),
            shape((4, RADIUS, SIDE, 128), BF16),
            shape((ROWS * PITCH, 128), F32),
            shape((128, 512), F32),
            shape((128, 512), F32),
            shape((8, 512), F32),
            shape((40, 128), F32),
        ),
        in_specs=[IN_SMEM, IN_SMEM] + [IN_VMEM] * 13,
        out_specs=(IN_VMEM,) * 8,
        scratch_shapes=[
            pltpu.VMEM((TAPS, PAIRS, SIDE, 256), BF16),
            pltpu.VMEM((4 * SIDE, 128), F32),
        ],
        compiler_params=pltpu.CompilerParams(vmem_limit_bytes=VMEM_BYTES),
        name="core",
    )(slot, listed, fields, arrived, cotangent, mask, taps, conv_bias, ln_gain, ln_bias,
      weight_in, bias_in, weight_out, bias_out, layer_scale)


def run_kernel_grad(padded, d_conv):
    return pl.pallas_call(
        kernel_grad_body,
        out_shape=jax.ShapeDtypeStruct((56, 128), F32),
        in_specs=[IN_VMEM] * 2,
        out_specs=IN_VMEM,
        compiler_params=pltpu.CompilerParams(vmem_limit_bytes=VMEM_BYTES),
        cost_estimate=pl.CostEstimate(flops=80_000_000, bytes_accessed=5_000_000, transcendentals=0),
        name="kernel_grad",
    )(padded, d_conv)


def run_back(slot, listed, d_conv, arrived, cotangent, mask, taps):
    return pl.pallas_call(
        back_body,
        out_shape=jax.ShapeDtypeStruct((SIDE, SIDE, 128), F32),
        in_specs=[IN_SMEM, IN_SMEM] + [IN_VMEM] * 5,
        out_specs=IN_VMEM,
        scratch_shapes=[
            pltpu.VMEM((ROWS * PITCH, 128), F32),
            pltpu.VMEM((TAPS, PAIRS, SIDE, 256), BF16),
            pltpu.VMEM((4 * SIDE, 128), F32),
        ],
        compiler_params=pltpu.CompilerParams(vmem_limit_bytes=VMEM_BYTES),
        cost_estimate=pl.CostEstimate(flops=7_000_000_000, bytes_accessed=8_000_000, transcendentals=0),
        name="back",
    )(slot, listed, d_conv, arrived, cotangent, mask, taps)


def frame_strips(tile, radius):
    extent = tile.shape[0]
    left_cols = jnp.swapaxes(tile[:, :radius], 0, 1)
    right_cols = jnp.swapaxes(tile[:, extent - radius :], 0, 1)
    return jnp.stack([tile[:radius], tile[extent - radius :], left_cols, right_cols], axis=0)


GROUP = 8
STRIP_FOR = (1, 0, 3, 2, 1, 1, 0, 0)
OPPOSITE = (1, 0, 3, 2, 7, 6, 5, 4)


def halo_maps(neighbours):
    peers = lax.axis_size("tiles")
    device = lax.axis_index("tiles")
    group = device // GROUP
    place = device % GROUP
    mine = neighbours[0]
    below = lax.ppermute(mine, "tiles", [(i, i + GROUP) for i in range(peers - GROUP)])
    above = lax.ppermute(mine, "tiles", [(i + GROUP, i) for i in range(peers - GROUP)])
    dest = jnp.arange(GROUP, dtype=jnp.int32)
    strip_of_side = jnp.array([STRIP_FOR[OPPOSITE[side]] for side in range(8)], jnp.int32)

    def strip_to(listing):
        hit = listing[None, :] == (group * GROUP + dest)[:, None]
        return jnp.sum(jnp.where(hit, strip_of_side[None, :], 0), axis=1)

    own = strip_to(mine)
    relayed = jnp.where(dest < place, 4 + strip_to(below), 8 + strip_to(above))
    send_index = jnp.stack([own, relayed], axis=1).reshape(-1)
    listed = mine >= 0
    slot = jnp.where(listed, (mine % GROUP) * 2 + (mine // GROUP != group), 0)
    return send_index, slot.astype(jnp.int32), listed.astype(jnp.int32)


def exchange(strips, maps):
    send_index = maps[0]
    peers = lax.axis_size("tiles")
    below = lax.ppermute(strips, "tiles", [(i, i + GROUP) for i in range(peers - GROUP)])
    above = lax.ppermute(strips, "tiles", [(i + GROUP, i) for i in range(peers - GROUP)])
    table = jnp.concatenate([strips, below, above], axis=0)
    blocks = jnp.take(table, send_index, axis=0, mode="clip")
    blocks = blocks.reshape((GROUP, 2) + strips.shape[1:])
    groups = [list(range(g, g + GROUP)) for g in range(0, peers, GROUP)]
    arrived = lax.all_to_all(blocks, "tiles", 0, 0, axis_index_groups=groups)
    return arrived.reshape((GROUP * 2,) + strips.shape[1:])


def sum_over_tiles(parts):
    peers = lax.axis_size("tiles")
    flat = jnp.concatenate([part.reshape(-1, 128) for part in parts], axis=0)
    rows = flat.shape[0]
    block = -(-rows // (peers * 8)) * 8
    flat = jnp.pad(flat, ((0, peers * block - rows), (0, 0))).reshape(peers, block, 128)
    summed = jnp.sum(lax.all_to_all(flat, "tiles", 0, 0), axis=0)
    shared = jnp.broadcast_to(summed.astype(jnp.bfloat16)[None], (peers, block, 128))
    total = lax.all_to_all(shared, "tiles", 0, 0).reshape(-1, 128).astype(jnp.float32)
    out = []
    at = 0
    for part in parts:
        size = part.size // 128
        out.append(total[at : at + size].reshape(part.shape))
        at += size
    return out


def per_device(
    fields,
    cotangent,
    ocean_mask,
    neighbours,
    kernel,
    conv_bias,
    ln_gain,
    ln_bias,
    weight_in,
    bias_in,
    weight_out,
    bias_out,
    layer_scale,
):
    tile_count = fields.shape[0]
    tile_side = fields.shape[1]
    mask = jnp.broadcast_to(ocean_mask[0].astype(BF16)[..., None], fields.shape[1:])
    masked = fields[0] * mask
    maps = halo_maps(neighbours)
    slot, listed = maps[1], maps[2]
    arrived = exchange(frame_strips(masked, RADIUS), maps)
    vectors = [v.reshape(1, -1) for v in (conv_bias, ln_gain, ln_bias, bias_in, bias_out, layer_scale)]
    updated, d_conv, strips, padded, d_weight_in, d_weight_out, d_bias_in, small = run_core(
        slot, listed, fields[0], arrived, cotangent[0], mask, tap_matrices(kernel), vectors,
        (weight_in, weight_out),
    )
    arrived_back = exchange(strips, maps)
    d_kernel = run_kernel_grad(padded, d_conv)
    grad_scale = 1.0 / math.sqrt(lax.axis_size("tiles") * tile_count * tile_side * tile_side)
    small = jnp.sum(small.reshape(5, 8, 128), axis=1)
    parts = [d_weight_in, d_weight_out, jnp.sum(d_bias_in, axis=0), d_kernel[:49], small]
    totals = sum_over_tiles([part * grad_scale for part in parts])
    d_fields = run_back(
        slot, listed, d_conv, arrived_back, cotangent[0], mask, tap_matrices(kernel[::-1, ::-1])
    )
    t_in, t_out, t_bias_in, t_kernel, t_small = totals
    return (
        updated[None],
        d_fields[None],
        t_kernel.reshape(kernel.shape),
        t_small[4],
        t_small[2],
        t_small[3],
        t_in,
        t_bias_in,
        t_out.T,
        t_small[1],
        t_small[0],
    )


def solution(mesh):
    placed = (
        P("tiles", None, None, None),
        P("tiles", None, None, None),
        P("tiles", None, None),
        P("tiles", None),
        P(),
        P(),
        P(),
        P(),
        P(),
        P(),
        P(),
        P(),
        P(),
    )
    return jax.shard_map(
        per_device,
        mesh=mesh,
        in_specs=placed,
        out_specs=(
            P("tiles", None, None, None),
            P("tiles", None, None, None),
            P(),
            P(),
            P(),
            P(),
            P(),
            P(),
            P(),
            P(),
            P(),
        ),
        check_vma=False,
    )
```

```python
import math

import jax
import jax.numpy as jnp
from jax import lax
from jax.experimental import pallas as pl
from jax.experimental.pallas import tpu as pltpu
from jax.sharding import PartitionSpec as P

EPS = 1e-06
GELU_K = 0.7978845608028654
GELU_C = 0.044715
CONTRACT_LAST = (((1,), (1,)), ((), ()))
CONTRACT_ROWS = (((0,), (0,)), ((), ()))


SIDE = 64
RADIUS = 3
TAPS = 7
PITCH = 72
ROWS = SIDE + 2 * RADIUS
PAIRS = ROWS // 2
BLOCK = 8
F32 = jnp.float32
BF16 = jnp.bfloat16


def tap_rows(kernel):
    wide = jnp.pad(kernel, ((1, 1), (0, 0), (0, 0)))
    both = jnp.concatenate([wide[1:9], wide[0:8]], axis=2)
    return both.transpose(1, 0, 2).reshape(TAPS * 8, 256)


def build_taps(rows, taps):
    shape = (128, 256)
    across = lax.broadcasted_iota(jnp.int32, shape, 1)
    down = lax.broadcasted_iota(jnp.int32, shape, 0)
    eye = ((across == down) | (across == down + 128)).astype(F32)

    def body(tap, carry):
        for position in range(8):
            at = tap * 8 + position
            taps[pl.ds(pl.multiple_of(at * 128, 128), 128), :] = (eye * rows[pl.ds(at, 1), :]).astype(BF16)
        return carry

    lax.fori_loop(0, TAPS, body, 0)


def place_strips(pick, padded, stage):
    for r in range(RADIUS):
        padded[r * PITCH + RADIUS : r * PITCH + RADIUS + SIDE, :] = pick(0, r)
        low = (RADIUS + SIDE + r) * PITCH
        padded[low + RADIUS : low + RADIUS + SIDE, :] = pick(1, r)
        padded[pl.ds(RADIUS * PITCH + r, SIDE, stride=PITCH), :] = pick(2, r)
        padded[pl.ds(RADIUS * PITCH + RADIUS + SIDE + r, SIDE, stride=PITCH), :] = pick(3, r)
        stage[0:SIDE, :] = pick(4, r)
        padded[r * PITCH : r * PITCH + RADIUS, :] = stage[SIDE - RADIUS : SIDE, :]
        stage[SIDE : 2 * SIDE, :] = pick(5, r)
        padded[r * PITCH + RADIUS + SIDE : r * PITCH + 2 * RADIUS + SIDE, :] = stage[SIDE : SIDE + RADIUS, :]
        stage[2 * SIDE : 3 * SIDE, :] = pick(6, r)
        padded[low : low + RADIUS, :] = stage[3 * SIDE - RADIUS : 3 * SIDE, :]
        stage[3 * SIDE : 4 * SIDE, :] = pick(7, r)
        padded[low + RADIUS + SIDE : low + 2 * RADIUS + SIDE, :] = stage[3 * SIDE : 3 * SIDE + RADIUS, :]


def shift_copies(padded, shifted):
    def body(pair, carry):
        for half in range(2):
            at = (2 * pair + half) * PITCH
            for tap in range(TAPS):
                row = padded[pl.ds(at + tap, SIDE), :].astype(BF16)
                shifted[tap, pair, :, half * 128 : (half + 1) * 128] = row
        return carry

    lax.fori_loop(0, PAIRS, body, 0)


def conv_block(shifted, taps, first, count):
    total = None
    for tap in range(TAPS):
        rows = [
            shifted[tap, pl.ds(first + move, count)].reshape(count * SIDE, 256) for move in range(4)
        ]
        part = jnp.dot(
            jnp.concatenate(rows, axis=1),
            taps[tap * 1024 : (tap + 1) * 1024, :],
            preferred_element_type=F32,
        )
        total = part if total is None else total + part
    return total


def picker(slot, listed, arrived):
    def pick(side, r):
        value = arrived[slot[side], r].astype(F32)
        return jnp.where(listed[side] > 0, value, 0.0)

    return pick


def core_body(
    slot, listed, fields, arrived, cotangent, mask, tap_table, conv_bias, ln_gain, ln_bias, weight_in,
    bias_in, weight_out, bias_out, layer_scale,
    updated, d_conv, strips, padded, d_weight_in, d_weight_out, d_bias_in, small,
    shifted, stage, taps,
):
    build_taps(tap_table, taps)
    place_strips(picker(slot, listed, arrived), padded, stage)

    def fill(i, carry):
        padded[pl.ds((i + RADIUS) * PITCH + RADIUS, SIDE), :] = fields[i].astype(F32) * mask[i].astype(F32)
        return carry

    lax.fori_loop(0, SIDE, fill, 0)
    shift_copies(padded, shifted)
    d_weight_in[...] = jnp.zeros_like(d_weight_in)
    d_weight_out[...] = jnp.zeros_like(d_weight_out)
    d_bias_in[...] = jnp.zeros_like(d_bias_in)
    small[...] = jnp.zeros_like(small)
    d_conv[...] = jnp.zeros_like(d_conv)
    half_in = weight_in[...] * jnp.bfloat16(0.5)
    half_bias = bias_in[...] * 0.5
    count = BLOCK // 2
    points = BLOCK * SIDE

    def by_half(ref, at):
        part = ref[pl.ds(at, BLOCK)].astype(F32).reshape(count, 2, SIDE, 128)
        return jnp.concatenate([part[:, 0], part[:, 1]], axis=0).reshape(points, 128)

    def by_row(value):
        part = value.reshape(2, count, SIDE, 128)
        return jnp.stack([part[0], part[1]], axis=1).reshape(BLOCK, SIDE, 128)

    def fold(value):
        return jnp.sum(value.reshape(-1, 8, value.shape[-1]), axis=0)

    def step(index, both, last=False):
        at = index * BLOCK
        conv = jnp.concatenate([both[:, :128], both[:, 128:]], axis=0) + conv_bias[...]
        following = both if last else conv_block(shifted, taps, (index + 1) * count, count)
        live = by_half(mask, at)
        signal = by_half(cotangent, at) * live
        centred = conv - jnp.mean(conv, axis=-1, keepdims=True)
        inv_std = lax.rsqrt(jnp.mean(centred * centred, axis=-1, keepdims=True) + EPS)
        normed = centred * inv_std
        lifted = (normed * ln_gain[...] + ln_bias[...]).astype(BF16)
        half = jnp.dot(lifted, half_in, preferred_element_type=F32) + half_bias
        square = half * half
        tanh_part = jnp.tanh(half * (2.0 * GELU_K + 8.0 * GELU_K * GELU_C * square))
        above = 1.0 + tanh_part
        activated = (half * above).astype(BF16)
        slope = above * (
            0.5 + (half * (GELU_K + 12.0 * GELU_K * GELU_C * square)) * (1.0 - tanh_part)
        )
        branch = jnp.dot(activated, weight_out[...], preferred_element_type=F32) + bias_out[...]
        d_branch = signal * layer_scale[...]
        branch_low = d_branch.astype(BF16)
        d_hidden = slope * lax.dot_general(
            branch_low, weight_out[...], CONTRACT_LAST, preferred_element_type=F32
        )
        hidden_low = d_hidden.astype(BF16)
        d_lifted = lax.dot_general(
            hidden_low, weight_in[...], CONTRACT_LAST, preferred_element_type=F32
        )
        d_normed = d_lifted * ln_gain[...]
        d_out = inv_std * (
            d_normed
            - jnp.mean(d_normed, axis=-1, keepdims=True)
            - normed * jnp.mean(d_normed * normed, axis=-1, keepdims=True)
        )
        masked = by_half(fields, at) * live
        updated[pl.ds(at, BLOCK)] = by_row(live * (masked + layer_scale[...] * branch)).astype(BF16)
        rows = by_row(d_out)
        for i in range(BLOCK):
            d_conv[pl.ds((at + i + RADIUS) * PITCH + RADIUS, SIDE), :] = rows[i]
        d_weight_out[...] += lax.dot_general(
            branch_low, activated, CONTRACT_ROWS, preferred_element_type=F32
        )
        d_weight_in[...] += lax.dot_general(
            lifted, hidden_low, CONTRACT_ROWS, preferred_element_type=F32
        )
        d_bias_in[...] += fold(d_hidden)
        small[0:8] += fold(signal * branch)
        small[8:16] += fold(d_branch)
        small[16:24] += fold(d_lifted * normed)
        small[24:32] += fold(d_lifted)
        small[32:40] += fold(d_out)
        return following

    both = conv_block(shifted, taps, 0, count)
    both = lax.fori_loop(0, SIDE // BLOCK - 1, step, both)
    step(SIDE // BLOCK - 1, both, last=True)
    for r in range(RADIUS):
        corner = RADIUS * PITCH + RADIUS
        far = SIDE - RADIUS + r
        strips[0, r] = d_conv[corner + r * PITCH : corner + r * PITCH + SIDE, :].astype(BF16)
        strips[1, r] = d_conv[corner + far * PITCH : corner + far * PITCH + SIDE, :].astype(BF16)
        strips[2, r] = d_conv[pl.ds(corner + r, SIDE, stride=PITCH), :].astype(BF16)
        strips[3, r] = d_conv[pl.ds(corner + far, SIDE, stride=PITCH), :].astype(BF16)


def inner_body(padded, d_conv, cotangent, mask, tap_table, d_kernel, d_fields, sums, shifted, taps):
    build_taps(tap_table, taps)
    shift_copies(d_conv, shifted)
    sums[...] = jnp.zeros_like(sums)
    count = BLOCK // 2

    def step(index, carry):
        at = index * BLOCK
        both = conv_block(shifted, taps, index * count, count).reshape(count, SIDE, 256)
        for b in range(TAPS):
            part = [None] * TAPS
            for left in range(0, SIDE, 8):
                near = [
                    d_conv[pl.ds((at + i + RADIUS) * PITCH + RADIUS + left, 8), :] for i in range(BLOCK)
                ]
                for row in range(BLOCK + TAPS - 1):
                    piece = padded[pl.ds((at + row) * PITCH + left + b, 8), :]
                    for a in range(TAPS):
                        if 0 <= row - a < BLOCK:
                            term = piece * near[row - a]
                            part[a] = term if part[a] is None else part[a] + term
            for a in range(TAPS):
                sums[a * TAPS + b] += part[a]
        back = jnp.stack([both[:, :, :128], both[:, :, 128:]], axis=1).reshape(BLOCK, SIDE, 128)
        live = mask[pl.ds(at, BLOCK)].astype(F32)
        d_fields[pl.ds(at, BLOCK)] = live * (live * cotangent[pl.ds(at, BLOCK)].astype(F32) + back)
        return carry

    lax.fori_loop(0, SIDE // BLOCK, step, 0)
    d_kernel[...] = jnp.sum(sums[...], axis=1)


def edge_body(slot, listed, partial, arrived, mask_strips, weights, d_fields,
              frame, columns, beside, top, bottom, left, right, sems):
    inner = SIDE - 2 * RADIUS
    parts = (
        (top, (pl.ds(0, RADIUS),)),
        (bottom, (pl.ds(SIDE - RADIUS, RADIUS),)),
        (left, (pl.ds(RADIUS, inner), pl.ds(0, 8))),
        (right, (pl.ds(RADIUS, inner), pl.ds(SIDE - 8, 8))),
    )
    loads = [
        pltpu.make_async_copy(partial.at[where], held, sems.at[i])
        for i, (held, where) in enumerate(parts)
    ]
    for load in loads:
        load.start()
    pick = picker(slot, listed, arrived)
    frame[...] = jnp.zeros_like(frame)
    columns[...] = jnp.zeros_like(columns)
    for r in range(RADIUS):
        frame[0, r, RADIUS : RADIUS + SIDE, :] = pick(0, r)
        frame[1, r, RADIUS : RADIUS + SIDE, :] = pick(1, r)
        columns[0, r, RADIUS : RADIUS + SIDE, :] = pick(2, r)
        columns[1, r, RADIUS : RADIUS + SIDE, :] = pick(3, r)
        frame[0, r, 0:RADIUS, :] = pick(4, r)[SIDE - RADIUS :]
        frame[0, r, RADIUS + SIDE : 2 * RADIUS + SIDE, :] = pick(5, r)[:RADIUS]
        frame[1, r, 0:RADIUS, :] = pick(6, r)[SIDE - RADIUS :]
        frame[1, r, RADIUS + SIDE : 2 * RADIUS + SIDE, :] = pick(7, r)[:RADIUS]

    def rim(source, far, line, at, tap):
        total = None
        for r in range(RADIUS):
            across = r + 6 - line if far else r - line
            if 0 <= across < TAPS:
                for along in range(TAPS):
                    term = source[far, r, pl.ds(at + along, 8), :] * tap(across, along)
                    total = term if total is None else total + term
        return total

    def weight_row(a, b):
        return weights[a * TAPS + b : a * TAPS + b + 1, :]

    for load in loads:
        load.wait()

    def along(step, carry):
        at = pl.multiple_of(step * 8, 8)
        for line in range(RADIUS):
            for far, held in ((0, top), (1, bottom)):
                live = mask_strips[far, line, pl.ds(at, 8), :]
                add = rim(frame, far, line, at, weight_row)
                held[line, pl.ds(at, 8), :] += live * add
            for far in range(2):
                live = mask_strips[2 + far, line, pl.ds(at, 8), :]
                add = rim(columns, far, line, at, lambda across, along: weight_row(along, across))
                beside[far, line, pl.ds(at, 8), :] = live * add
        return carry

    lax.fori_loop(0, SIDE // 8, along, 0)
    for far, held in ((0, left), (1, right)):
        flat = held.reshape(inner * 8, 128)
        for line in range(RADIUS):
            column = 5 + line if far else line
            flat[pl.ds(column, inner, stride=8), :] += beside[far, line, RADIUS : SIDE - RADIUS, :]
            place = SIDE - RADIUS + line if far else line
            for i in range(RADIUS):
                top[i, place : place + 1, :] += beside[far, line, i : i + 1, :]
                low = SIDE - RADIUS + i
                bottom[i, place : place + 1, :] += beside[far, line, low : low + 1, :]
    stores = [
        pltpu.make_async_copy(held, d_fields.at[where], sems.at[i])
        for i, (held, where) in enumerate(parts)
    ]
    for store in stores:
        store.start()
    for store in stores:
        store.wait()


VMEM_BYTES = 60 * 1024 * 1024
IN_VMEM = pl.BlockSpec(memory_space=pltpu.VMEM)
IN_SMEM = pl.BlockSpec(memory_space=pltpu.SMEM)


def run_core(slot, listed, fields, arrived, cotangent, mask, tap_table, vectors, weights):
    conv_bias, ln_gain, ln_bias, bias_in, bias_out, layer_scale = vectors
    weight_in, weight_out = weights
    shape = jax.ShapeDtypeStruct
    return pl.pallas_call(
        core_body,
        out_shape=(
            shape((SIDE, SIDE, 128), BF16),
            shape((ROWS * PITCH, 128), F32),
            shape((4, RADIUS, SIDE, 128), BF16),
            shape((ROWS * PITCH, 128), F32),
            shape((128, 512), F32),
            shape((128, 512), F32),
            shape((8, 512), F32),
            shape((40, 128), F32),
        ),
        in_specs=[IN_SMEM, IN_SMEM] + [IN_VMEM] * 13,
        out_specs=(IN_VMEM,) * 8,
        scratch_shapes=[
            pltpu.VMEM((TAPS, PAIRS, SIDE, 256), BF16),
            pltpu.VMEM((4 * SIDE, 128), F32),
            pltpu.VMEM((TAPS * 1024, 256), BF16),
        ],
        compiler_params=pltpu.CompilerParams(vmem_limit_bytes=VMEM_BYTES),
        name="core",
    )(slot, listed, fields, arrived, cotangent, mask, tap_table, conv_bias, ln_gain, ln_bias,
      weight_in, bias_in, weight_out, bias_out, layer_scale)


def run_inner(padded, d_conv, cotangent, mask, tap_table):
    return pl.pallas_call(
        inner_body,
        out_shape=(
            jax.ShapeDtypeStruct((TAPS * TAPS, 128), F32),
            jax.ShapeDtypeStruct((SIDE, SIDE, 128), F32),
        ),
        in_specs=[IN_VMEM] * 5,
        out_specs=(IN_VMEM,) * 2,
        scratch_shapes=[
            pltpu.VMEM((TAPS * TAPS, 8, 128), F32),
            pltpu.VMEM((TAPS, PAIRS, SIDE, 256), BF16),
            pltpu.VMEM((TAPS * 1024, 256), BF16),
        ],
        compiler_params=pltpu.CompilerParams(vmem_limit_bytes=VMEM_BYTES),
        cost_estimate=pl.CostEstimate(flops=16_000_000_000, bytes_accessed=8_000_000, transcendentals=0),
        name="inner",
    )(padded, d_conv, cotangent, mask, tap_table)


def run_edge(slot, listed, partial, arrived, mask_strips, weights):
    rim = pltpu.VMEM((RADIUS, SIDE, 128), F32)
    side = pltpu.VMEM((SIDE - 2 * RADIUS, 8, 128), F32)
    return pl.pallas_call(
        edge_body,
        out_shape=jax.ShapeDtypeStruct((SIDE, SIDE, 128), F32),
        in_specs=[IN_SMEM, IN_SMEM, pl.BlockSpec(memory_space=pl.ANY)] + [IN_VMEM] * 3,
        out_specs=pl.BlockSpec(memory_space=pl.ANY),
        scratch_shapes=[
            pltpu.VMEM((2, RADIUS, PITCH, 128), F32),
            pltpu.VMEM((2, RADIUS, PITCH, 128), F32),
            pltpu.VMEM((2, RADIUS, SIDE, 128), F32),
            rim, rim, side, side,
            pltpu.SemaphoreType.DMA((4,)),
        ],
        input_output_aliases={2: 0},
        compiler_params=pltpu.CompilerParams(vmem_limit_bytes=VMEM_BYTES),
        name="edge",
    )(slot, listed, partial, arrived, mask_strips, weights)


def frame_strips(tile, radius):
    extent = tile.shape[0]
    left_cols = jnp.swapaxes(tile[:, :radius], 0, 1)
    right_cols = jnp.swapaxes(tile[:, extent - radius :], 0, 1)
    return jnp.stack([tile[:radius], tile[extent - radius :], left_cols, right_cols], axis=0)


GROUP = 8
STRIP_FOR = (1, 0, 3, 2, 1, 1, 0, 0)
OPPOSITE = (1, 0, 3, 2, 7, 6, 5, 4)


def halo_maps(neighbours):
    peers = lax.axis_size("tiles")
    device = lax.axis_index("tiles")
    group = device // GROUP
    place = device % GROUP
    mine = neighbours[0]
    below = lax.ppermute(mine, "tiles", [(i, i + GROUP) for i in range(peers - GROUP)])
    above = lax.ppermute(mine, "tiles", [(i + GROUP, i) for i in range(peers - GROUP)])
    dest = jnp.arange(GROUP, dtype=jnp.int32)
    strip_of_side = jnp.array([STRIP_FOR[OPPOSITE[side]] for side in range(8)], jnp.int32)

    def strip_to(listing):
        hit = listing[None, :] == (group * GROUP + dest)[:, None]
        return jnp.sum(jnp.where(hit, strip_of_side[None, :], 0), axis=1)

    own = strip_to(mine)
    relayed = jnp.where(dest < place, 4 + strip_to(below), 8 + strip_to(above))
    send_index = jnp.stack([own, relayed], axis=1).reshape(-1)
    listed = mine >= 0
    slot = jnp.where(listed, (mine % GROUP) * 2 + (mine // GROUP != group), 0)
    return send_index, slot.astype(jnp.int32), listed.astype(jnp.int32)


def exchange(strips, maps):
    send_index = maps[0]
    peers = lax.axis_size("tiles")
    below = lax.ppermute(strips, "tiles", [(i, i + GROUP) for i in range(peers - GROUP)])
    above = lax.ppermute(strips, "tiles", [(i + GROUP, i) for i in range(peers - GROUP)])
    table = jnp.concatenate([strips, below, above], axis=0)
    blocks = jnp.take(table, send_index, axis=0, mode="clip")
    blocks = blocks.reshape((GROUP, 2) + strips.shape[1:])
    groups = [list(range(g, g + GROUP)) for g in range(0, peers, GROUP)]
    arrived = lax.all_to_all(blocks, "tiles", 0, 0, axis_index_groups=groups)
    return arrived.reshape((GROUP * 2,) + strips.shape[1:])


def sum_over_tiles(parts):
    peers = lax.axis_size("tiles")
    flat = jnp.concatenate([part.reshape(-1, 128) for part in parts], axis=0)
    rows = flat.shape[0]
    block = -(-rows // (peers * 8)) * 8
    flat = jnp.pad(flat, ((0, peers * block - rows), (0, 0))).reshape(peers, block, 128)
    summed = jnp.sum(lax.all_to_all(flat, "tiles", 0, 0), axis=0)
    shared = jnp.broadcast_to(summed.astype(jnp.bfloat16)[None], (peers, block, 128))
    total = lax.all_to_all(shared, "tiles", 0, 0).reshape(-1, 128).astype(jnp.float32)
    out = []
    at = 0
    for part in parts:
        size = part.size // 128
        out.append(total[at : at + size].reshape(part.shape))
        at += size
    return out


def per_device(
    fields,
    cotangent,
    ocean_mask,
    neighbours,
    kernel,
    conv_bias,
    ln_gain,
    ln_bias,
    weight_in,
    bias_in,
    weight_out,
    bias_out,
    layer_scale,
):
    tile_count = fields.shape[0]
    tile_side = fields.shape[1]
    mask = jnp.broadcast_to(ocean_mask[0].astype(BF16)[..., None], fields.shape[1:])
    maps = halo_maps(neighbours)
    slot, listed = maps[1], maps[2]
    mask_strips = frame_strips(ocean_mask[0].astype(F32)[..., None], RADIUS)
    strips = frame_strips(fields[0], RADIUS) * mask_strips.astype(BF16)
    arrived = exchange(strips, maps)
    vectors = [v.reshape(1, -1) for v in (conv_bias, ln_gain, ln_bias, bias_in, bias_out, layer_scale)]
    updated, d_conv, strips, padded, d_weight_in, d_weight_out, d_bias_in, small = run_core(
        slot, listed, fields[0], arrived, cotangent[0], mask, tap_rows(kernel), vectors,
        (weight_in, weight_out),
    )
    arrived_back = exchange(strips, maps)
    flipped = kernel[::-1, ::-1]
    d_kernel, partial = run_inner(padded, d_conv, cotangent[0], mask, tap_rows(flipped))
    grad_scale = 1.0 / math.sqrt(lax.axis_size("tiles") * tile_count * tile_side * tile_side)
    small = jnp.sum(small.reshape(5, 8, 128), axis=1)
    parts = [d_weight_in, d_weight_out, jnp.sum(d_bias_in, axis=0), d_kernel, small]
    totals = sum_over_tiles([part * grad_scale for part in parts])
    d_fields = run_edge(
        slot, listed, partial, arrived_back,
        jnp.broadcast_to(mask_strips, (4, RADIUS, SIDE, 128)), flipped.reshape(TAPS * TAPS, 128),
    )
    t_in, t_out, t_bias_in, t_kernel, t_small = totals
    return (
        updated[None],
        d_fields[None],
        t_kernel.reshape(kernel.shape),
        t_small[4],
        t_small[2],
        t_small[3],
        t_in,
        t_bias_in,
        t_out.T,
        t_small[1],
        t_small[0],
    )


def solution(mesh):
    placed = (
        P("tiles", None, None, None),
        P("tiles", None, None, None),
        P("tiles", None, None),
        P("tiles", None),
        P(),
        P(),
        P(),
        P(),
        P(),
        P(),
        P(),
        P(),
        P(),
    )
    return jax.shard_map(
        per_device,
        mesh=mesh,
        in_specs=placed,
        out_specs=(
            P("tiles", None, None, None),
            P("tiles", None, None, None),
            P(),
            P(),
            P(),
            P(),
            P(),
            P(),
            P(),
            P(),
            P(),
        ),
        check_vma=False,
    )
```

```python
import math

import jax
import jax.numpy as jnp
from jax import lax
from jax.experimental import pallas as pl
from jax.experimental.pallas import tpu as pltpu
from jax.sharding import PartitionSpec as P

EPS = 1e-06
GELU_K = 0.7978845608028654
GELU_C = 0.044715
CONTRACT_LAST = (((1,), (1,)), ((), ()))
CONTRACT_ROWS = (((0,), (0,)), ((), ()))
SIDE = 64
RADIUS = 3
STRIP_ROWS = RADIUS * SIDE
GROUP = 8
STRIP_FOR = (1, 0, 3, 2, 1, 1, 0, 0)
OPPOSITE = (1, 0, 3, 2, 7, 6, 5, 4)
TAPS = 7
PITCH = 72
ROWS = SIDE + 2 * RADIUS
PAIRS = ROWS // 2
BLOCK = 8
AT_KERNEL = 1024
AT_BIAS_IN = 1080
AT_SMALL = 1088
PACKED_ROWS = 1096
F32 = jnp.float32
BF16 = jnp.bfloat16


def tap_rows(kernel):
    wide = jnp.pad(kernel, ((1, 1), (0, 0), (0, 0)))
    both = jnp.concatenate([wide[1:9], wide[0:8]], axis=2)
    return both.transpose(1, 0, 2).reshape(TAPS * 8, 256)


def build_taps(rows, taps):
    shape = (128, 256)
    across = lax.broadcasted_iota(jnp.int32, shape, 1)
    down = lax.broadcasted_iota(jnp.int32, shape, 0)
    eye = ((across == down) | (across == down + 128)).astype(F32)

    def body(tap, carry):
        for position in range(8):
            at = tap * 8 + position
            taps[pl.ds(pl.multiple_of(at * 128, 128), 128), :] = (eye * rows[pl.ds(at, 1), :]).astype(BF16)
        return carry

    lax.fori_loop(0, TAPS, body, 0)


def place_strips(pick, padded, stage):
    for r in range(RADIUS):
        padded[r * PITCH + RADIUS : r * PITCH + RADIUS + SIDE, :] = pick(0, r)
        low = (RADIUS + SIDE + r) * PITCH
        padded[low + RADIUS : low + RADIUS + SIDE, :] = pick(1, r)
        padded[pl.ds(RADIUS * PITCH + r, SIDE, stride=PITCH), :] = pick(2, r)
        padded[pl.ds(RADIUS * PITCH + RADIUS + SIDE + r, SIDE, stride=PITCH), :] = pick(3, r)
        stage[0:SIDE, :] = pick(4, r)
        padded[r * PITCH : r * PITCH + RADIUS, :] = stage[SIDE - RADIUS : SIDE, :]
        stage[SIDE : 2 * SIDE, :] = pick(5, r)
        padded[r * PITCH + RADIUS + SIDE : r * PITCH + 2 * RADIUS + SIDE, :] = stage[SIDE : SIDE + RADIUS, :]
        stage[2 * SIDE : 3 * SIDE, :] = pick(6, r)
        padded[low : low + RADIUS, :] = stage[3 * SIDE - RADIUS : 3 * SIDE, :]
        stage[3 * SIDE : 4 * SIDE, :] = pick(7, r)
        padded[low + RADIUS + SIDE : low + 2 * RADIUS + SIDE, :] = stage[3 * SIDE : 3 * SIDE + RADIUS, :]


def shift_copies(padded, shifted):
    def body(pair, carry):
        for half in range(2):
            at = (2 * pair + half) * PITCH
            for tap in range(TAPS):
                row = padded[pl.ds(at + tap, SIDE), :].astype(BF16)
                shifted[tap, pair, :, half * 128 : (half + 1) * 128] = row
        return carry

    lax.fori_loop(0, PAIRS, body, 0)


def conv_block(shifted, taps, first, count):
    total = None
    for tap in range(TAPS):
        rows = [
            shifted[tap, pl.ds(first + move, count)].reshape(count * SIDE, 256) for move in range(4)
        ]
        part = jnp.dot(
            jnp.concatenate(rows, axis=1),
            taps[tap * 1024 : (tap + 1) * 1024, :],
            preferred_element_type=F32,
        )
        total = part if total is None else total + part
    return total


def picker(place, arrived):
    group = lax.div(place[8], GROUP)

    def pick(side, r):
        tile = place[side]
        owner = jnp.maximum(tile, 0)
        slot = 2 * lax.rem(owner, GROUP) + jnp.where(lax.div(owner, GROUP) != group, 1, 0)
        at = pl.multiple_of(slot * STRIP_ROWS + r * SIDE, SIDE)
        value = arrived[pl.ds(at, SIDE), :].astype(F32)
        return jnp.where(tile >= 0, value, 0.0)

    return pick


def outgoing_body(place, fields, mask_strips, out, near, far):
    def fill(i, carry):
        near[pl.ds(i * 16, 16), :] = fields[i, 0:16, :].astype(F32)
        far[pl.ds(i * 16, 16), :] = fields[i, SIDE - 16 : SIDE, :].astype(F32)
        return carry

    lax.fori_loop(0, SIDE, fill, 0, unroll=4)
    for r in range(RADIUS):
        rows = (
            fields[r].astype(F32),
            fields[SIDE - RADIUS + r].astype(F32),
            near[pl.ds(r, SIDE, stride=16), :],
            far[pl.ds(16 - RADIUS + r, SIDE, stride=16), :],
        )
        for side in range(4):
            at = side * STRIP_ROWS + r * SIDE
            out[at : at + SIDE, :] = (rows[side] * mask_strips[side, r]).astype(BF16)
    lane = lax.broadcasted_iota(jnp.int32, (16, 128), 1)
    listing = jnp.zeros((16, 128), F32)
    for side in range(8):
        listing = jnp.where(lane == side, place[side].astype(F32), listing)
    out[4 * STRIP_ROWS :, :] = listing.astype(BF16)


def relay_body(place, lists, own, below, above, out):
    group = lax.div(place[8], GROUP)
    mine = lax.rem(place[8], GROUP)

    def strip_for(read, tile):
        strip = jnp.int32(0)
        for side in range(8):
            strip = jnp.where(read(side) == tile, STRIP_FOR[OPPOSITE[side]], strip)
        return pl.multiple_of(strip * STRIP_ROWS, STRIP_ROWS)

    for dest in range(GROUP):
        tile = group * GROUP + dest
        at = strip_for(lambda side: place[side], tile)
        out[2 * dest * STRIP_ROWS : (2 * dest + 1) * STRIP_ROWS, :] = own[pl.ds(at, STRIP_ROWS), :]
        at = strip_for(lambda side: jnp.where(dest < mine, lists[0, side], lists[1, side]), tile)
        out[(2 * dest + 1) * STRIP_ROWS : (2 * dest + 2) * STRIP_ROWS, :] = jnp.where(
            dest < mine, below[pl.ds(at, STRIP_ROWS), :], above[pl.ds(at, STRIP_ROWS), :]
        )


def core_body(
    place, fields, arrived, cotangent, mask, tap_table, conv_bias, ln_gain, ln_bias, weight_in,
    bias_in, weight_out, bias_out, layer_scale,
    updated, d_conv, strips, padded, d_weight_in, d_weight_out, d_bias_in, small,
    shifted, stage, taps,
):
    build_taps(tap_table, taps)
    place_strips(picker(place, arrived), padded, stage)

    def fill(i, carry):
        padded[pl.ds((i + RADIUS) * PITCH + RADIUS, SIDE), :] = fields[i].astype(F32) * mask[i].astype(F32)
        return carry

    lax.fori_loop(0, SIDE, fill, 0)
    shift_copies(padded, shifted)
    d_weight_in[...] = jnp.zeros_like(d_weight_in)
    d_weight_out[...] = jnp.zeros_like(d_weight_out)
    d_bias_in[...] = jnp.zeros_like(d_bias_in)
    small[...] = jnp.zeros_like(small)
    d_conv[...] = jnp.zeros_like(d_conv)
    half_in = weight_in[...] * jnp.bfloat16(0.5)
    half_bias = bias_in[...] * 0.5
    count = BLOCK // 2
    points = BLOCK * SIDE

    def by_half(ref, at):
        part = ref[pl.ds(at, BLOCK)].astype(F32).reshape(count, 2, SIDE, 128)
        return jnp.concatenate([part[:, 0], part[:, 1]], axis=0).reshape(points, 128)

    def by_row(value):
        part = value.reshape(2, count, SIDE, 128)
        return jnp.stack([part[0], part[1]], axis=1).reshape(BLOCK, SIDE, 128)

    def fold(value):
        return jnp.sum(value.reshape(-1, 8, value.shape[-1]), axis=0)

    def step(index, both, last=False):
        at = index * BLOCK
        conv = jnp.concatenate([both[:, :128], both[:, 128:]], axis=0) + conv_bias[...]
        following = both if last else conv_block(shifted, taps, (index + 1) * count, count)
        live = by_half(mask, at)
        signal = by_half(cotangent, at) * live
        centred = conv - jnp.mean(conv, axis=-1, keepdims=True)
        inv_std = lax.rsqrt(jnp.mean(centred * centred, axis=-1, keepdims=True) + EPS)
        normed = centred * inv_std
        lifted = (normed * ln_gain[...] + ln_bias[...]).astype(BF16)
        half = jnp.dot(lifted, half_in, preferred_element_type=F32) + half_bias
        square = half * half
        tanh_part = jnp.tanh(half * (2.0 * GELU_K + 8.0 * GELU_K * GELU_C * square))
        above = 1.0 + tanh_part
        activated = (half * above).astype(BF16)
        slope = above * (
            0.5 + (half * (GELU_K + 12.0 * GELU_K * GELU_C * square)) * (1.0 - tanh_part)
        )
        branch = jnp.dot(activated, weight_out[...], preferred_element_type=F32) + bias_out[...]
        d_branch = signal * layer_scale[...]
        branch_low = d_branch.astype(BF16)
        d_hidden = slope * lax.dot_general(
            branch_low, weight_out[...], CONTRACT_LAST, preferred_element_type=F32
        )
        hidden_low = d_hidden.astype(BF16)
        d_lifted = lax.dot_general(
            hidden_low, weight_in[...], CONTRACT_LAST, preferred_element_type=F32
        )
        d_normed = d_lifted * ln_gain[...]
        d_out = inv_std * (
            d_normed
            - jnp.mean(d_normed, axis=-1, keepdims=True)
            - normed * jnp.mean(d_normed * normed, axis=-1, keepdims=True)
        )
        masked = by_half(fields, at) * live
        updated[pl.ds(at, BLOCK)] = by_row(live * (masked + layer_scale[...] * branch)).astype(BF16)
        rows = by_row(d_out)
        for i in range(BLOCK):
            d_conv[pl.ds((at + i + RADIUS) * PITCH + RADIUS, SIDE), :] = rows[i]
        d_weight_out[...] += lax.dot_general(
            branch_low, activated, CONTRACT_ROWS, preferred_element_type=F32
        )
        d_weight_in[...] += lax.dot_general(
            lifted, hidden_low, CONTRACT_ROWS, preferred_element_type=F32
        )
        d_bias_in[...] += fold(d_hidden)
        small[0:8] += fold(signal * branch)
        small[8:16] += fold(d_branch)
        small[16:24] += fold(d_lifted * normed)
        small[24:32] += fold(d_lifted)
        small[32:40] += fold(d_out)
        return following

    both = conv_block(shifted, taps, 0, count)
    both = lax.fori_loop(0, SIDE // BLOCK - 1, step, both)
    step(SIDE // BLOCK - 1, both, last=True)
    for r in range(RADIUS):
        corner = RADIUS * PITCH + RADIUS
        far = SIDE - RADIUS + r
        rows = (
            d_conv[corner + r * PITCH : corner + r * PITCH + SIDE, :],
            d_conv[corner + far * PITCH : corner + far * PITCH + SIDE, :],
            d_conv[pl.ds(corner + r, SIDE, stride=PITCH), :],
            d_conv[pl.ds(corner + far, SIDE, stride=PITCH), :],
        )
        for side in range(4):
            at = side * STRIP_ROWS + r * SIDE
            strips[at : at + SIDE, :] = rows[side].astype(BF16)


def inner_body(
    scale, padded, d_conv, cotangent, mask, tap_table, d_weight_in, d_weight_out, d_bias_in, small,
    packed, d_fields, sums, shifted, taps, held,
):
    build_taps(tap_table, taps)
    shift_copies(d_conv, shifted)
    sums[...] = jnp.zeros_like(sums)
    count = BLOCK // 2

    def step(index, carry):
        at = index * BLOCK
        both = conv_block(shifted, taps, index * count, count).reshape(count, SIDE, 256)
        for b in range(TAPS):
            part = [None] * TAPS
            for left in range(0, SIDE, 8):
                near = [
                    d_conv[pl.ds((at + i + RADIUS) * PITCH + RADIUS + left, 8), :] for i in range(BLOCK)
                ]
                for row in range(BLOCK + TAPS - 1):
                    piece = padded[pl.ds((at + row) * PITCH + left + b, 8), :]
                    for a in range(TAPS):
                        if 0 <= row - a < BLOCK:
                            term = piece * near[row - a]
                            part[a] = term if part[a] is None else part[a] + term
            for a in range(TAPS):
                sums[a * TAPS + b] += part[a]
        back = jnp.stack([both[:, :, :128], both[:, :, 128:]], axis=1).reshape(BLOCK, SIDE, 128)
        live = mask[pl.ds(at, BLOCK)].astype(F32)
        d_fields[pl.ds(at, BLOCK)] = live * (live * cotangent[pl.ds(at, BLOCK)].astype(F32) + back)
        return carry

    lax.fori_loop(0, SIDE // BLOCK, step, 0)
    for tile in range(4):
        across = slice(tile * 128, (tile + 1) * 128)
        held[tile * 128 : (tile + 1) * 128, :] = d_weight_in[:, across] * scale[0]
        held[512 + tile * 128 : 512 + (tile + 1) * 128, :] = d_weight_out[:, across].T * scale[0]
        at = AT_BIAS_IN + tile
        held[at : at + 1, :] = jnp.sum(d_bias_in[:, across], axis=0, keepdims=True) * scale[0]
    held[AT_KERNEL : AT_KERNEL + TAPS * TAPS, :] = jnp.sum(sums[...], axis=1) * scale[0]
    for i in range(5):
        at = AT_SMALL + i
        held[at : at + 1, :] = jnp.sum(small[8 * i : 8 * i + 8, :], axis=0, keepdims=True) * scale[0]
    held[AT_SMALL + 5 :, :] = jnp.zeros((held.shape[0] - AT_SMALL - 5, 128), F32)
    packed[...] = held[...].astype(packed.dtype)


def unpack_body(total, d_weight_in, d_weight_out, d_bias_in, d_kernel, small, held):
    held[...] = total[...].astype(F32)
    for tile in range(4):
        across = slice(tile * 128, (tile + 1) * 128)
        d_weight_in[:, across] = held[tile * 128 : (tile + 1) * 128, :]
        at = AT_BIAS_IN + tile
        d_bias_in[:, across] = held[at : at + 1, :]
    d_weight_out[...] = held[512:1024, :]
    d_kernel[...] = held[AT_KERNEL : AT_KERNEL + TAPS * TAPS, :]
    small[...] = held[AT_SMALL : AT_SMALL + 8, :]


def edge_body(place, partial, arrived, mask_strips, weights, d_fields,
              frame, columns, beside, top, bottom, left, right, sems):
    inner = SIDE - 2 * RADIUS
    parts = (
        (top, (pl.ds(0, RADIUS),)),
        (bottom, (pl.ds(SIDE - RADIUS, RADIUS),)),
        (left, (pl.ds(RADIUS, inner), pl.ds(0, 8))),
        (right, (pl.ds(RADIUS, inner), pl.ds(SIDE - 8, 8))),
    )
    loads = [
        pltpu.make_async_copy(partial.at[where], held, sems.at[i])
        for i, (held, where) in enumerate(parts)
    ]
    for load in loads:
        load.start()
    pick = picker(place, arrived)
    frame[...] = jnp.zeros_like(frame)
    columns[...] = jnp.zeros_like(columns)
    for r in range(RADIUS):
        frame[0, r, RADIUS : RADIUS + SIDE, :] = pick(0, r)
        frame[1, r, RADIUS : RADIUS + SIDE, :] = pick(1, r)
        columns[0, r, RADIUS : RADIUS + SIDE, :] = pick(2, r)
        columns[1, r, RADIUS : RADIUS + SIDE, :] = pick(3, r)
        frame[0, r, 0:RADIUS, :] = pick(4, r)[SIDE - RADIUS :]
        frame[0, r, RADIUS + SIDE : 2 * RADIUS + SIDE, :] = pick(5, r)[:RADIUS]
        frame[1, r, 0:RADIUS, :] = pick(6, r)[SIDE - RADIUS :]
        frame[1, r, RADIUS + SIDE : 2 * RADIUS + SIDE, :] = pick(7, r)[:RADIUS]

    def rim(source, far, line, at, tap):
        total = None
        for r in range(RADIUS):
            across = r + 6 - line if far else r - line
            if 0 <= across < TAPS:
                for along in range(TAPS):
                    term = source[far, r, pl.ds(at + along, 8), :] * tap(across, along)
                    total = term if total is None else total + term
        return total

    def weight_row(a, b):
        return weights[a * TAPS + b : a * TAPS + b + 1, :]

    for load in loads:
        load.wait()

    def along(step, carry):
        at = pl.multiple_of(step * 8, 8)
        for line in range(RADIUS):
            for far, held in ((0, top), (1, bottom)):
                live = mask_strips[far, line, pl.ds(at, 8), :]
                add = rim(frame, far, line, at, weight_row)
                held[line, pl.ds(at, 8), :] += live * add
            for far in range(2):
                live = mask_strips[2 + far, line, pl.ds(at, 8), :]
                add = rim(columns, far, line, at, lambda across, along: weight_row(along, across))
                beside[far, line, pl.ds(at, 8), :] = live * add
        return carry

    lax.fori_loop(0, SIDE // 8, along, 0)
    for far, held in ((0, left), (1, right)):
        flat = held.reshape(inner * 8, 128)
        for line in range(RADIUS):
            column = 5 + line if far else line
            flat[pl.ds(column, inner, stride=8), :] += beside[far, line, RADIUS : SIDE - RADIUS, :]
            place = SIDE - RADIUS + line if far else line
            for i in range(RADIUS):
                top[i, place : place + 1, :] += beside[far, line, i : i + 1, :]
                low = SIDE - RADIUS + i
                bottom[i, place : place + 1, :] += beside[far, line, low : low + 1, :]
    stores = [
        pltpu.make_async_copy(held, d_fields.at[where], sems.at[i])
        for i, (held, where) in enumerate(parts)
    ]
    for store in stores:
        store.start()
    for store in stores:
        store.wait()


VMEM_BYTES = 60 * 1024 * 1024
IN_VMEM = pl.BlockSpec(memory_space=pltpu.VMEM)
IN_SMEM = pl.BlockSpec(memory_space=pltpu.SMEM)


def params():
    return pltpu.CompilerParams(vmem_limit_bytes=VMEM_BYTES)


def run_outgoing(place, fields, mask_strips):
    return pl.pallas_call(
        outgoing_body,
        out_shape=jax.ShapeDtypeStruct((4 * STRIP_ROWS + 16, 128), BF16),
        in_specs=[IN_SMEM] + [IN_VMEM] * 2,
        out_specs=IN_VMEM,
        scratch_shapes=[pltpu.VMEM((SIDE * 16, 128), F32)] * 2,
        compiler_params=params(),
        name="outgoing",
    )(place, fields, mask_strips)


def run_relay(place, lists, own, below, above):
    return pl.pallas_call(
        relay_body,
        out_shape=jax.ShapeDtypeStruct((2 * GROUP * STRIP_ROWS, 128), BF16),
        in_specs=[IN_SMEM] * 2 + [IN_VMEM] * 3,
        out_specs=IN_VMEM,
        compiler_params=params(),
        name="relay",
    )(place, lists, own, below, above)


def run_core(place, fields, arrived, cotangent, mask, tap_table, vectors, weights):
    conv_bias, ln_gain, ln_bias, bias_in, bias_out, layer_scale = vectors
    weight_in, weight_out = weights
    shape = jax.ShapeDtypeStruct
    return pl.pallas_call(
        core_body,
        out_shape=(
            shape((SIDE, SIDE, 128), BF16),
            shape((ROWS * PITCH, 128), F32),
            shape((4 * STRIP_ROWS, 128), BF16),
            shape((ROWS * PITCH, 128), F32),
            shape((128, 512), F32),
            shape((128, 512), F32),
            shape((8, 512), F32),
            shape((40, 128), F32),
        ),
        in_specs=[IN_SMEM] + [IN_VMEM] * 13,
        out_specs=(IN_VMEM,) * 8,
        scratch_shapes=[
            pltpu.VMEM((TAPS, PAIRS, SIDE, 256), BF16),
            pltpu.VMEM((4 * SIDE, 128), F32),
            pltpu.VMEM((TAPS * 1024, 256), BF16),
        ],
        compiler_params=params(),
        cost_estimate=pl.CostEstimate(flops=22_000_000_000, bytes_accessed=8_000_000, transcendentals=0),
        name="core",
    )(place, fields, arrived, cotangent, mask, tap_table, conv_bias, ln_gain, ln_bias,
      weight_in, bias_in, weight_out, bias_out, layer_scale)


def run_inner(rows, scale, padded, d_conv, cotangent, mask, tap_table, gradients):
    return pl.pallas_call(
        inner_body,
        out_shape=(
            jax.ShapeDtypeStruct((rows, 128), BF16),
            jax.ShapeDtypeStruct((SIDE, SIDE, 128), F32),
        ),
        in_specs=[IN_SMEM] + [IN_VMEM] * 9,
        out_specs=(IN_VMEM,) * 2,
        scratch_shapes=[
            pltpu.VMEM((TAPS * TAPS, 8, 128), F32),
            pltpu.VMEM((TAPS, PAIRS, SIDE, 256), BF16),
            pltpu.VMEM((TAPS * 1024, 256), BF16),
            pltpu.VMEM((rows, 128), F32),
        ],
        compiler_params=params(),
        cost_estimate=pl.CostEstimate(flops=16_000_000_000, bytes_accessed=8_000_000, transcendentals=0),
        name="inner",
    )(scale, padded, d_conv, cotangent, mask, tap_table, *gradients)


def run_unpack(total):
    shape = jax.ShapeDtypeStruct
    return pl.pallas_call(
        unpack_body,
        out_shape=(
            shape((128, 512), F32),
            shape((512, 128), F32),
            shape((1, 512), F32),
            shape((TAPS * TAPS, 128), F32),
            shape((8, 128), F32),
        ),
        in_specs=[IN_VMEM],
        out_specs=(IN_VMEM,) * 5,
        scratch_shapes=[pltpu.VMEM(total.shape, F32)],
        compiler_params=params(),
        name="unpack",
    )(total)


def run_edge(place, partial, arrived, mask_strips, weights):
    rim = pltpu.VMEM((RADIUS, SIDE, 128), F32)
    side = pltpu.VMEM((SIDE - 2 * RADIUS, 8, 128), F32)
    return pl.pallas_call(
        edge_body,
        out_shape=jax.ShapeDtypeStruct((SIDE, SIDE, 128), F32),
        in_specs=[IN_SMEM, pl.BlockSpec(memory_space=pl.ANY)] + [IN_VMEM] * 3,
        out_specs=pl.BlockSpec(memory_space=pl.ANY),
        scratch_shapes=[
            pltpu.VMEM((2, RADIUS, PITCH, 128), F32),
            pltpu.VMEM((2, RADIUS, PITCH, 128), F32),
            pltpu.VMEM((2, RADIUS, SIDE, 128), F32),
            rim, rim, side, side,
            pltpu.SemaphoreType.DMA((4,)),
        ],
        input_output_aliases={1: 0},
        compiler_params=params(),
        cost_estimate=pl.CostEstimate(flops=4_000_000_000, bytes_accessed=1_000_000, transcendentals=0),
        name="edge",
    )(place, partial, arrived, mask_strips, weights)


def strip_lines(plane):
    far = plane.shape[0] - RADIUS
    across = plane.T
    return jnp.stack([plane[:RADIUS], plane[far:], across[:RADIUS], across[far:]], axis=0)


def swap_groups(value):
    peers = lax.axis_size("tiles")
    below = lax.ppermute(value, "tiles", [(i, i + GROUP) for i in range(peers - GROUP)])
    above = lax.ppermute(value, "tiles", [(i + GROUP, i) for i in range(peers - GROUP)])
    return below, above


def within_group(blocks):
    peers = lax.axis_size("tiles")
    groups = [list(range(g, g + GROUP)) for g in range(0, peers, GROUP)]
    blocks = blocks.reshape(GROUP, -1, 128)
    return lax.all_to_all(blocks, "tiles", 0, 0, axis_index_groups=groups).reshape(-1, 128)


def sum_over_tiles(packed):
    peers = lax.axis_size("tiles")
    blocks = packed.reshape(peers, -1, 128)
    summed = jnp.sum(lax.all_to_all(blocks, "tiles", 0, 0).astype(F32), axis=0)
    shared = jnp.broadcast_to(summed.astype(BF16)[None], blocks.shape)
    return lax.all_to_all(shared, "tiles", 0, 0).reshape(packed.shape)


def per_device(
    fields,
    cotangent,
    ocean_mask,
    neighbours,
    kernel,
    conv_bias,
    ln_gain,
    ln_bias,
    weight_in,
    bias_in,
    weight_out,
    bias_out,
    layer_scale,
):
    peers = lax.axis_size("tiles")
    device = lax.axis_index("tiles").astype(jnp.int32)
    place = jnp.concatenate([neighbours[0], device[None]])
    mask_strips = jnp.broadcast_to(
        strip_lines(ocean_mask[0]).astype(F32)[..., None], (4, RADIUS, SIDE, 128)
    )
    own = run_outgoing(place, fields[0], mask_strips)
    below, above = swap_groups(own)
    lists = jnp.stack([below[-16, :8], above[-16, :8]]).astype(jnp.int32)
    arrived = within_group(run_relay(place, lists, own, below, above))
    mask = jnp.broadcast_to(ocean_mask[0].astype(BF16)[..., None], fields.shape[1:])
    vectors = [v.reshape(1, -1) for v in (conv_bias, ln_gain, ln_bias, bias_in, bias_out, layer_scale)]
    updated, d_conv, strips, padded, *gradients = run_core(
        place, fields[0], arrived, cotangent[0], mask, tap_rows(kernel), vectors,
        (weight_in, weight_out),
    )
    below, above = swap_groups(strips)
    blocks = run_relay(place, lists, strips, below, above)
    d_conv, blocks = lax.optimization_barrier((d_conv, blocks))
    arrived = within_group(blocks)
    flipped = kernel[::-1, ::-1]
    scale = jnp.full((1,), 1.0 / math.sqrt(peers * SIDE * SIDE), F32)
    rows = -(-PACKED_ROWS // (peers * 8)) * (peers * 8)
    packed, partial = run_inner(
        rows, scale, padded, d_conv, cotangent[0], mask, tap_rows(flipped), gradients
    )
    d_fields = run_edge(place, partial, arrived, mask_strips, flipped.reshape(TAPS * TAPS, 128))
    t_in, t_out, t_bias_in, t_kernel, t_small = run_unpack(sum_over_tiles(packed))
    return (
        updated[None],
        d_fields[None],
        t_kernel.reshape(kernel.shape),
        t_small[4],
        t_small[2],
        t_small[3],
        t_in,
        t_bias_in[0],
        t_out,
        t_small[1],
        t_small[0],
    )


def solution(mesh):
    placed = (
        P("tiles", None, None, None),
        P("tiles", None, None, None),
        P("tiles", None, None),
        P("tiles", None),
        P(),
        P(),
        P(),
        P(),
        P(),
        P(),
        P(),
        P(),
        P(),
    )
    return jax.shard_map(
        per_device,
        mesh=mesh,
        in_specs=placed,
        out_specs=(
            P("tiles", None, None, None),
            P("tiles", None, None, None),
            P(),
            P(),
            P(),
            P(),
            P(),
            P(),
            P(),
            P(),
            P(),
        ),
        check_vma=False,
    )
```

```python
import math

import jax
import jax.numpy as jnp
from jax import lax
from jax.experimental import pallas as pl
from jax.experimental.pallas import tpu as pltpu
from jax.sharding import PartitionSpec as P

EPS = 1e-06
GELU_K = 0.7978845608028654
GELU_C = 0.044715
CONTRACT_LAST = (((1,), (1,)), ((), ()))
CONTRACT_ROWS = (((0,), (0,)), ((), ()))
SIDE = 64
RADIUS = 3
STRIP_ROWS = RADIUS * SIDE
GROUP = 8
STRIP_FOR = (1, 0, 3, 2, 1, 1, 0, 0)
OPPOSITE = (1, 0, 3, 2, 7, 6, 5, 4)
TAPS = 7
PITCH = 72
ROWS = SIDE + 2 * RADIUS
PAIRS = ROWS // 2
BLOCK = 8
AT_KERNEL = 1024
AT_BIAS_IN = 1080
AT_SMALL = 1088
PACKED_ROWS = 1096
F32 = jnp.float32
BF16 = jnp.bfloat16


def tap_rows(kernel):
    wide = jnp.pad(kernel, ((1, 1), (0, 0), (0, 0)))
    both = jnp.concatenate([wide[1:9], wide[0:8]], axis=2)
    return both.transpose(1, 0, 2).reshape(TAPS * 8, 256)


def build_taps(rows, taps):
    shape = (128, 256)
    across = lax.broadcasted_iota(jnp.int32, shape, 1)
    down = lax.broadcasted_iota(jnp.int32, shape, 0)
    eye = ((across == down) | (across == down + 128)).astype(F32)

    def body(tap, carry):
        for position in range(8):
            at = tap * 8 + position
            taps[pl.ds(pl.multiple_of(at * 128, 128), 128), :] = (eye * rows[pl.ds(at, 1), :]).astype(BF16)
        return carry

    lax.fori_loop(0, TAPS, body, 0)


def place_strips(pick, padded, stage):
    for r in range(RADIUS):
        padded[r * PITCH + RADIUS : r * PITCH + RADIUS + SIDE, :] = pick(0, r)
        low = (RADIUS + SIDE + r) * PITCH
        padded[low + RADIUS : low + RADIUS + SIDE, :] = pick(1, r)
        padded[pl.ds(RADIUS * PITCH + r, SIDE, stride=PITCH), :] = pick(2, r)
        padded[pl.ds(RADIUS * PITCH + RADIUS + SIDE + r, SIDE, stride=PITCH), :] = pick(3, r)
        stage[0:SIDE, :] = pick(4, r)
        padded[r * PITCH : r * PITCH + RADIUS, :] = stage[SIDE - RADIUS : SIDE, :]
        stage[SIDE : 2 * SIDE, :] = pick(5, r)
        padded[r * PITCH + RADIUS + SIDE : r * PITCH + 2 * RADIUS + SIDE, :] = stage[SIDE : SIDE + RADIUS, :]
        stage[2 * SIDE : 3 * SIDE, :] = pick(6, r)
        padded[low : low + RADIUS, :] = stage[3 * SIDE - RADIUS : 3 * SIDE, :]
        stage[3 * SIDE : 4 * SIDE, :] = pick(7, r)
        padded[low + RADIUS + SIDE : low + 2 * RADIUS + SIDE, :] = stage[3 * SIDE : 3 * SIDE + RADIUS, :]


def shift_copies(padded, shifted):
    def body(pair, carry):
        for half in range(2):
            at = (2 * pair + half) * PITCH
            for tap in range(TAPS):
                row = padded[pl.ds(at + tap, SIDE), :].astype(BF16)
                shifted[tap, pair, :, half * 128 : (half + 1) * 128] = row
        return carry

    lax.fori_loop(0, PAIRS, body, 0)


def conv_block(shifted, taps, first, count):
    total = None
    for tap in range(TAPS):
        rows = [
            shifted[tap, pl.ds(first + move, count)].reshape(count * SIDE, 256) for move in range(4)
        ]
        part = jnp.dot(
            jnp.concatenate(rows, axis=1),
            taps[tap * 1024 : (tap + 1) * 1024, :],
            preferred_element_type=F32,
        )
        total = part if total is None else total + part
    return total


def picker(place, device, arrived):
    group = lax.div(device[0], GROUP)

    def pick(side, r):
        tile = place[0, side]
        owner = jnp.maximum(tile, 0)
        slot = 2 * lax.rem(owner, GROUP) + jnp.where(lax.div(owner, GROUP) != group, 1, 0)
        at = pl.multiple_of(slot * STRIP_ROWS + r * SIDE, SIDE)
        value = arrived[pl.ds(at, SIDE), :].astype(F32)
        return jnp.where(tile >= 0, value, 0.0)

    return pick


def outgoing_body(place, fields, ocean_mask, out, mask_strips, near, far):
    def fill(i, carry):
        near[pl.ds(i * 16, 16), :] = fields[i, 0:16, :].astype(F32)
        far[pl.ds(i * 16, 16), :] = fields[i, SIDE - 16 : SIDE, :].astype(F32)
        return carry

    lax.fori_loop(0, SIDE, fill, 0, unroll=4)
    live = ocean_mask[...].astype(F32)
    across = live.T
    for r in range(RADIUS):
        back = SIDE - RADIUS + r
        rows = (
            (fields[r].astype(F32), across[:, r : r + 1]),
            (fields[back].astype(F32), across[:, back : back + 1]),
            (near[pl.ds(r, SIDE, stride=16), :], live[:, r : r + 1]),
            (far[pl.ds(16 - RADIUS + r, SIDE, stride=16), :], live[:, back : back + 1]),
        )
        for side, (values, column) in enumerate(rows):
            at = side * STRIP_ROWS + r * SIDE
            wide = jnp.broadcast_to(column, (SIDE, 128))
            mask_strips[side, r] = wide
            out[at : at + SIDE, :] = (values * wide).astype(BF16)
    lane = lax.broadcasted_iota(jnp.int32, (16, 128), 1)
    listing = jnp.zeros((16, 128), F32)
    for side in range(8):
        listing = jnp.where(lane == side, place[0, side].astype(F32), listing)
    out[4 * STRIP_ROWS :, :] = listing.astype(BF16)


def relay_body(place, device, lists, own, paired, other, out):
    group = lax.div(device[0], GROUP)
    mine = lax.rem(device[0], GROUP)

    def strip_for(read, tile):
        strip = jnp.int32(0)
        for side in range(8):
            strip = jnp.where(read(side) == tile, STRIP_FOR[OPPOSITE[side]], strip)
        return pl.multiple_of(strip * STRIP_ROWS, STRIP_ROWS)

    for dest in range(GROUP):
        tile = group * GROUP + dest
        at = strip_for(lambda side: place[0, side], tile)
        out[2 * dest * STRIP_ROWS : (2 * dest + 1) * STRIP_ROWS, :] = own[pl.ds(at, STRIP_ROWS), :]
        use_pair = (dest < mine) == (lax.rem(group, 2) == 1)
        at = strip_for(lambda side: jnp.where(use_pair, lists[0, side], lists[1, side]), tile)
        out[(2 * dest + 1) * STRIP_ROWS : (2 * dest + 2) * STRIP_ROWS, :] = jnp.where(
            use_pair, paired[pl.ds(at, STRIP_ROWS), :], other[pl.ds(at, STRIP_ROWS), :]
        )


def core_body(
    place, device, fields, arrived, cotangent, mask, tap_table, conv_bias, ln_gain, ln_bias, weight_in,
    bias_in, weight_out, bias_out, layer_scale,
    updated, d_conv, strips, padded, d_weight_in, d_weight_out, d_bias_in, small,
    shifted, stage, taps,
):
    build_taps(tap_table, taps)
    place_strips(picker(place, device, arrived), padded, stage)

    def fill(i, carry):
        padded[pl.ds((i + RADIUS) * PITCH + RADIUS, SIDE), :] = fields[i].astype(F32) * mask[i].astype(F32)
        return carry

    lax.fori_loop(0, SIDE, fill, 0)
    shift_copies(padded, shifted)
    d_weight_in[...] = jnp.zeros_like(d_weight_in)
    d_weight_out[...] = jnp.zeros_like(d_weight_out)
    d_bias_in[...] = jnp.zeros_like(d_bias_in)
    small[...] = jnp.zeros_like(small)
    d_conv[...] = jnp.zeros_like(d_conv)
    half_in = weight_in[...] * jnp.bfloat16(0.5)
    half_bias = bias_in[...] * 0.5
    count = BLOCK // 2
    points = BLOCK * SIDE

    def by_half(ref, at):
        part = ref[pl.ds(at, BLOCK)].astype(F32).reshape(count, 2, SIDE, 128)
        return jnp.concatenate([part[:, 0], part[:, 1]], axis=0).reshape(points, 128)

    def by_row(value):
        part = value.reshape(2, count, SIDE, 128)
        return jnp.stack([part[0], part[1]], axis=1).reshape(BLOCK, SIDE, 128)

    def fold(value):
        return jnp.sum(value.reshape(-1, 8, value.shape[-1]), axis=0)

    def step(index, both, last=False):
        at = index * BLOCK
        conv = jnp.concatenate([both[:, :128], both[:, 128:]], axis=0) + conv_bias[...]
        following = both if last else conv_block(shifted, taps, (index + 1) * count, count)
        live = by_half(mask, at)
        signal = by_half(cotangent, at) * live
        centred = conv - jnp.mean(conv, axis=-1, keepdims=True)
        inv_std = lax.rsqrt(jnp.mean(centred * centred, axis=-1, keepdims=True) + EPS)
        normed = centred * inv_std
        lifted = (normed * ln_gain[...] + ln_bias[...]).astype(BF16)
        half = jnp.dot(lifted, half_in, preferred_element_type=F32) + half_bias
        square = half * half
        tanh_part = jnp.tanh(half * (2.0 * GELU_K + 8.0 * GELU_K * GELU_C * square))
        above = 1.0 + tanh_part
        activated = (half * above).astype(BF16)
        slope = above * (
            0.5 + (half * (GELU_K + 12.0 * GELU_K * GELU_C * square)) * (1.0 - tanh_part)
        )
        branch = jnp.dot(activated, weight_out[...], preferred_element_type=F32) + bias_out[...]
        d_branch = signal * layer_scale[...]
        branch_low = d_branch.astype(BF16)
        d_hidden = slope * lax.dot_general(
            branch_low, weight_out[...], CONTRACT_LAST, preferred_element_type=F32
        )
        hidden_low = d_hidden.astype(BF16)
        d_lifted = lax.dot_general(
            hidden_low, weight_in[...], CONTRACT_LAST, preferred_element_type=F32
        )
        d_normed = d_lifted * ln_gain[...]
        d_out = inv_std * (
            d_normed
            - jnp.mean(d_normed, axis=-1, keepdims=True)
            - normed * jnp.mean(d_normed * normed, axis=-1, keepdims=True)
        )
        masked = by_half(fields, at) * live
        updated[pl.ds(at, BLOCK)] = by_row(live * (masked + layer_scale[...] * branch)).astype(BF16)
        rows = by_row(d_out)
        for i in range(BLOCK):
            d_conv[pl.ds((at + i + RADIUS) * PITCH + RADIUS, SIDE), :] = rows[i]
        d_weight_out[...] += lax.dot_general(
            branch_low, activated, CONTRACT_ROWS, preferred_element_type=F32
        )
        d_weight_in[...] += lax.dot_general(
            lifted, hidden_low, CONTRACT_ROWS, preferred_element_type=F32
        )
        d_bias_in[...] += fold(d_hidden)
        small[0:8] += fold(signal * branch)
        small[8:16] += fold(d_branch)
        small[16:24] += fold(d_lifted * normed)
        small[24:32] += fold(d_lifted)
        small[32:40] += fold(d_out)
        return following

    both = conv_block(shifted, taps, 0, count)
    both = lax.fori_loop(0, SIDE // BLOCK - 1, step, both)
    step(SIDE // BLOCK - 1, both, last=True)
    for r in range(RADIUS):
        corner = RADIUS * PITCH + RADIUS
        far = SIDE - RADIUS + r
        rows = (
            d_conv[corner + r * PITCH : corner + r * PITCH + SIDE, :],
            d_conv[corner + far * PITCH : corner + far * PITCH + SIDE, :],
            d_conv[pl.ds(corner + r, SIDE, stride=PITCH), :],
            d_conv[pl.ds(corner + far, SIDE, stride=PITCH), :],
        )
        for side in range(4):
            at = side * STRIP_ROWS + r * SIDE
            strips[at : at + SIDE, :] = rows[side].astype(BF16)


def inner_body(
    scale, padded, d_conv, cotangent, mask, tap_table, d_weight_in, d_weight_out, d_bias_in, small,
    packed, d_fields, sums, shifted, taps, held,
):
    build_taps(tap_table, taps)
    shift_copies(d_conv, shifted)
    sums[...] = jnp.zeros_like(sums)
    count = BLOCK // 2

    def step(index, carry):
        at = index * BLOCK
        both = conv_block(shifted, taps, index * count, count).reshape(count, SIDE, 256)
        for b in range(TAPS):
            part = [None] * TAPS
            for left in range(0, SIDE, 8):
                near = [
                    d_conv[pl.ds((at + i + RADIUS) * PITCH + RADIUS + left, 8), :] for i in range(BLOCK)
                ]
                for row in range(BLOCK + TAPS - 1):
                    piece = padded[pl.ds((at + row) * PITCH + left + b, 8), :]
                    for a in range(TAPS):
                        if 0 <= row - a < BLOCK:
                            term = piece * near[row - a]
                            part[a] = term if part[a] is None else part[a] + term
            for a in range(TAPS):
                sums[a * TAPS + b] += part[a]
        back = jnp.stack([both[:, :, :128], both[:, :, 128:]], axis=1).reshape(BLOCK, SIDE, 128)
        live = mask[pl.ds(at, BLOCK)].astype(F32)
        d_fields[pl.ds(at, BLOCK)] = live * (live * cotangent[pl.ds(at, BLOCK)].astype(F32) + back)
        return carry

    lax.fori_loop(0, SIDE // BLOCK, step, 0)
    for tile in range(4):
        across = slice(tile * 128, (tile + 1) * 128)
        held[tile * 128 : (tile + 1) * 128, :] = d_weight_in[:, across] * scale[0]
        held[512 + tile * 128 : 512 + (tile + 1) * 128, :] = d_weight_out[:, across].T * scale[0]
        at = AT_BIAS_IN + tile
        held[at : at + 1, :] = jnp.sum(d_bias_in[:, across], axis=0, keepdims=True) * scale[0]
    held[AT_KERNEL : AT_KERNEL + TAPS * TAPS, :] = jnp.sum(sums[...], axis=1) * scale[0]
    for i in range(5):
        at = AT_SMALL + i
        held[at : at + 1, :] = jnp.sum(small[8 * i : 8 * i + 8, :], axis=0, keepdims=True) * scale[0]
    held[AT_SMALL + 5 :, :] = jnp.zeros((held.shape[0] - AT_SMALL - 5, 128), F32)
    packed[...] = held[...].astype(packed.dtype)


def unpack_body(total, d_weight_in, d_weight_out, d_bias_in, d_kernel, *rest):
    small, held = rest[:5], rest[5]
    held[...] = total[...].astype(F32)
    for tile in range(4):
        across = slice(tile * 128, (tile + 1) * 128)
        d_weight_in[:, across] = held[tile * 128 : (tile + 1) * 128, :]
        at = AT_BIAS_IN + tile
        d_bias_in[:, across] = held[at : at + 1, :]
    d_weight_out[...] = held[512:1024, :]
    for a in range(TAPS):
        d_kernel[a] = held[AT_KERNEL + a * TAPS : AT_KERNEL + (a + 1) * TAPS, :]
    for i in range(5):
        small[i][...] = held[AT_SMALL + i : AT_SMALL + i + 1, :]


def edge_body(place, device, partial, arrived, mask_strips, weights, d_fields,
              frame, columns, beside, top, bottom, left, right, sems):
    inner = SIDE - 2 * RADIUS
    parts = (
        (top, (pl.ds(0, RADIUS),)),
        (bottom, (pl.ds(SIDE - RADIUS, RADIUS),)),
        (left, (pl.ds(RADIUS, inner), pl.ds(0, 8))),
        (right, (pl.ds(RADIUS, inner), pl.ds(SIDE - 8, 8))),
    )
    loads = [
        pltpu.make_async_copy(partial.at[where], held, sems.at[i])
        for i, (held, where) in enumerate(parts)
    ]
    for load in loads:
        load.start()
    pick = picker(place, device, arrived)
    frame[...] = jnp.zeros_like(frame)
    columns[...] = jnp.zeros_like(columns)
    for r in range(RADIUS):
        frame[0, r, RADIUS : RADIUS + SIDE, :] = pick(0, r)
        frame[1, r, RADIUS : RADIUS + SIDE, :] = pick(1, r)
        columns[0, r, RADIUS : RADIUS + SIDE, :] = pick(2, r)
        columns[1, r, RADIUS : RADIUS + SIDE, :] = pick(3, r)
        frame[0, r, 0:RADIUS, :] = pick(4, r)[SIDE - RADIUS :]
        frame[0, r, RADIUS + SIDE : 2 * RADIUS + SIDE, :] = pick(5, r)[:RADIUS]
        frame[1, r, 0:RADIUS, :] = pick(6, r)[SIDE - RADIUS :]
        frame[1, r, RADIUS + SIDE : 2 * RADIUS + SIDE, :] = pick(7, r)[:RADIUS]

    def rim(source, far, line, at, tap):
        total = None
        for r in range(RADIUS):
            across = r + 6 - line if far else r - line
            if 0 <= across < TAPS:
                for along in range(TAPS):
                    term = source[far, r, pl.ds(at + along, 8), :] * tap(across, along)
                    total = term if total is None else total + term
        return total

    def weight_row(a, b):
        return weights[a * TAPS + b : a * TAPS + b + 1, :]

    for load in loads:
        load.wait()

    def along(step, carry):
        at = pl.multiple_of(step * 8, 8)
        for line in range(RADIUS):
            for far, held in ((0, top), (1, bottom)):
                live = mask_strips[far, line, pl.ds(at, 8), :]
                add = rim(frame, far, line, at, weight_row)
                held[line, pl.ds(at, 8), :] += live * add
            for far in range(2):
                live = mask_strips[2 + far, line, pl.ds(at, 8), :]
                add = rim(columns, far, line, at, lambda across, along: weight_row(along, across))
                beside[far, line, pl.ds(at, 8), :] = live * add
        return carry

    lax.fori_loop(0, SIDE // 8, along, 0)
    for far, held in ((0, left), (1, right)):
        flat = held.reshape(inner * 8, 128)
        for line in range(RADIUS):
            column = 5 + line if far else line
            flat[pl.ds(column, inner, stride=8), :] += beside[far, line, RADIUS : SIDE - RADIUS, :]
            place = SIDE - RADIUS + line if far else line
            for i in range(RADIUS):
                top[i, place : place + 1, :] += beside[far, line, i : i + 1, :]
                low = SIDE - RADIUS + i
                bottom[i, place : place + 1, :] += beside[far, line, low : low + 1, :]
    stores = [
        pltpu.make_async_copy(held, d_fields.at[where], sems.at[i])
        for i, (held, where) in enumerate(parts)
    ]
    for store in stores:
        store.start()
    for store in stores:
        store.wait()


VMEM_BYTES = 60 * 1024 * 1024
IN_VMEM = pl.BlockSpec(memory_space=pltpu.VMEM)
IN_SMEM = pl.BlockSpec(memory_space=pltpu.SMEM)


def params():
    return pltpu.CompilerParams(vmem_limit_bytes=VMEM_BYTES)


def run_outgoing(place, fields, ocean_mask):
    return pl.pallas_call(
        outgoing_body,
        out_shape=(
            jax.ShapeDtypeStruct((4 * STRIP_ROWS + 16, 128), BF16),
            jax.ShapeDtypeStruct((4, RADIUS, SIDE, 128), F32),
        ),
        in_specs=[IN_SMEM] + [IN_VMEM] * 2,
        out_specs=(IN_VMEM,) * 2,
        scratch_shapes=[pltpu.VMEM((SIDE * 16, 128), F32)] * 2,
        compiler_params=params(),
        name="outgoing",
    )(place, fields, ocean_mask)


def run_relay(place, device, lists, own, paired, other):
    return pl.pallas_call(
        relay_body,
        out_shape=jax.ShapeDtypeStruct((2 * GROUP * STRIP_ROWS, 128), BF16),
        in_specs=[IN_SMEM] * 3 + [IN_VMEM] * 3,
        out_specs=IN_VMEM,
        compiler_params=params(),
        name="relay",
    )(place, device, lists, own, paired, other)


def run_core(place, device, fields, arrived, cotangent, mask, tap_table, vectors, weights):
    conv_bias, ln_gain, ln_bias, bias_in, bias_out, layer_scale = vectors
    weight_in, weight_out = weights
    shape = jax.ShapeDtypeStruct
    return pl.pallas_call(
        core_body,
        out_shape=(
            shape((SIDE, SIDE, 128), BF16),
            shape((ROWS * PITCH, 128), F32),
            shape((4 * STRIP_ROWS, 128), BF16),
            shape((ROWS * PITCH, 128), F32),
            shape((128, 512), F32),
            shape((128, 512), F32),
            shape((8, 512), F32),
            shape((40, 128), F32),
        ),
        in_specs=[IN_SMEM] * 2 + [IN_VMEM] * 13,
        out_specs=(IN_VMEM,) * 8,
        scratch_shapes=[
            pltpu.VMEM((TAPS, PAIRS, SIDE, 256), BF16),
            pltpu.VMEM((4 * SIDE, 128), F32),
            pltpu.VMEM((TAPS * 1024, 256), BF16),
        ],
        compiler_params=params(),
        cost_estimate=pl.CostEstimate(flops=22_000_000_000, bytes_accessed=8_000_000, transcendentals=0),
        name="core",
    )(place, device, fields, arrived, cotangent, mask, tap_table, conv_bias, ln_gain, ln_bias,
      weight_in, bias_in, weight_out, bias_out, layer_scale)


def run_inner(rows, scale, padded, d_conv, cotangent, mask, tap_table, gradients):
    return pl.pallas_call(
        inner_body,
        out_shape=(
            jax.ShapeDtypeStruct((rows, 128), BF16),
            jax.ShapeDtypeStruct((SIDE, SIDE, 128), F32),
        ),
        in_specs=[IN_SMEM] + [IN_VMEM] * 9,
        out_specs=(IN_VMEM,) * 2,
        scratch_shapes=[
            pltpu.VMEM((TAPS * TAPS, 8, 128), F32),
            pltpu.VMEM((TAPS, PAIRS, SIDE, 256), BF16),
            pltpu.VMEM((TAPS * 1024, 256), BF16),
            pltpu.VMEM((rows, 128), F32),
        ],
        compiler_params=params(),
        cost_estimate=pl.CostEstimate(flops=16_000_000_000, bytes_accessed=8_000_000, transcendentals=0),
        name="inner",
    )(scale, padded, d_conv, cotangent, mask, tap_table, *gradients)


def run_unpack(total):
    shape = jax.ShapeDtypeStruct
    return pl.pallas_call(
        unpack_body,
        out_shape=(
            shape((128, 512), F32),
            shape((512, 128), F32),
            shape((1, 512), F32),
            shape((TAPS, TAPS, 128), F32),
        )
        + (shape((1, 128), F32),) * 5,
        in_specs=[IN_VMEM],
        out_specs=(IN_VMEM,) * 9,
        scratch_shapes=[pltpu.VMEM(total.shape, F32)],
        compiler_params=params(),
        name="unpack",
    )(total)


def run_edge(place, device, partial, arrived, mask_strips, weights):
    rim = pltpu.VMEM((RADIUS, SIDE, 128), F32)
    side = pltpu.VMEM((SIDE - 2 * RADIUS, 8, 128), F32)
    return pl.pallas_call(
        edge_body,
        out_shape=jax.ShapeDtypeStruct((SIDE, SIDE, 128), F32),
        in_specs=[IN_SMEM, IN_SMEM, pl.BlockSpec(memory_space=pl.ANY)] + [IN_VMEM] * 3,
        out_specs=pl.BlockSpec(memory_space=pl.ANY),
        scratch_shapes=[
            pltpu.VMEM((2, RADIUS, PITCH, 128), F32),
            pltpu.VMEM((2, RADIUS, PITCH, 128), F32),
            pltpu.VMEM((2, RADIUS, SIDE, 128), F32),
            rim, rim, side, side,
            pltpu.SemaphoreType.DMA((4,)),
        ],
        input_output_aliases={2: 0},
        compiler_params=params(),
        cost_estimate=pl.CostEstimate(flops=4_000_000_000, bytes_accessed=1_000_000, transcendentals=0),
        name="edge",
    )(place, device, partial, arrived, mask_strips, weights)


def swap_groups(value):
    groups = lax.axis_size("tiles") // GROUP

    def swap(first):
        pairs = []
        for low in range(first, groups - 1, 2):
            for i in range(low * GROUP, (low + 1) * GROUP):
                pairs += [(i, i + GROUP), (i + GROUP, i)]
        return lax.ppermute(value, "tiles", pairs)

    return swap(0), swap(1)


def within_group(blocks):
    peers = lax.axis_size("tiles")
    groups = [list(range(g, g + GROUP)) for g in range(0, peers, GROUP)]
    blocks = blocks.reshape(GROUP, -1, 128)
    return lax.all_to_all(blocks, "tiles", 0, 0, axis_index_groups=groups).reshape(-1, 128)


def sum_over_tiles(packed):
    peers = lax.axis_size("tiles")
    blocks = packed.reshape(peers, -1, 128)
    summed = jnp.sum(lax.all_to_all(blocks, "tiles", 0, 0).astype(F32), axis=0)
    shared = jnp.broadcast_to(summed.astype(BF16)[None], blocks.shape)
    return lax.all_to_all(shared, "tiles", 0, 0).reshape(packed.shape)


def per_device(
    fields,
    cotangent,
    ocean_mask,
    neighbours,
    kernel,
    conv_bias,
    ln_gain,
    ln_bias,
    weight_in,
    bias_in,
    weight_out,
    bias_out,
    layer_scale,
):
    peers = lax.axis_size("tiles")
    device = lax.axis_index("tiles").astype(jnp.int32).reshape(1)
    own, mask_strips = run_outgoing(neighbours, fields[0], ocean_mask[0])
    paired, other = swap_groups(own)
    mask = jnp.broadcast_to(ocean_mask[0].astype(BF16)[..., None], fields.shape[1:])
    lists = jnp.stack([paired[-16, :8], other[-16, :8]]).astype(jnp.int32)
    lists, mask = lax.optimization_barrier((lists, mask))
    arrived = within_group(run_relay(neighbours, device, lists, own, paired, other))
    vectors = [v.reshape(1, -1) for v in (conv_bias, ln_gain, ln_bias, bias_in, bias_out, layer_scale)]
    updated, d_conv, strips, padded, *gradients = run_core(
        neighbours, device, fields[0], arrived, cotangent[0], mask, tap_rows(kernel), vectors,
        (weight_in, weight_out),
    )
    paired, other = swap_groups(strips)
    blocks = run_relay(neighbours, device, lists, strips, paired, other)
    d_conv, blocks = lax.optimization_barrier((d_conv, blocks))
    arrived = within_group(blocks)
    flipped = kernel[::-1, ::-1]
    scale = jnp.full((1,), 1.0 / math.sqrt(peers * SIDE * SIDE), F32)
    rows = -(-PACKED_ROWS // (peers * 8)) * (peers * 8)
    packed, partial = run_inner(
        rows, scale, padded, d_conv, cotangent[0], mask, tap_rows(flipped), gradients
    )
    packed, arrived = lax.optimization_barrier((packed, arrived))
    weights = flipped.reshape(TAPS * TAPS, 128)
    d_fields = run_edge(neighbours, device, partial, arrived, mask_strips, weights)
    t_in, t_out, t_bias_in, t_kernel, *t_small = run_unpack(sum_over_tiles(packed))
    return (
        updated[None],
        d_fields[None],
        t_kernel,
        t_small[4][0],
        t_small[2][0],
        t_small[3][0],
        t_in,
        t_bias_in[0],
        t_out,
        t_small[1][0],
        t_small[0][0],
    )


def solution(mesh):
    placed = (
        P("tiles", None, None, None),
        P("tiles", None, None, None),
        P("tiles", None, None),
        P("tiles", None),
        P(),
        P(),
        P(),
        P(),
        P(),
        P(),
        P(),
        P(),
        P(),
    )
    return jax.shard_map(
        per_device,
        mesh=mesh,
        in_specs=placed,
        out_specs=(
            P("tiles", None, None, None),
            P("tiles", None, None, None),
            P(),
            P(),
            P(),
            P(),
            P(),
            P(),
            P(),
            P(),
            P(),
        ),
        check_vma=False,
    )
```

```python
import math

import jax
import jax.numpy as jnp
from jax import lax
from jax.experimental import pallas as pl
from jax.experimental.pallas import tpu as pltpu
from jax.sharding import PartitionSpec as P

EPS = 1e-06
GELU_K = 0.7978845608028654
GELU_C = 0.044715
CONTRACT_LAST = (((1,), (1,)), ((), ()))
CONTRACT_ROWS = (((0,), (0,)), ((), ()))
SIDE = 64
RADIUS = 3
STRIP_ROWS = RADIUS * SIDE
GROUP = 8
STRIP_FOR = (1, 0, 3, 2, 1, 1, 0, 0)
OPPOSITE = (1, 0, 3, 2, 7, 6, 5, 4)
TAPS = 7
PITCH = 72
ROWS = SIDE + 2 * RADIUS
PAIRS = ROWS // 2
BLOCK = 16
AT_KERNEL = 1024
AT_BIAS_IN = 1080
AT_SMALL = 1088
PACKED_ROWS = 1096
F32 = jnp.float32
BF16 = jnp.bfloat16


def tap_rows(kernel):
    wide = jnp.pad(kernel, ((1, 1), (0, 0), (0, 0)))
    both = jnp.concatenate([wide[1:9], wide[0:8]], axis=2)
    return both.transpose(1, 0, 2).reshape(TAPS * 8, 256)


def build_taps(rows, taps):
    shape = (128, 256)
    across = lax.broadcasted_iota(jnp.int32, shape, 1)
    down = lax.broadcasted_iota(jnp.int32, shape, 0)
    eye = ((across == down) | (across == down + 128)).astype(F32)

    def body(tap, carry):
        for position in range(8):
            at = tap * 8 + position
            taps[pl.ds(pl.multiple_of(at * 128, 128), 128), :] = (eye * rows[pl.ds(at, 1), :]).astype(BF16)
        return carry

    lax.fori_loop(0, TAPS, body, 0)


def place_strips(pick, padded, stage):
    for r in range(RADIUS):
        padded[r * PITCH + RADIUS : r * PITCH + RADIUS + SIDE, :] = pick(0, r)
        low = (RADIUS + SIDE + r) * PITCH
        padded[low + RADIUS : low + RADIUS + SIDE, :] = pick(1, r)
        padded[pl.ds(RADIUS * PITCH + r, SIDE, stride=PITCH), :] = pick(2, r)
        padded[pl.ds(RADIUS * PITCH + RADIUS + SIDE + r, SIDE, stride=PITCH), :] = pick(3, r)
        stage[0:SIDE, :] = pick(4, r)
        padded[r * PITCH : r * PITCH + RADIUS, :] = stage[SIDE - RADIUS : SIDE, :]
        stage[SIDE : 2 * SIDE, :] = pick(5, r)
        padded[r * PITCH + RADIUS + SIDE : r * PITCH + 2 * RADIUS + SIDE, :] = stage[SIDE : SIDE + RADIUS, :]
        stage[2 * SIDE : 3 * SIDE, :] = pick(6, r)
        padded[low : low + RADIUS, :] = stage[3 * SIDE - RADIUS : 3 * SIDE, :]
        stage[3 * SIDE : 4 * SIDE, :] = pick(7, r)
        padded[low + RADIUS + SIDE : low + 2 * RADIUS + SIDE, :] = stage[3 * SIDE : 3 * SIDE + RADIUS, :]


def shift_copies(padded, shifted):
    def body(pair, carry):
        for half in range(2):
            at = (2 * pair + half) * PITCH
            for tap in range(TAPS):
                row = padded[pl.ds(at + tap, SIDE), :].astype(BF16)
                shifted[tap, pair, :, half * 128 : (half + 1) * 128] = row
        return carry

    lax.fori_loop(0, PAIRS, body, 0)


def conv_block(shifted, taps, first, count):
    total = None
    for tap in range(TAPS):
        rows = [
            shifted[tap, pl.ds(first + move, count)].reshape(count * SIDE, 256) for move in range(4)
        ]
        part = jnp.dot(
            jnp.concatenate(rows, axis=1),
            taps[tap * 1024 : (tap + 1) * 1024, :],
            preferred_element_type=F32,
        )
        total = part if total is None else total + part
    return total


def picker(place, device, arrived):
    group = lax.div(device[0], GROUP)

    def pick(side, r):
        tile = place[0, side]
        owner = jnp.maximum(tile, 0)
        slot = 2 * lax.rem(owner, GROUP) + jnp.where(lax.div(owner, GROUP) != group, 1, 0)
        at = pl.multiple_of(slot * STRIP_ROWS + r * SIDE, SIDE)
        value = arrived[pl.ds(at, SIDE), :].astype(F32)
        return jnp.where(tile >= 0, value, 0.0)

    return pick


def start_all(pairs, sems):
    copies = [pltpu.make_async_copy(src, dst, sems.at[i]) for i, (src, dst) in enumerate(pairs)]
    for copy in copies:
        copy.start()
    return copies


def mask_body(ocean_mask, mask):
    across = ocean_mask[...].astype(F32).T
    for i in range(SIDE):
        mask[i] = jnp.broadcast_to(across[:, i : i + 1], (SIDE, 128)).astype(BF16)


def outgoing_body(place, fields, ocean_mask, out, mask_strips, near, far):
    def fill(i, carry):
        near[pl.ds(i * 16, 16), :] = fields[i, 0:16, :].astype(F32)
        far[pl.ds(i * 16, 16), :] = fields[i, SIDE - 16 : SIDE, :].astype(F32)
        return carry

    lax.fori_loop(0, SIDE, fill, 0, unroll=4)
    live = ocean_mask[...].astype(F32)
    across = live.T
    for r in range(RADIUS):
        back = SIDE - RADIUS + r
        rows = (
            (fields[r].astype(F32), across[:, r : r + 1]),
            (fields[back].astype(F32), across[:, back : back + 1]),
            (near[pl.ds(r, SIDE, stride=16), :], live[:, r : r + 1]),
            (far[pl.ds(16 - RADIUS + r, SIDE, stride=16), :], live[:, back : back + 1]),
        )
        for side, (values, column) in enumerate(rows):
            at = side * STRIP_ROWS + r * SIDE
            wide = jnp.broadcast_to(column, (SIDE, 128))
            mask_strips[side, r] = wide
            out[at : at + SIDE, :] = (values * wide).astype(BF16)
    lane = lax.broadcasted_iota(jnp.int32, (16, 128), 1)
    listing = jnp.zeros((16, 128), F32)
    for side in range(8):
        listing = jnp.where(lane == side, place[0, side].astype(F32), listing)
    out[4 * STRIP_ROWS :, :] = listing.astype(BF16)


def relay_body(place, device, lists, own, paired, other, out):
    group = lax.div(device[0], GROUP)
    mine = lax.rem(device[0], GROUP)

    def strip_for(read, tile):
        strip = jnp.int32(0)
        for side in range(8):
            strip = jnp.where(read(side) == tile, STRIP_FOR[OPPOSITE[side]], strip)
        return pl.multiple_of(strip * STRIP_ROWS, STRIP_ROWS)

    for dest in range(GROUP):
        tile = group * GROUP + dest
        at = strip_for(lambda side: place[0, side], tile)
        out[2 * dest * STRIP_ROWS : (2 * dest + 1) * STRIP_ROWS, :] = own[pl.ds(at, STRIP_ROWS), :]
        use_pair = (dest < mine) == (lax.rem(group, 2) == 1)
        at = strip_for(lambda side: jnp.where(use_pair, lists[0, side], lists[1, side]), tile)
        out[(2 * dest + 1) * STRIP_ROWS : (2 * dest + 2) * STRIP_ROWS, :] = jnp.where(
            use_pair, paired[pl.ds(at, STRIP_ROWS), :], other[pl.ds(at, STRIP_ROWS), :]
        )


def core_body(
    place, device, fields, arrived, cotangent, mask, tap_table, conv_bias, ln_gain, ln_bias, weight_in,
    bias_in, weight_out, bias_out, layer_scale,
    updated_out, d_conv_out, strips, padded_out, d_weight_in, d_weight_out, d_bias_in, small,
    shifted, stage, taps, fields_in, arrived_in, cotangent_in, mask_in, updated, d_conv, padded,
    in_sems, out_sems, row_sems,
):
    loads = start_all(
        ((mask, mask_in), (fields, fields_in), (arrived, arrived_in), (cotangent, cotangent_in)), in_sems
    )
    mask, fields, arrived, cotangent = mask_in, fields_in, arrived_in, cotangent_in
    build_taps(tap_table, taps)
    for load in loads[:3]:
        load.wait()
    place_strips(picker(place, device, arrived), padded, stage)

    def fill(i, carry):
        padded[pl.ds((i + RADIUS) * PITCH + RADIUS, SIDE), :] = fields[i].astype(F32) * mask[i].astype(F32)
        return carry

    lax.fori_loop(0, SIDE, fill, 0)
    stores = start_all(((padded, padded_out),), out_sems)
    shift_copies(padded, shifted)
    loads[3].wait()
    d_weight_in[...] = jnp.zeros_like(d_weight_in)
    d_weight_out[...] = jnp.zeros_like(d_weight_out)
    d_bias_in[...] = jnp.zeros_like(d_bias_in)
    small[...] = jnp.zeros_like(small)
    d_conv[...] = jnp.zeros_like(d_conv)
    half_in = weight_in[...] * jnp.bfloat16(0.5)
    half_bias = bias_in[...] * 0.5
    count = BLOCK // 2
    points = BLOCK * SIDE

    def by_half(ref, at):
        part = ref[pl.ds(at, BLOCK)].astype(F32).reshape(count, 2, SIDE, 128)
        return jnp.concatenate([part[:, 0], part[:, 1]], axis=0).reshape(points, 128)

    def by_row(value):
        part = value.reshape(2, count, SIDE, 128)
        return jnp.stack([part[0], part[1]], axis=1).reshape(BLOCK, SIDE, 128)

    def fold(value):
        return jnp.sum(value.reshape(-1, 8, value.shape[-1]), axis=0)

    def step(index, both, last=False):
        at = index * BLOCK
        conv = jnp.concatenate([both[:, :128], both[:, 128:]], axis=0) + conv_bias[...]
        following = both if last else conv_block(shifted, taps, (index + 1) * count, count)
        live = by_half(mask, at)
        signal = by_half(cotangent, at) * live
        centred = conv - jnp.mean(conv, axis=-1, keepdims=True)
        inv_std = lax.rsqrt(jnp.mean(centred * centred, axis=-1, keepdims=True) + EPS)
        normed = centred * inv_std
        lifted = (normed * ln_gain[...] + ln_bias[...]).astype(BF16)
        half = jnp.dot(lifted, half_in, preferred_element_type=F32) + half_bias
        square = half * half
        tanh_part = jnp.tanh(half * (2.0 * GELU_K + 8.0 * GELU_K * GELU_C * square))
        above = 1.0 + tanh_part
        activated = (half * above).astype(BF16)
        slope = above * (
            0.5 + (half * (GELU_K + 12.0 * GELU_K * GELU_C * square)) * (1.0 - tanh_part)
        )
        branch = jnp.dot(activated, weight_out[...], preferred_element_type=F32) + bias_out[...]
        d_branch = signal * layer_scale[...]
        branch_low = d_branch.astype(BF16)
        d_hidden = slope * lax.dot_general(
            branch_low, weight_out[...], CONTRACT_LAST, preferred_element_type=F32
        )
        hidden_low = d_hidden.astype(BF16)
        d_lifted = lax.dot_general(
            hidden_low, weight_in[...], CONTRACT_LAST, preferred_element_type=F32
        )
        d_normed = d_lifted * ln_gain[...]
        d_out = inv_std * (
            d_normed
            - jnp.mean(d_normed, axis=-1, keepdims=True)
            - normed * jnp.mean(d_normed * normed, axis=-1, keepdims=True)
        )
        masked = by_half(fields, at) * live
        updated[pl.ds(at, BLOCK)] = by_row(live * (masked + layer_scale[...] * branch)).astype(BF16)
        rows = by_row(d_out)
        for i in range(BLOCK):
            d_conv[pl.ds((at + i + RADIUS) * PITCH + RADIUS, SIDE), :] = rows[i]
        d_weight_out[...] += lax.dot_general(
            branch_low, activated, CONTRACT_ROWS, preferred_element_type=F32
        )
        d_weight_in[...] += lax.dot_general(
            lifted, hidden_low, CONTRACT_ROWS, preferred_element_type=F32
        )
        d_bias_in[...] += fold(d_hidden)
        small[0:8] += fold(signal * branch)
        small[8:16] += fold(d_branch)
        small[16:24] += fold(d_lifted * normed)
        small[24:32] += fold(d_lifted)
        small[32:40] += fold(d_out)
        for store in rows_out(index):
            store.start()
        return following

    def rows_out(index):
        rows = pl.ds(index * BLOCK, BLOCK)
        wide = pl.ds(pl.multiple_of((index * BLOCK + RADIUS) * PITCH, 8), BLOCK * PITCH)
        return (
            pltpu.make_async_copy(updated.at[rows], updated_out.at[rows], row_sems.at[0, index]),
            pltpu.make_async_copy(d_conv.at[wide], d_conv_out.at[wide], row_sems.at[1, index]),
        )

    both = conv_block(shifted, taps, 0, count)
    both = lax.fori_loop(0, SIDE // BLOCK - 1, step, both)
    step(SIDE // BLOCK - 1, both, last=True)
    edge = RADIUS * PITCH
    for i, rows in enumerate((pl.ds(0, edge), pl.ds(edge + SIDE * PITCH, edge))):
        store = pltpu.make_async_copy(d_conv.at[rows], d_conv_out.at[rows], out_sems.at[1 + i])
        store.start()
        stores.append(store)
    for r in range(RADIUS):
        corner = RADIUS * PITCH + RADIUS
        far = SIDE - RADIUS + r
        rows = (
            d_conv[corner + r * PITCH : corner + r * PITCH + SIDE, :],
            d_conv[corner + far * PITCH : corner + far * PITCH + SIDE, :],
            d_conv[pl.ds(corner + r, SIDE, stride=PITCH), :],
            d_conv[pl.ds(corner + far, SIDE, stride=PITCH), :],
        )
        for side in range(4):
            at = side * STRIP_ROWS + r * SIDE
            strips[at : at + SIDE, :] = rows[side].astype(BF16)
    for index in range(SIDE // BLOCK):
        stores += rows_out(index)
    for store in stores:
        store.wait()


def inner_body(
    scale, padded, d_conv, cotangent, mask, tap_table, d_weight_in, d_weight_out, d_bias_in, small,
    packed, d_fields_out, sums, shifted, taps, held, padded_in, d_conv_in, cotangent_in, mask_in, d_fields,
    in_sems, row_sems,
):
    loads = start_all(
        ((d_conv, d_conv_in), (padded, padded_in), (mask, mask_in), (cotangent, cotangent_in)), in_sems
    )
    d_conv, padded, mask, cotangent = d_conv_in, padded_in, mask_in, cotangent_in
    build_taps(tap_table, taps)
    loads[0].wait()
    shift_copies(d_conv, shifted)
    sums[...] = jnp.zeros_like(sums)
    for load in loads[1:]:
        load.wait()
    count = BLOCK // 2

    def step(index, carry):
        at = index * BLOCK
        both = conv_block(shifted, taps, index * count, count).reshape(count, SIDE, 256)
        for b in range(TAPS):
            part = [None] * TAPS
            for left in range(0, SIDE, 8):
                near = [
                    d_conv[pl.ds((at + i + RADIUS) * PITCH + RADIUS + left, 8), :] for i in range(BLOCK)
                ]
                for row in range(BLOCK + TAPS - 1):
                    piece = padded[pl.ds((at + row) * PITCH + left + b, 8), :]
                    for a in range(TAPS):
                        if 0 <= row - a < BLOCK:
                            term = piece * near[row - a]
                            part[a] = term if part[a] is None else part[a] + term
            for a in range(TAPS):
                sums[a * TAPS + b] += part[a]
        back = jnp.stack([both[:, :, :128], both[:, :, 128:]], axis=1).reshape(BLOCK, SIDE, 128)
        live = mask[pl.ds(at, BLOCK)].astype(F32)
        d_fields[pl.ds(at, BLOCK)] = live * (live * cotangent[pl.ds(at, BLOCK)].astype(F32) + back)
        rows_out(index).start()
        return carry

    def rows_out(index):
        rows = pl.ds(index * BLOCK, BLOCK)
        return pltpu.make_async_copy(d_fields.at[rows], d_fields_out.at[rows], row_sems.at[index])

    lax.fori_loop(0, SIDE // BLOCK, step, 0)
    for tile in range(4):
        across = slice(tile * 128, (tile + 1) * 128)
        held[tile * 128 : (tile + 1) * 128, :] = d_weight_in[:, across] * scale[0]
        held[512 + tile * 128 : 512 + (tile + 1) * 128, :] = d_weight_out[:, across].T * scale[0]
        at = AT_BIAS_IN + tile
        held[at : at + 1, :] = jnp.sum(d_bias_in[:, across], axis=0, keepdims=True) * scale[0]
    held[AT_KERNEL : AT_KERNEL + TAPS * TAPS, :] = jnp.sum(sums[...], axis=1) * scale[0]
    for i in range(5):
        at = AT_SMALL + i
        held[at : at + 1, :] = jnp.sum(small[8 * i : 8 * i + 8, :], axis=0, keepdims=True) * scale[0]
    held[AT_SMALL + 5 :, :] = jnp.zeros((held.shape[0] - AT_SMALL - 5, 128), F32)
    packed[...] = held[...].astype(packed.dtype)
    for index in range(SIDE // BLOCK):
        rows_out(index).wait()


def unpack_body(total, d_weight_in, d_weight_out, d_bias_in, d_kernel, *rest):
    small, held = rest[:5], rest[5]
    held[...] = total[...].astype(F32)
    for tile in range(4):
        across = slice(tile * 128, (tile + 1) * 128)
        d_weight_in[:, across] = held[tile * 128 : (tile + 1) * 128, :]
        at = AT_BIAS_IN + tile
        d_bias_in[:, across] = held[at : at + 1, :]
    d_weight_out[...] = held[512:1024, :]
    for a in range(TAPS):
        d_kernel[a] = held[AT_KERNEL + a * TAPS : AT_KERNEL + (a + 1) * TAPS, :]
    for i in range(5):
        small[i][...] = held[AT_SMALL + i : AT_SMALL + i + 1, :]


def edge_body(place, device, partial, arrived, mask_strips, weights, d_fields,
              frame, columns, beside, top, bottom, left, right, sems):
    inner = SIDE - 2 * RADIUS
    parts = (
        (top, (pl.ds(0, RADIUS),)),
        (bottom, (pl.ds(SIDE - RADIUS, RADIUS),)),
        (left, (pl.ds(RADIUS, inner), pl.ds(0, 8))),
        (right, (pl.ds(RADIUS, inner), pl.ds(SIDE - 8, 8))),
    )
    loads = [
        pltpu.make_async_copy(partial.at[where], held, sems.at[i])
        for i, (held, where) in enumerate(parts)
    ]
    for load in loads:
        load.start()
    pick = picker(place, device, arrived)
    frame[...] = jnp.zeros_like(frame)
    columns[...] = jnp.zeros_like(columns)
    for r in range(RADIUS):
        frame[0, r, RADIUS : RADIUS + SIDE, :] = pick(0, r)
        frame[1, r, RADIUS : RADIUS + SIDE, :] = pick(1, r)
        columns[0, r, RADIUS : RADIUS + SIDE, :] = pick(2, r)
        columns[1, r, RADIUS : RADIUS + SIDE, :] = pick(3, r)
        frame[0, r, 0:RADIUS, :] = pick(4, r)[SIDE - RADIUS :]
        frame[0, r, RADIUS + SIDE : 2 * RADIUS + SIDE, :] = pick(5, r)[:RADIUS]
        frame[1, r, 0:RADIUS, :] = pick(6, r)[SIDE - RADIUS :]
        frame[1, r, RADIUS + SIDE : 2 * RADIUS + SIDE, :] = pick(7, r)[:RADIUS]

    def rim(source, far, line, at, tap):
        total = None
        for r in range(RADIUS):
            across = r + 6 - line if far else r - line
            if 0 <= across < TAPS:
                for along in range(TAPS):
                    term = source[far, r, pl.ds(at + along, 8), :] * tap(across, along)
                    total = term if total is None else total + term
        return total

    def weight_row(a, b):
        return weights[a * TAPS + b : a * TAPS + b + 1, :]

    for load in loads:
        load.wait()

    def along(step, carry):
        at = pl.multiple_of(step * 8, 8)
        for line in range(RADIUS):
            for far, held in ((0, top), (1, bottom)):
                live = mask_strips[far, line, pl.ds(at, 8), :]
                add = rim(frame, far, line, at, weight_row)
                held[line, pl.ds(at, 8), :] += live * add
            for far in range(2):
                live = mask_strips[2 + far, line, pl.ds(at, 8), :]
                add = rim(columns, far, line, at, lambda across, along: weight_row(along, across))
                beside[far, line, pl.ds(at, 8), :] = live * add
        return carry

    lax.fori_loop(0, SIDE // 8, along, 0)
    for far, held in ((0, left), (1, right)):
        flat = held.reshape(inner * 8, 128)
        for line in range(RADIUS):
            column = 5 + line if far else line
            flat[pl.ds(column, inner, stride=8), :] += beside[far, line, RADIUS : SIDE - RADIUS, :]
            place = SIDE - RADIUS + line if far else line
            for i in range(RADIUS):
                top[i, place : place + 1, :] += beside[far, line, i : i + 1, :]
                low = SIDE - RADIUS + i
                bottom[i, place : place + 1, :] += beside[far, line, low : low + 1, :]
    stores = [
        pltpu.make_async_copy(held, d_fields.at[where], sems.at[i])
        for i, (held, where) in enumerate(parts)
    ]
    for store in stores:
        store.start()
    for store in stores:
        store.wait()


MIB = 1024 * 1024
IN_VMEM = pl.BlockSpec(memory_space=pltpu.VMEM)
IN_SMEM = pl.BlockSpec(memory_space=pltpu.SMEM)
ANYWHERE = pl.BlockSpec(memory_space=pl.ANY)


def params(mib):
    return pltpu.CompilerParams(vmem_limit_bytes=mib * MIB)


def run_outgoing(place, fields, ocean_mask):
    return pl.pallas_call(
        outgoing_body,
        out_shape=(
            jax.ShapeDtypeStruct((4 * STRIP_ROWS + 16, 128), BF16),
            jax.ShapeDtypeStruct((4, RADIUS, SIDE, 128), F32),
        ),
        in_specs=[IN_SMEM] + [IN_VMEM] * 2,
        out_specs=(IN_VMEM,) * 2,
        scratch_shapes=[pltpu.VMEM((SIDE * 16, 128), F32)] * 2,
        compiler_params=params(64),
        name="outgoing",
    )(place, fields, ocean_mask)


def run_mask(ocean_mask):
    return pl.pallas_call(
        mask_body,
        out_shape=jax.ShapeDtypeStruct((SIDE, SIDE, 128), BF16),
        in_specs=[IN_VMEM],
        out_specs=IN_VMEM,
        compiler_params=params(64),
        cost_estimate=pl.CostEstimate(flops=4_000_000_000, bytes_accessed=1_000_000, transcendentals=0),
        name="mask",
    )(ocean_mask)


def run_relay(place, device, lists, own, paired, other):
    return pl.pallas_call(
        relay_body,
        out_shape=jax.ShapeDtypeStruct((2 * GROUP * STRIP_ROWS, 128), BF16),
        in_specs=[IN_SMEM] * 3 + [IN_VMEM] * 3,
        out_specs=IN_VMEM,
        compiler_params=params(64),
        name="relay",
    )(place, device, lists, own, paired, other)


def run_core(place, device, fields, arrived, cotangent, mask, tap_table, vectors, weights):
    conv_bias, ln_gain, ln_bias, bias_in, bias_out, layer_scale = vectors
    weight_in, weight_out = weights
    shape = jax.ShapeDtypeStruct
    return pl.pallas_call(
        core_body,
        out_shape=(
            shape((SIDE, SIDE, 128), BF16),
            shape((ROWS * PITCH, 128), F32),
            shape((4 * STRIP_ROWS, 128), BF16),
            shape((ROWS * PITCH, 128), F32),
            shape((128, 512), F32),
            shape((128, 512), F32),
            shape((8, 512), F32),
            shape((40, 128), F32),
        ),
        in_specs=[IN_SMEM] * 2 + [ANYWHERE] * 4 + [IN_VMEM] * 9,
        out_specs=(ANYWHERE, ANYWHERE, IN_VMEM, ANYWHERE) + (IN_VMEM,) * 4,
        scratch_shapes=[
            pltpu.VMEM((TAPS, PAIRS, SIDE, 256), BF16),
            pltpu.VMEM((4 * SIDE, 128), F32),
            pltpu.VMEM((TAPS * 1024, 256), BF16),
            pltpu.VMEM((SIDE, SIDE, 128), BF16),
            pltpu.VMEM((2 * GROUP * STRIP_ROWS, 128), BF16),
            pltpu.VMEM((SIDE, SIDE, 128), BF16),
            pltpu.VMEM((SIDE, SIDE, 128), BF16),
            pltpu.VMEM((SIDE, SIDE, 128), BF16),
            pltpu.VMEM((ROWS * PITCH, 128), F32),
            pltpu.VMEM((ROWS * PITCH, 128), F32),
            pltpu.SemaphoreType.DMA((4,)),
            pltpu.SemaphoreType.DMA((3,)),
            pltpu.SemaphoreType.DMA((2, SIDE // BLOCK)),
        ],
        compiler_params=params(64),
        cost_estimate=pl.CostEstimate(flops=22_000_000_000, bytes_accessed=8_000_000, transcendentals=0),
        name="core",
    )(place, device, fields, arrived, cotangent, mask, tap_table, conv_bias, ln_gain, ln_bias,
      weight_in, bias_in, weight_out, bias_out, layer_scale)


def run_inner(rows, scale, padded, d_conv, cotangent, mask, tap_table, gradients):
    return pl.pallas_call(
        inner_body,
        out_shape=(
            jax.ShapeDtypeStruct((rows, 128), BF16),
            jax.ShapeDtypeStruct((SIDE, SIDE, 128), F32),
        ),
        in_specs=[IN_SMEM] + [ANYWHERE] * 4 + [IN_VMEM] * 5,
        out_specs=(IN_VMEM, ANYWHERE),
        scratch_shapes=[
            pltpu.VMEM((TAPS * TAPS, 8, 128), F32),
            pltpu.VMEM((TAPS, PAIRS, SIDE, 256), BF16),
            pltpu.VMEM((TAPS * 1024, 256), BF16),
            pltpu.VMEM((rows, 128), F32),
            pltpu.VMEM((ROWS * PITCH, 128), F32),
            pltpu.VMEM((ROWS * PITCH, 128), F32),
            pltpu.VMEM((SIDE, SIDE, 128), BF16),
            pltpu.VMEM((SIDE, SIDE, 128), BF16),
            pltpu.VMEM((SIDE, SIDE, 128), F32),
            pltpu.SemaphoreType.DMA((4,)),
            pltpu.SemaphoreType.DMA((SIDE // BLOCK,)),
        ],
        compiler_params=params(64),
        cost_estimate=pl.CostEstimate(flops=16_000_000_000, bytes_accessed=8_000_000, transcendentals=0),
        name="inner",
    )(scale, padded, d_conv, cotangent, mask, tap_table, *gradients)


def run_unpack(total):
    shape = jax.ShapeDtypeStruct
    return pl.pallas_call(
        unpack_body,
        out_shape=(
            shape((128, 512), F32),
            shape((512, 128), F32),
            shape((1, 512), F32),
            shape((TAPS, TAPS, 128), F32),
        )
        + (shape((1, 128), F32),) * 5,
        in_specs=[IN_VMEM],
        out_specs=(IN_VMEM,) * 9,
        scratch_shapes=[pltpu.VMEM(total.shape, F32)],
        compiler_params=params(6),
        name="unpack",
    )(total)


def run_edge(place, device, partial, arrived, mask_strips, weights):
    rim = pltpu.VMEM((RADIUS, SIDE, 128), F32)
    side = pltpu.VMEM((SIDE - 2 * RADIUS, 8, 128), F32)
    return pl.pallas_call(
        edge_body,
        out_shape=jax.ShapeDtypeStruct((SIDE, SIDE, 128), F32),
        in_specs=[IN_SMEM, IN_SMEM, ANYWHERE] + [IN_VMEM] * 3,
        out_specs=ANYWHERE,
        scratch_shapes=[
            pltpu.VMEM((2, RADIUS, PITCH, 128), F32),
            pltpu.VMEM((2, RADIUS, PITCH, 128), F32),
            pltpu.VMEM((2, RADIUS, SIDE, 128), F32),
            rim, rim, side, side,
            pltpu.SemaphoreType.DMA((4,)),
        ],
        input_output_aliases={2: 0},
        compiler_params=params(6),
        cost_estimate=pl.CostEstimate(flops=4_000_000_000, bytes_accessed=1_000_000, transcendentals=0),
        name="edge",
    )(place, device, partial, arrived, mask_strips, weights)


def swap_groups(value):
    groups = lax.axis_size("tiles") // GROUP

    def swap(first):
        pairs = []
        for low in range(first, groups - 1, 2):
            for i in range(low * GROUP, (low + 1) * GROUP):
                pairs += [(i, i + GROUP), (i + GROUP, i)]
        return lax.ppermute(value, "tiles", pairs)

    return swap(0), swap(1)


def within_group(blocks):
    peers = lax.axis_size("tiles")
    groups = [list(range(g, g + GROUP)) for g in range(0, peers, GROUP)]
    blocks = blocks.reshape(GROUP, -1, 128)
    return lax.all_to_all(blocks, "tiles", 0, 0, axis_index_groups=groups).reshape(-1, 128)


def sum_over_tiles(packed):
    peers = lax.axis_size("tiles")
    blocks = packed.reshape(peers, -1, 128)
    summed = jnp.sum(lax.all_to_all(blocks, "tiles", 0, 0).astype(F32), axis=0)
    shared = jnp.broadcast_to(summed.astype(BF16)[None], blocks.shape)
    return lax.all_to_all(shared, "tiles", 0, 0).reshape(packed.shape)


def per_device(
    fields,
    cotangent,
    ocean_mask,
    neighbours,
    kernel,
    conv_bias,
    ln_gain,
    ln_bias,
    weight_in,
    bias_in,
    weight_out,
    bias_out,
    layer_scale,
):
    peers = lax.axis_size("tiles")
    device = lax.axis_index("tiles").astype(jnp.int32).reshape(1)
    own, mask_strips = run_outgoing(neighbours, fields[0], ocean_mask[0])
    paired, other = swap_groups(own)
    mask = run_mask(ocean_mask[0])
    lists = jnp.stack([paired[-16, :8], other[-16, :8]]).astype(jnp.int32)
    arrived = within_group(run_relay(neighbours, device, lists, own, paired, other))
    vectors = [v.reshape(1, -1) for v in (conv_bias, ln_gain, ln_bias, bias_in, bias_out, layer_scale)]
    updated, d_conv, strips, padded, *gradients = run_core(
        neighbours, device, fields[0], arrived, cotangent[0], mask, tap_rows(kernel), vectors,
        (weight_in, weight_out),
    )
    paired, other = swap_groups(strips)
    blocks = run_relay(neighbours, device, lists, strips, paired, other)
    d_conv, blocks = lax.optimization_barrier((d_conv, blocks))
    arrived = within_group(blocks)
    flipped = kernel[::-1, ::-1]
    scale = jnp.full((1,), 1.0 / math.sqrt(peers * SIDE * SIDE), F32)
    rows = -(-PACKED_ROWS // (peers * 8)) * (peers * 8)
    packed, partial = run_inner(
        rows, scale, padded, d_conv, cotangent[0], mask, tap_rows(flipped), gradients
    )
    packed, arrived = lax.optimization_barrier((packed, arrived))
    weights = flipped.reshape(TAPS * TAPS, 128)
    d_fields = run_edge(neighbours, device, partial, arrived, mask_strips, weights)
    t_in, t_out, t_bias_in, t_kernel, *t_small = run_unpack(sum_over_tiles(packed))
    return (
        updated[None],
        d_fields[None],
        t_kernel,
        t_small[4][0],
        t_small[2][0],
        t_small[3][0],
        t_in,
        t_bias_in[0],
        t_out,
        t_small[1][0],
        t_small[0][0],
    )


def solution(mesh):
    placed = (
        P("tiles", None, None, None),
        P("tiles", None, None, None),
        P("tiles", None, None),
        P("tiles", None),
        P(),
        P(),
        P(),
        P(),
        P(),
        P(),
        P(),
        P(),
        P(),
    )
    return jax.shard_map(
        per_device,
        mesh=mesh,
        in_specs=placed,
        out_specs=(
            P("tiles", None, None, None),
            P("tiles", None, None, None),
            P(),
            P(),
            P(),
            P(),
            P(),
            P(),
            P(),
            P(),
            P(),
        ),
        check_vma=False,
    )
```

```python
import math

import jax
import jax.numpy as jnp
from jax import lax
from jax.experimental import pallas as pl
from jax.experimental.pallas import tpu as pltpu
from jax.sharding import PartitionSpec as P

EPS = 1e-06
GELU_K = 0.7978845608028654
GELU_C = 0.044715
CONTRACT_LAST = (((1,), (1,)), ((), ()))
CONTRACT_ROWS = (((0,), (0,)), ((), ()))
SIDE = 64
RADIUS = 3
STRIP_ROWS = RADIUS * SIDE
GROUP = 8
STRIP_FOR = (1, 0, 3, 2, 1, 1, 0, 0)
OPPOSITE = (1, 0, 3, 2, 7, 6, 5, 4)
TAPS = 7
PITCH = 72
ROWS = SIDE + 2 * RADIUS
PAIRS = ROWS // 2
BLOCK = 16
AT_KERNEL = 1024
AT_BIAS_IN = 1080
AT_SMALL = 1088
PACKED_ROWS = 1096
F32 = jnp.float32
BF16 = jnp.bfloat16


def tap_rows(kernel):
    wide = jnp.pad(kernel, ((1, 1), (0, 0), (0, 0)))
    both = jnp.concatenate([wide[1:9], wide[0:8]], axis=2)
    return both.transpose(1, 0, 2).reshape(TAPS * 8, 256)


def build_taps(rows, taps):
    shape = (128, 256)
    across = lax.broadcasted_iota(jnp.int32, shape, 1)
    down = lax.broadcasted_iota(jnp.int32, shape, 0)
    eye = ((across == down) | (across == down + 128)).astype(F32)

    def body(tap, carry):
        for position in range(8):
            at = tap * 8 + position
            taps[pl.ds(pl.multiple_of(at * 128, 128), 128), :] = (eye * rows[pl.ds(at, 1), :]).astype(BF16)
        return carry

    lax.fori_loop(0, TAPS, body, 0)


def place_strips(pick, padded, stage):
    for r in range(RADIUS):
        padded[r * PITCH + RADIUS : r * PITCH + RADIUS + SIDE, :] = pick(0, r)
        low = (RADIUS + SIDE + r) * PITCH
        padded[low + RADIUS : low + RADIUS + SIDE, :] = pick(1, r)
        padded[pl.ds(RADIUS * PITCH + r, SIDE, stride=PITCH), :] = pick(2, r)
        padded[pl.ds(RADIUS * PITCH + RADIUS + SIDE + r, SIDE, stride=PITCH), :] = pick(3, r)
        stage[0:SIDE, :] = pick(4, r)
        padded[r * PITCH : r * PITCH + RADIUS, :] = stage[SIDE - RADIUS : SIDE, :]
        stage[SIDE : 2 * SIDE, :] = pick(5, r)
        padded[r * PITCH + RADIUS + SIDE : r * PITCH + 2 * RADIUS + SIDE, :] = stage[SIDE : SIDE + RADIUS, :]
        stage[2 * SIDE : 3 * SIDE, :] = pick(6, r)
        padded[low : low + RADIUS, :] = stage[3 * SIDE - RADIUS : 3 * SIDE, :]
        stage[3 * SIDE : 4 * SIDE, :] = pick(7, r)
        padded[low + RADIUS + SIDE : low + 2 * RADIUS + SIDE, :] = stage[3 * SIDE : 3 * SIDE + RADIUS, :]


def shift_copies(padded, shifted):
    def body(pair, carry):
        for half in range(2):
            at = (2 * pair + half) * PITCH
            for tap in range(TAPS):
                row = padded[pl.ds(at + tap, SIDE), :].astype(BF16)
                shifted[tap, pair, :, half * 128 : (half + 1) * 128] = row
        return carry

    lax.fori_loop(0, PAIRS, body, 0)


def conv_block(shifted, taps, first, count):
    total = None
    for tap in range(TAPS):
        rows = [
            shifted[tap, pl.ds(first + move, count)].reshape(count * SIDE, 256) for move in range(4)
        ]
        part = jnp.dot(
            jnp.concatenate(rows, axis=1),
            taps[tap * 1024 : (tap + 1) * 1024, :],
            preferred_element_type=F32,
        )
        total = part if total is None else total + part
    return total


def picker(place, device, arrived, swapped):
    group = lax.div(device[0], GROUP)
    mine = lax.rem(device[0], GROUP)

    def pick(side, r):
        tile = place[0, side]
        owner = jnp.maximum(tile, 0)
        source = lax.rem(owner, GROUP)
        slot = 2 * (source ^ mine if swapped else source) + jnp.where(lax.div(owner, GROUP) != group, 1, 0)
        at = pl.multiple_of(slot * STRIP_ROWS + r * SIDE, SIDE)
        return jnp.where(tile >= 0, arrived[pl.ds(at, SIDE), :].astype(F32), 0.0)

    return pick


def arrivals(blocks, held):
    pairs = []
    for k in range(1, GROUP):
        pairs.append((blocks[k - 1], held.at[pl.ds(2 * k * STRIP_ROWS, 2 * STRIP_ROWS)]))
    return tuple(pairs)


def start_all(pairs, sems):
    copies = [pltpu.make_async_copy(src, dst, sems.at[i]) for i, (src, dst) in enumerate(pairs)]
    for copy in copies:
        copy.start()
    return copies


def mask_body(ocean_mask, mask):
    across = ocean_mask[...].astype(F32).T
    for i in range(SIDE):
        mask[i] = jnp.broadcast_to(across[:, i : i + 1], (SIDE, 128)).astype(BF16)


def outgoing_body(place, fields, ocean_mask, out, mask_strips, near, far):
    def fill(i, carry):
        near[pl.ds(i * 16, 16), :] = fields[i, 0:16, :].astype(F32)
        far[pl.ds(i * 16, 16), :] = fields[i, SIDE - 16 : SIDE, :].astype(F32)
        return carry

    lax.fori_loop(0, SIDE, fill, 0, unroll=4)
    live = ocean_mask[...].astype(F32)
    across = live.T
    for r in range(RADIUS):
        back = SIDE - RADIUS + r
        rows = (
            (fields[r].astype(F32), across[:, r : r + 1]),
            (fields[back].astype(F32), across[:, back : back + 1]),
            (near[pl.ds(r, SIDE, stride=16), :], live[:, r : r + 1]),
            (far[pl.ds(16 - RADIUS + r, SIDE, stride=16), :], live[:, back : back + 1]),
        )
        for side, (values, column) in enumerate(rows):
            at = side * STRIP_ROWS + r * SIDE
            wide = jnp.broadcast_to(column, (SIDE, 128))
            mask_strips[side, r] = wide
            out[at : at + SIDE, :] = (values * wide).astype(BF16)
    lane = lax.broadcasted_iota(jnp.int32, (16, 128), 1)
    listing = jnp.zeros((16, 128), F32)
    for side in range(8):
        listing = jnp.where(lane == side, place[0, side].astype(F32), listing)
    out[4 * STRIP_ROWS :, :] = listing.astype(BF16)


def strip_for(read, tile):
    strip = jnp.int32(0)
    for side in range(8):
        strip = jnp.where(read(side) == tile, STRIP_FOR[OPPOSITE[side]], strip)
    return pl.ds(pl.multiple_of(strip * STRIP_ROWS, STRIP_ROWS), STRIP_ROWS)


def relayed_strip(device, lists, paired, other, dest):
    group = lax.div(device[0], GROUP)
    use_pair = (dest < lax.rem(device[0], GROUP)) == (lax.rem(group, 2) == 1)
    rows = strip_for(lambda side: jnp.where(use_pair, lists[0, side], lists[1, side]), group * GROUP + dest)
    return jnp.where(use_pair, paired[rows, :], other[rows, :])


def relay_body(place, device, lists, own, paired, other, *out):
    group = lax.div(device[0], GROUP)
    mine = lax.rem(device[0], GROUP)
    for k in range(GROUP):
        if len(out) == 1:
            block, at, dest = out[0], 2 * k * STRIP_ROWS, k
        elif k:
            block, at, dest = out[k - 1], 0, mine ^ k
        else:
            continue
        rows = strip_for(lambda side: place[0, side], group * GROUP + dest)
        block[at : at + STRIP_ROWS, :] = own[rows, :]
        block[at + STRIP_ROWS : at + 2 * STRIP_ROWS, :] = relayed_strip(device, lists, paired, other, dest)


def core_body(
    place, device, fields, arrived, cotangent, mask, tap_table, conv_bias, ln_gain, ln_bias, weight_in,
    bias_in, weight_out, bias_out, layer_scale,
    updated_out, d_conv_out, strips, padded_out, d_weight_in, d_weight_out, d_bias_in, small,
    shifted, stage, taps, fields_in, arrived_in, cotangent_in, mask_in, updated, d_conv, padded,
    in_sems, out_sems, row_sems,
):
    loads = start_all(
        ((mask, mask_in), (fields, fields_in), (arrived, arrived_in), (cotangent, cotangent_in)), in_sems
    )
    mask, fields, arrived, cotangent = mask_in, fields_in, arrived_in, cotangent_in
    build_taps(tap_table, taps)
    for load in loads[:-1]:
        load.wait()
    place_strips(picker(place, device, arrived, False), padded, stage)

    def fill(i, carry):
        padded[pl.ds((i + RADIUS) * PITCH + RADIUS, SIDE), :] = fields[i].astype(F32) * mask[i].astype(F32)
        return carry

    lax.fori_loop(0, SIDE, fill, 0)
    stores = start_all(((padded, padded_out),), out_sems)
    shift_copies(padded, shifted)
    loads[-1].wait()
    d_weight_in[...] = jnp.zeros_like(d_weight_in)
    d_weight_out[...] = jnp.zeros_like(d_weight_out)
    d_bias_in[...] = jnp.zeros_like(d_bias_in)
    small[...] = jnp.zeros_like(small)
    d_conv[...] = jnp.zeros_like(d_conv)
    half_in = weight_in[...] * jnp.bfloat16(0.5)
    half_bias = bias_in[...] * 0.5
    count = BLOCK // 2
    points = BLOCK * SIDE

    def by_half(ref, at):
        part = ref[pl.ds(at, BLOCK)].astype(F32).reshape(count, 2, SIDE, 128)
        return jnp.concatenate([part[:, 0], part[:, 1]], axis=0).reshape(points, 128)

    def by_row(value):
        part = value.reshape(2, count, SIDE, 128)
        return jnp.stack([part[0], part[1]], axis=1).reshape(BLOCK, SIDE, 128)

    def fold(value):
        return jnp.sum(value.reshape(-1, 8, value.shape[-1]), axis=0)

    def step(index, both, last=False):
        at = index * BLOCK
        conv = jnp.concatenate([both[:, :128], both[:, 128:]], axis=0) + conv_bias[...]
        following = both if last else conv_block(shifted, taps, (index + 1) * count, count)
        live = by_half(mask, at)
        signal = by_half(cotangent, at) * live
        centred = conv - jnp.mean(conv, axis=-1, keepdims=True)
        inv_std = lax.rsqrt(jnp.mean(centred * centred, axis=-1, keepdims=True) + EPS)
        normed = centred * inv_std
        lifted = (normed * ln_gain[...] + ln_bias[...]).astype(BF16)
        half = jnp.dot(lifted, half_in, preferred_element_type=F32) + half_bias
        square = half * half
        tanh_part = jnp.tanh(half * (2.0 * GELU_K + 8.0 * GELU_K * GELU_C * square))
        above = 1.0 + tanh_part
        activated = (half * above).astype(BF16)
        slope = above * (
            0.5 + (half * (GELU_K + 12.0 * GELU_K * GELU_C * square)) * (1.0 - tanh_part)
        )
        branch = jnp.dot(activated, weight_out[...], preferred_element_type=F32) + bias_out[...]
        d_branch = signal * layer_scale[...]
        branch_low = d_branch.astype(BF16)
        d_hidden = slope * lax.dot_general(
            branch_low, weight_out[...], CONTRACT_LAST, preferred_element_type=F32
        )
        hidden_low = d_hidden.astype(BF16)
        d_lifted = lax.dot_general(
            hidden_low, weight_in[...], CONTRACT_LAST, preferred_element_type=F32
        )
        d_normed = d_lifted * ln_gain[...]
        d_out = inv_std * (
            d_normed
            - jnp.mean(d_normed, axis=-1, keepdims=True)
            - normed * jnp.mean(d_normed * normed, axis=-1, keepdims=True)
        )
        masked = by_half(fields, at) * live
        updated[pl.ds(at, BLOCK)] = by_row(live * (masked + layer_scale[...] * branch)).astype(BF16)
        rows = by_row(d_out)
        for i in range(BLOCK):
            d_conv[pl.ds((at + i + RADIUS) * PITCH + RADIUS, SIDE), :] = rows[i]
        d_weight_out[...] += lax.dot_general(
            branch_low, activated, CONTRACT_ROWS, preferred_element_type=F32
        )
        d_weight_in[...] += lax.dot_general(
            lifted, hidden_low, CONTRACT_ROWS, preferred_element_type=F32
        )
        d_bias_in[...] += fold(d_hidden)
        small[0:8] += fold(signal * branch)
        small[8:16] += fold(d_branch)
        small[16:24] += fold(d_lifted * normed)
        small[24:32] += fold(d_lifted)
        small[32:40] += fold(d_out)
        for store in rows_out(index):
            store.start()
        return following

    def rows_out(index):
        rows = pl.ds(index * BLOCK, BLOCK)
        wide = pl.ds(pl.multiple_of((index * BLOCK + RADIUS) * PITCH, 8), BLOCK * PITCH)
        return (
            pltpu.make_async_copy(updated.at[rows], updated_out.at[rows], row_sems.at[0, index]),
            pltpu.make_async_copy(d_conv.at[wide], d_conv_out.at[wide], row_sems.at[1, index]),
        )

    both = conv_block(shifted, taps, 0, count)
    both = lax.fori_loop(0, SIDE // BLOCK - 1, step, both)
    step(SIDE // BLOCK - 1, both, last=True)
    edge = RADIUS * PITCH
    for i, rows in enumerate((pl.ds(0, edge), pl.ds(edge + SIDE * PITCH, edge))):
        store = pltpu.make_async_copy(d_conv.at[rows], d_conv_out.at[rows], out_sems.at[1 + i])
        store.start()
        stores.append(store)
    for r in range(RADIUS):
        corner = RADIUS * PITCH + RADIUS
        far = SIDE - RADIUS + r
        rows = (
            d_conv[corner + r * PITCH : corner + r * PITCH + SIDE, :],
            d_conv[corner + far * PITCH : corner + far * PITCH + SIDE, :],
            d_conv[pl.ds(corner + r, SIDE, stride=PITCH), :],
            d_conv[pl.ds(corner + far, SIDE, stride=PITCH), :],
        )
        for side in range(4):
            at = side * STRIP_ROWS + r * SIDE
            strips[at : at + SIDE, :] = rows[side].astype(BF16)
    for index in range(SIDE // BLOCK):
        stores += rows_out(index)
    for store in stores:
        store.wait()


def inner_body(
    scale, padded, d_conv, cotangent, mask, tap_table, d_weight_in, d_weight_out, d_bias_in, small,
    packed, d_fields_out, sums, shifted, taps, held, padded_in, d_conv_in, cotangent_in, mask_in, d_fields,
    in_sems, row_sems,
):
    loads = start_all(
        ((d_conv, d_conv_in), (padded, padded_in), (mask, mask_in), (cotangent, cotangent_in)), in_sems
    )
    d_conv, padded, mask, cotangent = d_conv_in, padded_in, mask_in, cotangent_in
    build_taps(tap_table, taps)
    loads[0].wait()
    shift_copies(d_conv, shifted)
    sums[...] = jnp.zeros_like(sums)
    for load in loads[1:]:
        load.wait()
    count = BLOCK // 2

    def step(index, carry):
        at = index * BLOCK
        both = conv_block(shifted, taps, index * count, count).reshape(count, SIDE, 256)
        for b in range(TAPS):
            part = [None] * TAPS
            for left in range(0, SIDE, 8):
                near = [
                    d_conv[pl.ds((at + i + RADIUS) * PITCH + RADIUS + left, 8), :] for i in range(BLOCK)
                ]
                for row in range(BLOCK + TAPS - 1):
                    piece = padded[pl.ds((at + row) * PITCH + left + b, 8), :]
                    for a in range(TAPS):
                        if 0 <= row - a < BLOCK:
                            term = piece * near[row - a]
                            part[a] = term if part[a] is None else part[a] + term
            for a in range(TAPS):
                sums[a * TAPS + b] += part[a]
        back = jnp.stack([both[:, :, :128], both[:, :, 128:]], axis=1).reshape(BLOCK, SIDE, 128)
        live = mask[pl.ds(at, BLOCK)].astype(F32)
        d_fields[pl.ds(at, BLOCK)] = live * (live * cotangent[pl.ds(at, BLOCK)].astype(F32) + back)
        rows_out(index).start()
        return carry

    def rows_out(index):
        rows = pl.ds(index * BLOCK, BLOCK)
        return pltpu.make_async_copy(d_fields.at[rows], d_fields_out.at[rows], row_sems.at[index])

    lax.fori_loop(0, SIDE // BLOCK, step, 0)
    for tile in range(4):
        across = slice(tile * 128, (tile + 1) * 128)
        held[tile * 128 : (tile + 1) * 128, :] = d_weight_in[:, across] * scale[0]
        held[512 + tile * 128 : 512 + (tile + 1) * 128, :] = d_weight_out[:, across].T * scale[0]
        at = AT_BIAS_IN + tile
        held[at : at + 1, :] = jnp.sum(d_bias_in[:, across], axis=0, keepdims=True) * scale[0]
    held[AT_KERNEL : AT_KERNEL + TAPS * TAPS, :] = jnp.sum(sums[...], axis=1) * scale[0]
    for i in range(5):
        at = AT_SMALL + i
        held[at : at + 1, :] = jnp.sum(small[8 * i : 8 * i + 8, :], axis=0, keepdims=True) * scale[0]
    held[AT_SMALL + 5 :, :] = jnp.zeros((held.shape[0] - AT_SMALL - 5, 128), F32)
    packed[...] = held[...].astype(packed.dtype)
    for index in range(SIDE // BLOCK):
        rows_out(index).wait()


def unpack_body(total, d_weight_in, d_weight_out, d_bias_in, d_kernel, *rest):
    small, held = rest[:5], rest[5]
    held[...] = total[...].astype(F32)
    for tile in range(4):
        across = slice(tile * 128, (tile + 1) * 128)
        d_weight_in[:, across] = held[tile * 128 : (tile + 1) * 128, :]
        at = AT_BIAS_IN + tile
        d_bias_in[:, across] = held[at : at + 1, :]
    d_weight_out[...] = held[512:1024, :]
    for a in range(TAPS):
        d_kernel[a] = held[AT_KERNEL + a * TAPS : AT_KERNEL + (a + 1) * TAPS, :]
    for i in range(5):
        small[i][...] = held[AT_SMALL + i : AT_SMALL + i + 1, :]


def edge_body(place, device, partial, a1, a2, a3, a4, a5, a6, a7, mask_strips, weights, d_fields,
              frame, columns, beside, top, bottom, left, right, sems, arrived, in_sems):
    waits = start_all(arrivals((a1, a2, a3, a4, a5, a6, a7), arrived), in_sems)
    arrived[0 : 2 * STRIP_ROWS, :] = jnp.zeros((2 * STRIP_ROWS, 128), BF16)
    inner = SIDE - 2 * RADIUS
    parts = (
        (top, (pl.ds(0, RADIUS),)),
        (bottom, (pl.ds(SIDE - RADIUS, RADIUS),)),
        (left, (pl.ds(RADIUS, inner), pl.ds(0, 8))),
        (right, (pl.ds(RADIUS, inner), pl.ds(SIDE - 8, 8))),
    )
    loads = [
        pltpu.make_async_copy(partial.at[where], held, sems.at[i])
        for i, (held, where) in enumerate(parts)
    ]
    for load in loads:
        load.start()
    pick = picker(place, device, arrived, True)
    frame[...] = jnp.zeros_like(frame)
    columns[...] = jnp.zeros_like(columns)
    for wait in waits:
        wait.wait()
    for r in range(RADIUS):
        frame[0, r, RADIUS : RADIUS + SIDE, :] = pick(0, r)
        frame[1, r, RADIUS : RADIUS + SIDE, :] = pick(1, r)
        columns[0, r, RADIUS : RADIUS + SIDE, :] = pick(2, r)
        columns[1, r, RADIUS : RADIUS + SIDE, :] = pick(3, r)
        frame[0, r, 0:RADIUS, :] = pick(4, r)[SIDE - RADIUS :]
        frame[0, r, RADIUS + SIDE : 2 * RADIUS + SIDE, :] = pick(5, r)[:RADIUS]
        frame[1, r, 0:RADIUS, :] = pick(6, r)[SIDE - RADIUS :]
        frame[1, r, RADIUS + SIDE : 2 * RADIUS + SIDE, :] = pick(7, r)[:RADIUS]

    def rim(source, far, line, at, tap):
        total = None
        for r in range(RADIUS):
            across = r + 6 - line if far else r - line
            if 0 <= across < TAPS:
                for along in range(TAPS):
                    term = source[far, r, pl.ds(at + along, 8), :] * tap(across, along)
                    total = term if total is None else total + term
        return total

    def weight_row(a, b):
        return weights[a * TAPS + b : a * TAPS + b + 1, :]

    for load in loads:
        load.wait()

    def along(step, carry):
        at = pl.multiple_of(step * 8, 8)
        for line in range(RADIUS):
            for far, held in ((0, top), (1, bottom)):
                live = mask_strips[far, line, pl.ds(at, 8), :]
                add = rim(frame, far, line, at, weight_row)
                held[line, pl.ds(at, 8), :] += live * add
            for far in range(2):
                live = mask_strips[2 + far, line, pl.ds(at, 8), :]
                add = rim(columns, far, line, at, lambda across, along: weight_row(along, across))
                beside[far, line, pl.ds(at, 8), :] = live * add
        return carry

    lax.fori_loop(0, SIDE // 8, along, 0)
    for far, held in ((0, left), (1, right)):
        flat = held.reshape(inner * 8, 128)
        for line in range(RADIUS):
            column = 5 + line if far else line
            flat[pl.ds(column, inner, stride=8), :] += beside[far, line, RADIUS : SIDE - RADIUS, :]
            place = SIDE - RADIUS + line if far else line
            for i in range(RADIUS):
                top[i, place : place + 1, :] += beside[far, line, i : i + 1, :]
                low = SIDE - RADIUS + i
                bottom[i, place : place + 1, :] += beside[far, line, low : low + 1, :]
    stores = [
        pltpu.make_async_copy(held, d_fields.at[where], sems.at[i])
        for i, (held, where) in enumerate(parts)
    ]
    for store in stores:
        store.start()
    for store in stores:
        store.wait()


MIB = 1024 * 1024
IN_VMEM = pl.BlockSpec(memory_space=pltpu.VMEM)
IN_SMEM = pl.BlockSpec(memory_space=pltpu.SMEM)
ANYWHERE = pl.BlockSpec(memory_space=pl.ANY)


def params(mib):
    return pltpu.CompilerParams(vmem_limit_bytes=mib * MIB)


def run_outgoing(place, fields, ocean_mask):
    return pl.pallas_call(
        outgoing_body,
        out_shape=(
            jax.ShapeDtypeStruct((4 * STRIP_ROWS + 16, 128), BF16),
            jax.ShapeDtypeStruct((4, RADIUS, SIDE, 128), F32),
        ),
        in_specs=[IN_SMEM] + [IN_VMEM] * 2,
        out_specs=(IN_VMEM,) * 2,
        scratch_shapes=[pltpu.VMEM((SIDE * 16, 128), F32)] * 2,
        compiler_params=params(64),
        name="outgoing",
    )(place, fields, ocean_mask)


def run_mask(ocean_mask):
    return pl.pallas_call(
        mask_body,
        out_shape=jax.ShapeDtypeStruct((SIDE, SIDE, 128), BF16),
        in_specs=[IN_VMEM],
        out_specs=IN_VMEM,
        compiler_params=params(64),
        cost_estimate=pl.CostEstimate(flops=4_000_000_000, bytes_accessed=1_000_000, transcendentals=0),
        name="mask",
    )(ocean_mask)


def run_relay(place, device, lists, own, paired, other, swapped):
    pair = 2 * STRIP_ROWS
    shapes = [(pair, 128)] * (GROUP - 1) if swapped else [(GROUP * pair, 128)]
    return pl.pallas_call(
        relay_body,
        out_shape=tuple(jax.ShapeDtypeStruct(shape, BF16) for shape in shapes),
        in_specs=[IN_SMEM] * 3 + [IN_VMEM] * 3,
        out_specs=(IN_VMEM,) * len(shapes),
        compiler_params=params(64),
        cost_estimate=pl.CostEstimate(flops=2_000_000_000, bytes_accessed=1_000_000, transcendentals=0),
        name="relay",
    )(place, device, lists, own, paired, other)


def run_core(place, device, fields, arrived, cotangent, mask, tap_table, vectors, weights):
    conv_bias, ln_gain, ln_bias, bias_in, bias_out, layer_scale = vectors
    weight_in, weight_out = weights
    shape = jax.ShapeDtypeStruct
    return pl.pallas_call(
        core_body,
        out_shape=(
            shape((SIDE, SIDE, 128), BF16),
            shape((ROWS * PITCH, 128), F32),
            shape((4 * STRIP_ROWS, 128), BF16),
            shape((ROWS * PITCH, 128), F32),
            shape((128, 512), F32),
            shape((128, 512), F32),
            shape((8, 512), F32),
            shape((40, 128), F32),
        ),
        in_specs=[IN_SMEM] * 2 + [ANYWHERE] * 4 + [IN_VMEM] * 9,
        out_specs=(ANYWHERE, ANYWHERE, IN_VMEM, ANYWHERE) + (IN_VMEM,) * 4,
        scratch_shapes=[
            pltpu.VMEM((TAPS, PAIRS, SIDE, 256), BF16),
            pltpu.VMEM((4 * SIDE, 128), F32),
            pltpu.VMEM((TAPS * 1024, 256), BF16),
            pltpu.VMEM((SIDE, SIDE, 128), BF16),
            pltpu.VMEM((2 * GROUP * STRIP_ROWS, 128), BF16),
            pltpu.VMEM((SIDE, SIDE, 128), BF16),
            pltpu.VMEM((SIDE, SIDE, 128), BF16),
            pltpu.VMEM((SIDE, SIDE, 128), BF16),
            pltpu.VMEM((ROWS * PITCH, 128), F32),
            pltpu.VMEM((ROWS * PITCH, 128), F32),
            pltpu.SemaphoreType.DMA((4,)),
            pltpu.SemaphoreType.DMA((3,)),
            pltpu.SemaphoreType.DMA((2, SIDE // BLOCK)),
        ],
        compiler_params=params(64),
        cost_estimate=pl.CostEstimate(flops=22_000_000_000, bytes_accessed=8_000_000, transcendentals=0),
        name="core",
    )(place, device, fields, arrived, cotangent, mask, tap_table, conv_bias, ln_gain, ln_bias,
      weight_in, bias_in, weight_out, bias_out, layer_scale)


def run_inner(rows, scale, padded, d_conv, cotangent, mask, tap_table, gradients):
    return pl.pallas_call(
        inner_body,
        out_shape=(
            jax.ShapeDtypeStruct((rows, 128), BF16),
            jax.ShapeDtypeStruct((SIDE, SIDE, 128), F32),
        ),
        in_specs=[IN_SMEM] + [ANYWHERE] * 4 + [IN_VMEM] * 5,
        out_specs=(IN_VMEM, ANYWHERE),
        scratch_shapes=[
            pltpu.VMEM((TAPS * TAPS, 8, 128), F32),
            pltpu.VMEM((TAPS, PAIRS, SIDE, 256), BF16),
            pltpu.VMEM((TAPS * 1024, 256), BF16),
            pltpu.VMEM((rows, 128), F32),
            pltpu.VMEM((ROWS * PITCH, 128), F32),
            pltpu.VMEM((ROWS * PITCH, 128), F32),
            pltpu.VMEM((SIDE, SIDE, 128), BF16),
            pltpu.VMEM((SIDE, SIDE, 128), BF16),
            pltpu.VMEM((SIDE, SIDE, 128), F32),
            pltpu.SemaphoreType.DMA((4,)),
            pltpu.SemaphoreType.DMA((SIDE // BLOCK,)),
        ],
        compiler_params=params(64),
        cost_estimate=pl.CostEstimate(flops=16_000_000_000, bytes_accessed=8_000_000, transcendentals=0),
        name="inner",
    )(scale, padded, d_conv, cotangent, mask, tap_table, *gradients)


def run_unpack(total):
    shape = jax.ShapeDtypeStruct
    return pl.pallas_call(
        unpack_body,
        out_shape=(
            shape((128, 512), F32),
            shape((512, 128), F32),
            shape((1, 512), F32),
            shape((TAPS, TAPS, 128), F32),
        )
        + (shape((1, 128), F32),) * 5,
        in_specs=[IN_VMEM],
        out_specs=(IN_VMEM,) * 9,
        scratch_shapes=[pltpu.VMEM(total.shape, F32)],
        compiler_params=params(6),
        name="unpack",
    )(total)


def run_edge(place, device, partial, arrived, mask_strips, weights):
    rim = pltpu.VMEM((RADIUS, SIDE, 128), F32)
    side = pltpu.VMEM((SIDE - 2 * RADIUS, 8, 128), F32)
    return pl.pallas_call(
        edge_body,
        out_shape=jax.ShapeDtypeStruct((SIDE, SIDE, 128), F32),
        in_specs=[IN_SMEM, IN_SMEM, ANYWHERE] + [ANYWHERE] * 7 + [IN_VMEM] * 2,
        out_specs=ANYWHERE,
        scratch_shapes=[
            pltpu.VMEM((2, RADIUS, PITCH, 128), F32),
            pltpu.VMEM((2, RADIUS, PITCH, 128), F32),
            pltpu.VMEM((2, RADIUS, SIDE, 128), F32),
            rim, rim, side, side,
            pltpu.SemaphoreType.DMA((4,)),
            pltpu.VMEM((2 * GROUP * STRIP_ROWS, 128), BF16),
            pltpu.SemaphoreType.DMA((GROUP - 1,)),
        ],
        input_output_aliases={2: 0},
        compiler_params=params(6),
        cost_estimate=pl.CostEstimate(flops=4_000_000_000, bytes_accessed=1_000_000, transcendentals=0),
        name="edge",
    )(place, device, partial, *arrived, mask_strips, weights)


def swap_groups(value):
    groups = lax.axis_size("tiles") // GROUP

    def swap(first):
        pairs = []
        for low in range(first, groups - 1, 2):
            for i in range(low * GROUP, (low + 1) * GROUP):
                pairs += [(i, i + GROUP), (i + GROUP, i)]
        return lax.ppermute(value, "tiles", pairs)

    return swap(0), swap(1)


def within_group(blocks):
    peers = lax.axis_size("tiles")
    groups = [list(range(g, g + GROUP)) for g in range(0, peers, GROUP)]
    blocks = blocks.reshape(GROUP, -1, 128)
    return lax.all_to_all(blocks, "tiles", 0, 0, axis_index_groups=groups).reshape(-1, 128)


def swap_within_group(blocks):
    peers = lax.axis_size("tiles")
    return [
        lax.ppermute(block, "tiles", [(i, i ^ k) for i in range(peers)])
        for k, block in enumerate(blocks, start=1)
    ]


def sum_over_tiles(packed, tie):
    peers = lax.axis_size("tiles")
    blocks = packed.reshape(peers, -1, 128)
    summed = jnp.sum(lax.all_to_all(blocks, "tiles", 0, 0).astype(F32), axis=0)
    summed, *tie = lax.optimization_barrier((summed, *tie))
    shared = jnp.broadcast_to(summed.astype(BF16)[None], blocks.shape)
    return lax.all_to_all(shared, "tiles", 0, 0).reshape(packed.shape), tie


def per_device(
    fields,
    cotangent,
    ocean_mask,
    neighbours,
    kernel,
    conv_bias,
    ln_gain,
    ln_bias,
    weight_in,
    bias_in,
    weight_out,
    bias_out,
    layer_scale,
):
    peers = lax.axis_size("tiles")
    device = lax.axis_index("tiles").astype(jnp.int32).reshape(1)
    own, mask_strips = run_outgoing(neighbours, fields[0], ocean_mask[0])
    paired, other = swap_groups(own)
    mask = run_mask(ocean_mask[0])
    lists = jnp.stack([paired[-16, :8], other[-16, :8]]).astype(jnp.int32)
    (blocks,) = run_relay(neighbours, device, lists, own, paired, other, False)
    arrived = within_group(blocks)
    vectors = [v.reshape(1, -1) for v in (conv_bias, ln_gain, ln_bias, bias_in, bias_out, layer_scale)]
    updated, d_conv, strips, padded, *gradients = run_core(
        neighbours, device, fields[0], arrived, cotangent[0], mask, tap_rows(kernel), vectors,
        (weight_in, weight_out),
    )
    paired, other = swap_groups(strips)
    flipped = kernel[::-1, ::-1]
    scale = jnp.full((1,), 1.0 / math.sqrt(peers * SIDE * SIDE), F32)
    rows = -(-PACKED_ROWS // (peers * 8)) * (peers * 8)
    packed, partial = run_inner(
        rows, scale, padded, d_conv, cotangent[0], mask, tap_rows(flipped), gradients
    )
    packed, paired, other = lax.optimization_barrier((packed, paired, other))
    arrived = swap_within_group(run_relay(neighbours, device, lists, strips, paired, other, True))
    weights = flipped.reshape(TAPS * TAPS, 128)
    total, arrived = sum_over_tiles(packed, arrived)
    d_fields = run_edge(neighbours, device, partial, arrived, mask_strips, weights)
    t_in, t_out, t_bias_in, t_kernel, *t_small = run_unpack(total)
    return (
        updated[None],
        d_fields[None],
        t_kernel,
        t_small[4][0],
        t_small[2][0],
        t_small[3][0],
        t_in,
        t_bias_in[0],
        t_out,
        t_small[1][0],
        t_small[0][0],
    )


def solution(mesh):
    placed = (
        P("tiles", None, None, None),
        P("tiles", None, None, None),
        P("tiles", None, None),
        P("tiles", None),
        P(),
        P(),
        P(),
        P(),
        P(),
        P(),
        P(),
        P(),
        P(),
    )
    return jax.shard_map(
        per_device,
        mesh=mesh,
        in_specs=placed,
        out_specs=(
            P("tiles", None, None, None),
            P("tiles", None, None, None),
            P(),
            P(),
            P(),
            P(),
            P(),
            P(),
            P(),
            P(),
            P(),
        ),
        check_vma=False,
    )
```

```python
import math

import jax
import jax.numpy as jnp
from jax import lax
from jax.experimental import pallas as pl
from jax.experimental.pallas import tpu as pltpu
from jax.sharding import PartitionSpec as P

EPS = 1e-06
GELU_K = 0.7978845608028654
GELU_C = 0.044715
CONTRACT_LAST = (((1,), (1,)), ((), ()))
CONTRACT_ROWS = (((0,), (0,)), ((), ()))
SIDE = 64
RADIUS = 3
STRIP_ROWS = RADIUS * SIDE
GROUP = 8
STRIP_FOR = (1, 0, 3, 2, 1, 1, 0, 0)
OPPOSITE = (1, 0, 3, 2, 7, 6, 5, 4)
TAPS = 7
PITCH = 72
ROWS = SIDE + 2 * RADIUS
PAIRS = ROWS // 2
BLOCK = 16
AT_KERNEL = 1024
AT_BIAS_IN = 1080
AT_SMALL = 1088
PACKED_ROWS = 1096
F32 = jnp.float32
BF16 = jnp.bfloat16


def tap_rows(kernel):
    wide = jnp.pad(kernel, ((1, 1), (0, 0), (0, 0)))
    both = jnp.concatenate([wide[1:9], wide[0:8]], axis=2)
    return both.transpose(1, 0, 2).reshape(TAPS * 8, 256)


def build_taps(rows, taps):
    shape = (128, 256)
    across = lax.broadcasted_iota(jnp.int32, shape, 1)
    down = lax.broadcasted_iota(jnp.int32, shape, 0)
    eye = ((across == down) | (across == down + 128)).astype(F32)

    def body(tap, carry):
        for position in range(8):
            at = tap * 8 + position
            taps[pl.ds(pl.multiple_of(at * 128, 128), 128), :] = (eye * rows[pl.ds(at, 1), :]).astype(BF16)
        return carry

    lax.fori_loop(0, TAPS, body, 0)


def place_strips(pick, padded, stage):
    for r in range(RADIUS):
        padded[r * PITCH + RADIUS : r * PITCH + RADIUS + SIDE, :] = pick(0, r)
        low = (RADIUS + SIDE + r) * PITCH
        padded[low + RADIUS : low + RADIUS + SIDE, :] = pick(1, r)
        padded[pl.ds(RADIUS * PITCH + r, SIDE, stride=PITCH), :] = pick(2, r)
        padded[pl.ds(RADIUS * PITCH + RADIUS + SIDE + r, SIDE, stride=PITCH), :] = pick(3, r)
        stage[0:SIDE, :] = pick(4, r)
        padded[r * PITCH : r * PITCH + RADIUS, :] = stage[SIDE - RADIUS : SIDE, :]
        stage[SIDE : 2 * SIDE, :] = pick(5, r)
        padded[r * PITCH + RADIUS + SIDE : r * PITCH + 2 * RADIUS + SIDE, :] = stage[SIDE : SIDE + RADIUS, :]
        stage[2 * SIDE : 3 * SIDE, :] = pick(6, r)
        padded[low : low + RADIUS, :] = stage[3 * SIDE - RADIUS : 3 * SIDE, :]
        stage[3 * SIDE : 4 * SIDE, :] = pick(7, r)
        padded[low + RADIUS + SIDE : low + 2 * RADIUS + SIDE, :] = stage[3 * SIDE : 3 * SIDE + RADIUS, :]


def shift_copies(padded, shifted):
    def body(pair, carry):
        for half in range(2):
            at = (2 * pair + half) * PITCH
            for tap in range(TAPS):
                row = padded[pl.ds(at + tap, SIDE), :].astype(BF16)
                shifted[tap, pair, :, half * 128 : (half + 1) * 128] = row
        return carry

    lax.fori_loop(0, PAIRS, body, 0)


def conv_block(shifted, taps, first, count):
    total = None
    for tap in range(TAPS):
        rows = [
            shifted[tap, pl.ds(first + move, count)].reshape(count * SIDE, 256) for move in range(4)
        ]
        part = jnp.dot(
            jnp.concatenate(rows, axis=1),
            taps[tap * 1024 : (tap + 1) * 1024, :],
            preferred_element_type=F32,
        )
        total = part if total is None else total + part
    return total


def picker(place, device, arrived, swapped):
    group = lax.div(device[0], GROUP)
    mine = lax.rem(device[0], GROUP)

    def pick(side, r):
        tile = place[0, side]
        owner = jnp.maximum(tile, 0)
        source = lax.rem(owner, GROUP)
        slot = 2 * (source ^ mine if swapped else source) + jnp.where(lax.div(owner, GROUP) != group, 1, 0)
        at = pl.multiple_of(slot * STRIP_ROWS + r * SIDE, SIDE)
        return jnp.where(tile >= 0, arrived[pl.ds(at, SIDE), :].astype(F32), 0.0)

    return pick


def arrivals(blocks, held):
    pairs = []
    for k in range(1, GROUP):
        pairs.append((blocks[k - 1], held.at[pl.ds(2 * k * STRIP_ROWS, 2 * STRIP_ROWS)]))
    return tuple(pairs)


def start_all(pairs, sems):
    copies = [pltpu.make_async_copy(src, dst, sems.at[i]) for i, (src, dst) in enumerate(pairs)]
    for copy in copies:
        copy.start()
    return copies


def mask_body(ocean_mask, fields, cotangent, mask, masked, signal):
    across = ocean_mask[...].astype(F32).T
    for i in range(SIDE):
        live = jnp.broadcast_to(across[:, i : i + 1], (SIDE, 128))
        mask[i] = live.astype(BF16)
        masked[i] = (fields[i].astype(F32) * live).astype(BF16)
        signal[i] = (cotangent[i].astype(F32) * live).astype(BF16)


def outgoing_body(place, fields, ocean_mask, out, mask_strips, near, far):
    def fill(i, carry):
        near[pl.ds(i * 16, 16), :] = fields[i, 0:16, :].astype(F32)
        far[pl.ds(i * 16, 16), :] = fields[i, SIDE - 16 : SIDE, :].astype(F32)
        return carry

    lax.fori_loop(0, SIDE, fill, 0, unroll=4)
    live = ocean_mask[...].astype(F32)
    across = live.T
    for r in range(RADIUS):
        back = SIDE - RADIUS + r
        rows = (
            (fields[r].astype(F32), across[:, r : r + 1]),
            (fields[back].astype(F32), across[:, back : back + 1]),
            (near[pl.ds(r, SIDE, stride=16), :], live[:, r : r + 1]),
            (far[pl.ds(16 - RADIUS + r, SIDE, stride=16), :], live[:, back : back + 1]),
        )
        for side, (values, column) in enumerate(rows):
            at = side * STRIP_ROWS + r * SIDE
            wide = jnp.broadcast_to(column, (SIDE, 128))
            mask_strips[side, r] = wide
            out[at : at + SIDE, :] = (values * wide).astype(BF16)
    lane = lax.broadcasted_iota(jnp.int32, (16, 128), 1)
    listing = jnp.zeros((16, 128), F32)
    for side in range(8):
        listing = jnp.where(lane == side, place[0, side].astype(F32), listing)
    out[4 * STRIP_ROWS :, :] = listing.astype(BF16)


def strip_for(read, tile):
    strip = jnp.int32(0)
    for side in range(8):
        strip = jnp.where(read(side) == tile, STRIP_FOR[OPPOSITE[side]], strip)
    return pl.ds(pl.multiple_of(strip * STRIP_ROWS, STRIP_ROWS), STRIP_ROWS)


def relayed_strip(device, lists, paired, other, dest):
    group = lax.div(device[0], GROUP)
    use_pair = (dest < lax.rem(device[0], GROUP)) == (lax.rem(group, 2) == 1)
    rows = strip_for(lambda side: jnp.where(use_pair, lists[0, side], lists[1, side]), group * GROUP + dest)
    return jnp.where(use_pair, paired[rows, :], other[rows, :])


def relay_body(place, device, lists, own, paired, other, *out):
    group = lax.div(device[0], GROUP)
    mine = lax.rem(device[0], GROUP)
    for k in range(GROUP):
        if len(out) == 1:
            block, at, dest = out[0], 2 * k * STRIP_ROWS, k
        elif k:
            block, at, dest = out[k - 1], 0, mine ^ k
        else:
            continue
        rows = strip_for(lambda side: place[0, side], group * GROUP + dest)
        block[at : at + STRIP_ROWS, :] = own[rows, :]
        block[at + STRIP_ROWS : at + 2 * STRIP_ROWS, :] = relayed_strip(device, lists, paired, other, dest)


def core_body(
    place, device, fields, arrived, cotangent, mask, tap_table, conv_bias, ln_gain, ln_bias, weight_in,
    bias_in, weight_out, bias_out, layer_scale,
    updated_out, d_conv_out, strips, padded_out, d_weight_in, d_weight_out, d_bias_in, small,
    shifted, stage, taps, fields_in, arrived_in, cotangent_in, mask_in, updated, d_conv, padded,
    in_sems, out_sems, row_sems,
):
    loads = start_all(
        ((fields, fields_in), (arrived, arrived_in), (mask, mask_in), (cotangent, cotangent_in)), in_sems
    )
    mask, fields, arrived, cotangent = mask_in, fields_in, arrived_in, cotangent_in
    build_taps(tap_table, taps)
    for load in loads[:2]:
        load.wait()
    place_strips(picker(place, device, arrived, False), padded, stage)

    def fill(i, carry):
        padded[pl.ds((i + RADIUS) * PITCH + RADIUS, SIDE), :] = fields[i].astype(F32)
        return carry

    lax.fori_loop(0, SIDE, fill, 0)
    stores = start_all(((padded, padded_out),), out_sems)
    shift_copies(padded, shifted)
    for load in loads[2:]:
        load.wait()
    d_weight_in[...] = jnp.zeros_like(d_weight_in)
    d_weight_out[...] = jnp.zeros_like(d_weight_out)
    d_bias_in[...] = jnp.zeros_like(d_bias_in)
    small[...] = jnp.zeros_like(small)
    d_conv[...] = jnp.zeros_like(d_conv)
    half_in = weight_in[...] * jnp.bfloat16(0.5)
    half_bias = bias_in[...] * 0.5
    count = BLOCK // 2
    points = BLOCK * SIDE

    def by_half(ref, at):
        part = ref[pl.ds(at, BLOCK)].astype(F32).reshape(count, 2, SIDE, 128)
        return jnp.concatenate([part[:, 0], part[:, 1]], axis=0).reshape(points, 128)

    def by_row(value):
        part = value.reshape(2, count, SIDE, 128)
        return jnp.stack([part[0], part[1]], axis=1).reshape(BLOCK, SIDE, 128)

    def fold(value):
        return jnp.sum(value.reshape(-1, 8, value.shape[-1]), axis=0)

    def step(index, both, last=False):
        at = index * BLOCK
        conv = jnp.concatenate([both[:, :128], both[:, 128:]], axis=0) + conv_bias[...]
        following = both if last else conv_block(shifted, taps, (index + 1) * count, count)
        live = by_half(mask, at)
        signal = by_half(cotangent, at)
        centred = conv - jnp.mean(conv, axis=-1, keepdims=True)
        inv_std = lax.rsqrt(jnp.mean(centred * centred, axis=-1, keepdims=True) + EPS)
        normed = centred * inv_std
        lifted = (normed * ln_gain[...] + ln_bias[...]).astype(BF16)
        half = jnp.dot(lifted, half_in, preferred_element_type=F32) + half_bias
        square = half * half
        tanh_part = jnp.tanh(half * (2.0 * GELU_K + 8.0 * GELU_K * GELU_C * square))
        above = 1.0 + tanh_part
        activated = (half * above).astype(BF16)
        slope = above * (
            0.5 + (half * (GELU_K + 12.0 * GELU_K * GELU_C * square)) * (1.0 - tanh_part)
        )
        branch = jnp.dot(activated, weight_out[...], preferred_element_type=F32) + bias_out[...]
        d_branch = signal * layer_scale[...]
        branch_low = d_branch.astype(BF16)
        d_hidden = slope * lax.dot_general(
            branch_low, weight_out[...], CONTRACT_LAST, preferred_element_type=F32
        )
        hidden_low = d_hidden.astype(BF16)
        d_lifted = lax.dot_general(
            hidden_low, weight_in[...], CONTRACT_LAST, preferred_element_type=F32
        )
        d_normed = d_lifted * ln_gain[...]
        d_out = inv_std * (
            d_normed
            - jnp.mean(d_normed, axis=-1, keepdims=True)
            - normed * jnp.mean(d_normed * normed, axis=-1, keepdims=True)
        )
        masked = by_half(fields, at)
        updated[pl.ds(at, BLOCK)] = by_row(live * (masked + layer_scale[...] * branch)).astype(BF16)
        rows = by_row(d_out)
        for i in range(BLOCK):
            d_conv[pl.ds((at + i + RADIUS) * PITCH + RADIUS, SIDE), :] = rows[i]
        d_weight_out[...] += lax.dot_general(
            branch_low, activated, CONTRACT_ROWS, preferred_element_type=F32
        )
        d_weight_in[...] += lax.dot_general(
            lifted, hidden_low, CONTRACT_ROWS, preferred_element_type=F32
        )
        d_bias_in[...] += fold(d_hidden)
        small[0:8] += fold(signal * branch)
        small[8:16] += fold(d_branch)
        small[16:24] += fold(d_lifted * normed)
        small[24:32] += fold(d_lifted)
        small[32:40] += fold(d_out)
        for store in rows_out(index):
            store.start()
        return following

    def rows_out(index):
        rows = pl.ds(index * BLOCK, BLOCK)
        wide = pl.ds(pl.multiple_of((index * BLOCK + RADIUS) * PITCH, 8), BLOCK * PITCH)
        return (
            pltpu.make_async_copy(updated.at[rows], updated_out.at[rows], row_sems.at[0, index]),
            pltpu.make_async_copy(d_conv.at[wide], d_conv_out.at[wide], row_sems.at[1, index]),
        )

    both = conv_block(shifted, taps, 0, count)
    both = lax.fori_loop(0, SIDE // BLOCK - 1, step, both)
    step(SIDE // BLOCK - 1, both, last=True)
    edge = RADIUS * PITCH
    for i, rows in enumerate((pl.ds(0, edge), pl.ds(edge + SIDE * PITCH, edge))):
        store = pltpu.make_async_copy(d_conv.at[rows], d_conv_out.at[rows], out_sems.at[1 + i])
        store.start()
        stores.append(store)
    for r in range(RADIUS):
        corner = RADIUS * PITCH + RADIUS
        far = SIDE - RADIUS + r
        rows = (
            d_conv[corner + r * PITCH : corner + r * PITCH + SIDE, :],
            d_conv[corner + far * PITCH : corner + far * PITCH + SIDE, :],
            d_conv[pl.ds(corner + r, SIDE, stride=PITCH), :],
            d_conv[pl.ds(corner + far, SIDE, stride=PITCH), :],
        )
        for side in range(4):
            at = side * STRIP_ROWS + r * SIDE
            strips[at : at + SIDE, :] = rows[side].astype(BF16)
    for index in range(SIDE // BLOCK):
        stores += rows_out(index)
    for store in stores:
        store.wait()


def inner_body(
    scale, padded, d_conv, cotangent, mask, tap_table, d_weight_in, d_weight_out, d_bias_in, small,
    packed, d_fields_out, sums, shifted, taps, held, padded_in, d_conv_in, cotangent_in, mask_in, d_fields,
    in_sems, row_sems,
):
    loads = start_all(
        ((d_conv, d_conv_in), (padded, padded_in), (mask, mask_in), (cotangent, cotangent_in)), in_sems
    )
    d_conv, padded, mask, cotangent = d_conv_in, padded_in, mask_in, cotangent_in
    build_taps(tap_table, taps)
    loads[0].wait()
    shift_copies(d_conv, shifted)
    sums[...] = jnp.zeros_like(sums)
    for load in loads[1:]:
        load.wait()
    count = BLOCK // 2

    def step(index, carry):
        at = index * BLOCK
        both = conv_block(shifted, taps, index * count, count).reshape(count, SIDE, 256)
        for b in range(TAPS):
            part = [None] * TAPS
            for left in range(0, SIDE, 8):
                near = [
                    d_conv[pl.ds((at + i + RADIUS) * PITCH + RADIUS + left, 8), :] for i in range(BLOCK)
                ]
                for row in range(BLOCK + TAPS - 1):
                    piece = padded[pl.ds((at + row) * PITCH + left + b, 8), :]
                    for a in range(TAPS):
                        if 0 <= row - a < BLOCK:
                            term = piece * near[row - a]
                            part[a] = term if part[a] is None else part[a] + term
            for a in range(TAPS):
                sums[a * TAPS + b] += part[a]
        back = jnp.stack([both[:, :, :128], both[:, :, 128:]], axis=1).reshape(BLOCK, SIDE, 128)
        live = mask[pl.ds(at, BLOCK)].astype(F32)
        d_fields[pl.ds(at, BLOCK)] = live * (cotangent[pl.ds(at, BLOCK)].astype(F32) + back)
        rows_out(index).start()
        return carry

    def rows_out(index):
        rows = pl.ds(index * BLOCK, BLOCK)
        return pltpu.make_async_copy(d_fields.at[rows], d_fields_out.at[rows], row_sems.at[index])

    lax.fori_loop(0, SIDE // BLOCK, step, 0)
    for tile in range(4):
        across = slice(tile * 128, (tile + 1) * 128)
        held[tile * 128 : (tile + 1) * 128, :] = d_weight_in[:, across] * scale[0]
        held[512 + tile * 128 : 512 + (tile + 1) * 128, :] = d_weight_out[:, across].T * scale[0]
        at = AT_BIAS_IN + tile
        held[at : at + 1, :] = jnp.sum(d_bias_in[:, across], axis=0, keepdims=True) * scale[0]
    held[AT_KERNEL : AT_KERNEL + TAPS * TAPS, :] = jnp.sum(sums[...], axis=1) * scale[0]
    for i in range(5):
        at = AT_SMALL + i
        held[at : at + 1, :] = jnp.sum(small[8 * i : 8 * i + 8, :], axis=0, keepdims=True) * scale[0]
    held[AT_SMALL + 5 :, :] = jnp.zeros((held.shape[0] - AT_SMALL - 5, 128), F32)
    packed[...] = held[...].astype(packed.dtype)
    for index in range(SIDE // BLOCK):
        rows_out(index).wait()


def unpack_body(total, d_weight_in, d_weight_out, d_bias_in, d_kernel, *rest):
    small, held = rest[:5], rest[5]
    held[...] = total[...].astype(F32)
    for tile in range(4):
        across = slice(tile * 128, (tile + 1) * 128)
        d_weight_in[:, across] = held[tile * 128 : (tile + 1) * 128, :]
        at = AT_BIAS_IN + tile
        d_bias_in[:, across] = held[at : at + 1, :]
    d_weight_out[...] = held[512:1024, :]
    for a in range(TAPS):
        d_kernel[a] = held[AT_KERNEL + a * TAPS : AT_KERNEL + (a + 1) * TAPS, :]
    for i in range(5):
        small[i][...] = held[AT_SMALL + i : AT_SMALL + i + 1, :]


def edge_body(place, device, partial, a1, a2, a3, a4, a5, a6, a7, mask_strips, weights, d_fields,
              frame, columns, beside, top, bottom, left, right, sems, arrived, in_sems):
    waits = start_all(arrivals((a1, a2, a3, a4, a5, a6, a7), arrived), in_sems)
    arrived[0 : 2 * STRIP_ROWS, :] = jnp.zeros((2 * STRIP_ROWS, 128), BF16)
    inner = SIDE - 2 * RADIUS
    parts = (
        (top, (pl.ds(0, RADIUS),)),
        (bottom, (pl.ds(SIDE - RADIUS, RADIUS),)),
        (left, (pl.ds(RADIUS, inner), pl.ds(0, 8))),
        (right, (pl.ds(RADIUS, inner), pl.ds(SIDE - 8, 8))),
    )
    loads = [
        pltpu.make_async_copy(partial.at[where], held, sems.at[i])
        for i, (held, where) in enumerate(parts)
    ]
    for load in loads:
        load.start()
    pick = picker(place, device, arrived, True)
    frame[...] = jnp.zeros_like(frame)
    columns[...] = jnp.zeros_like(columns)
    for wait in waits:
        wait.wait()
    for r in range(RADIUS):
        frame[0, r, RADIUS : RADIUS + SIDE, :] = pick(0, r)
        frame[1, r, RADIUS : RADIUS + SIDE, :] = pick(1, r)
        columns[0, r, RADIUS : RADIUS + SIDE, :] = pick(2, r)
        columns[1, r, RADIUS : RADIUS + SIDE, :] = pick(3, r)
        frame[0, r, 0:RADIUS, :] = pick(4, r)[SIDE - RADIUS :]
        frame[0, r, RADIUS + SIDE : 2 * RADIUS + SIDE, :] = pick(5, r)[:RADIUS]
        frame[1, r, 0:RADIUS, :] = pick(6, r)[SIDE - RADIUS :]
        frame[1, r, RADIUS + SIDE : 2 * RADIUS + SIDE, :] = pick(7, r)[:RADIUS]

    def rim(source, far, line, at, tap):
        total = None
        for r in range(RADIUS):
            across = r + 6 - line if far else r - line
            if 0 <= across < TAPS:
                for along in range(TAPS):
                    term = source[far, r, pl.ds(at + along, 8), :] * tap(across, along)
                    total = term if total is None else total + term
        return total

    def weight_row(a, b):
        return weights[a * TAPS + b : a * TAPS + b + 1, :]

    for load in loads:
        load.wait()

    def along(step, carry):
        at = pl.multiple_of(step * 8, 8)
        for line in range(RADIUS):
            for far, held in ((0, top), (1, bottom)):
                live = mask_strips[far, line, pl.ds(at, 8), :]
                add = rim(frame, far, line, at, weight_row)
                held[line, pl.ds(at, 8), :] += live * add
            for far in range(2):
                live = mask_strips[2 + far, line, pl.ds(at, 8), :]
                add = rim(columns, far, line, at, lambda across, along: weight_row(along, across))
                beside[far, line, pl.ds(at, 8), :] = live * add
        return carry

    lax.fori_loop(0, SIDE // 8, along, 0)
    for far, held in ((0, left), (1, right)):
        flat = held.reshape(inner * 8, 128)
        for line in range(RADIUS):
            column = 5 + line if far else line
            flat[pl.ds(column, inner, stride=8), :] += beside[far, line, RADIUS : SIDE - RADIUS, :]
            place = SIDE - RADIUS + line if far else line
            for i in range(RADIUS):
                top[i, place : place + 1, :] += beside[far, line, i : i + 1, :]
                low = SIDE - RADIUS + i
                bottom[i, place : place + 1, :] += beside[far, line, low : low + 1, :]
    stores = [
        pltpu.make_async_copy(held, d_fields.at[where], sems.at[i])
        for i, (held, where) in enumerate(parts)
    ]
    for store in stores:
        store.start()
    for store in stores:
        store.wait()


MIB = 1024 * 1024
IN_VMEM = pl.BlockSpec(memory_space=pltpu.VMEM)
IN_SMEM = pl.BlockSpec(memory_space=pltpu.SMEM)
ANYWHERE = pl.BlockSpec(memory_space=pl.ANY)


def params(mib):
    return pltpu.CompilerParams(vmem_limit_bytes=mib * MIB)


def run_outgoing(place, fields, ocean_mask):
    return pl.pallas_call(
        outgoing_body,
        out_shape=(
            jax.ShapeDtypeStruct((4 * STRIP_ROWS + 16, 128), BF16),
            jax.ShapeDtypeStruct((4, RADIUS, SIDE, 128), F32),
        ),
        in_specs=[IN_SMEM] + [IN_VMEM] * 2,
        out_specs=(IN_VMEM,) * 2,
        scratch_shapes=[pltpu.VMEM((SIDE * 16, 128), F32)] * 2,
        compiler_params=params(64),
        name="outgoing",
    )(place, fields, ocean_mask)


def run_mask(ocean_mask, fields, cotangent):
    return pl.pallas_call(
        mask_body,
        out_shape=(jax.ShapeDtypeStruct((SIDE, SIDE, 128), BF16),) * 3,
        in_specs=[IN_VMEM] * 3,
        out_specs=(IN_VMEM,) * 3,
        compiler_params=params(64),
        cost_estimate=pl.CostEstimate(flops=4_000_000_000, bytes_accessed=1_000_000, transcendentals=0),
        name="mask",
    )(ocean_mask, fields, cotangent)


def run_relay(place, device, lists, own, paired, other, swapped):
    pair = 2 * STRIP_ROWS
    shapes = [(pair, 128)] * (GROUP - 1) if swapped else [(GROUP * pair, 128)]
    return pl.pallas_call(
        relay_body,
        out_shape=tuple(jax.ShapeDtypeStruct(shape, BF16) for shape in shapes),
        in_specs=[IN_SMEM] * 3 + [IN_VMEM] * 3,
        out_specs=(IN_VMEM,) * len(shapes),
        compiler_params=params(64),
        cost_estimate=pl.CostEstimate(flops=2_000_000_000, bytes_accessed=1_000_000, transcendentals=0),
        name="relay",
    )(place, device, lists, own, paired, other)


def run_core(place, device, fields, arrived, cotangent, mask, tap_table, vectors, weights):
    conv_bias, ln_gain, ln_bias, bias_in, bias_out, layer_scale = vectors
    weight_in, weight_out = weights
    shape = jax.ShapeDtypeStruct
    return pl.pallas_call(
        core_body,
        out_shape=(
            shape((SIDE, SIDE, 128), BF16),
            shape((ROWS * PITCH, 128), F32),
            shape((4 * STRIP_ROWS, 128), BF16),
            shape((ROWS * PITCH, 128), F32),
            shape((128, 512), F32),
            shape((128, 512), F32),
            shape((8, 512), F32),
            shape((40, 128), F32),
        ),
        in_specs=[IN_SMEM] * 2 + [ANYWHERE] * 4 + [IN_VMEM] * 9,
        out_specs=(ANYWHERE, ANYWHERE, IN_VMEM, ANYWHERE) + (IN_VMEM,) * 4,
        scratch_shapes=[
            pltpu.VMEM((TAPS, PAIRS, SIDE, 256), BF16),
            pltpu.VMEM((4 * SIDE, 128), F32),
            pltpu.VMEM((TAPS * 1024, 256), BF16),
            pltpu.VMEM((SIDE, SIDE, 128), BF16),
            pltpu.VMEM((2 * GROUP * STRIP_ROWS, 128), BF16),
            pltpu.VMEM((SIDE, SIDE, 128), BF16),
            pltpu.VMEM((SIDE, SIDE, 128), BF16),
            pltpu.VMEM((SIDE, SIDE, 128), BF16),
            pltpu.VMEM((ROWS * PITCH, 128), F32),
            pltpu.VMEM((ROWS * PITCH, 128), F32),
            pltpu.SemaphoreType.DMA((4,)),
            pltpu.SemaphoreType.DMA((3,)),
            pltpu.SemaphoreType.DMA((2, SIDE // BLOCK)),
        ],
        compiler_params=params(64),
        cost_estimate=pl.CostEstimate(flops=22_000_000_000, bytes_accessed=8_000_000, transcendentals=0),
        name="core",
    )(place, device, fields, arrived, cotangent, mask, tap_table, conv_bias, ln_gain, ln_bias,
      weight_in, bias_in, weight_out, bias_out, layer_scale)


def run_inner(rows, scale, padded, d_conv, cotangent, mask, tap_table, gradients):
    return pl.pallas_call(
        inner_body,
        out_shape=(
            jax.ShapeDtypeStruct((rows, 128), BF16),
            jax.ShapeDtypeStruct((SIDE, SIDE, 128), F32),
        ),
        in_specs=[IN_SMEM] + [ANYWHERE] * 4 + [IN_VMEM] * 5,
        out_specs=(IN_VMEM, ANYWHERE),
        scratch_shapes=[
            pltpu.VMEM((TAPS * TAPS, 8, 128), F32),
            pltpu.VMEM((TAPS, PAIRS, SIDE, 256), BF16),
            pltpu.VMEM((TAPS * 1024, 256), BF16),
            pltpu.VMEM((rows, 128), F32),
            pltpu.VMEM((ROWS * PITCH, 128), F32),
            pltpu.VMEM((ROWS * PITCH, 128), F32),
            pltpu.VMEM((SIDE, SIDE, 128), BF16),
            pltpu.VMEM((SIDE, SIDE, 128), BF16),
            pltpu.VMEM((SIDE, SIDE, 128), F32),
            pltpu.SemaphoreType.DMA((4,)),
            pltpu.SemaphoreType.DMA((SIDE // BLOCK,)),
        ],
        compiler_params=params(64),
        cost_estimate=pl.CostEstimate(flops=16_000_000_000, bytes_accessed=8_000_000, transcendentals=0),
        name="inner",
    )(scale, padded, d_conv, cotangent, mask, tap_table, *gradients)


def run_unpack(total):
    shape = jax.ShapeDtypeStruct
    return pl.pallas_call(
        unpack_body,
        out_shape=(
            shape((128, 512), F32),
            shape((512, 128), F32),
            shape((1, 512), F32),
            shape((TAPS, TAPS, 128), F32),
        )
        + (shape((1, 128), F32),) * 5,
        in_specs=[IN_VMEM],
        out_specs=(IN_VMEM,) * 9,
        scratch_shapes=[pltpu.VMEM(total.shape, F32)],
        compiler_params=params(6),
        name="unpack",
    )(total)


def run_edge(place, device, partial, arrived, mask_strips, weights):
    rim = pltpu.VMEM((RADIUS, SIDE, 128), F32)
    side = pltpu.VMEM((SIDE - 2 * RADIUS, 8, 128), F32)
    return pl.pallas_call(
        edge_body,
        out_shape=jax.ShapeDtypeStruct((SIDE, SIDE, 128), F32),
        in_specs=[IN_SMEM, IN_SMEM, ANYWHERE] + [ANYWHERE] * 7 + [IN_VMEM] * 2,
        out_specs=ANYWHERE,
        scratch_shapes=[
            pltpu.VMEM((2, RADIUS, PITCH, 128), F32),
            pltpu.VMEM((2, RADIUS, PITCH, 128), F32),
            pltpu.VMEM((2, RADIUS, SIDE, 128), F32),
            rim, rim, side, side,
            pltpu.SemaphoreType.DMA((4,)),
            pltpu.VMEM((2 * GROUP * STRIP_ROWS, 128), BF16),
            pltpu.SemaphoreType.DMA((GROUP - 1,)),
        ],
        input_output_aliases={2: 0},
        compiler_params=params(6),
        cost_estimate=pl.CostEstimate(flops=4_000_000_000, bytes_accessed=1_000_000, transcendentals=0),
        name="edge",
    )(place, device, partial, *arrived, mask_strips, weights)


def swap_groups(value):
    groups = lax.axis_size("tiles") // GROUP

    def swap(first):
        pairs = []
        for low in range(first, groups - 1, 2):
            for i in range(low * GROUP, (low + 1) * GROUP):
                pairs += [(i, i + GROUP), (i + GROUP, i)]
        return lax.ppermute(value, "tiles", pairs)

    return swap(0), swap(1)


def within_group(blocks):
    peers = lax.axis_size("tiles")
    groups = [list(range(g, g + GROUP)) for g in range(0, peers, GROUP)]
    blocks = blocks.reshape(GROUP, -1, 128)
    return lax.all_to_all(blocks, "tiles", 0, 0, axis_index_groups=groups).reshape(-1, 128)


def swap_within_group(blocks):
    peers = lax.axis_size("tiles")
    return [
        lax.ppermute(block, "tiles", [(i, i ^ k) for i in range(peers)])
        for k, block in enumerate(blocks, start=1)
    ]


def sum_over_tiles(packed, tie):
    peers = lax.axis_size("tiles")
    blocks = packed.reshape(peers, -1, 128)
    summed = jnp.sum(lax.all_to_all(blocks, "tiles", 0, 0).astype(F32), axis=0)
    summed, *tie = lax.optimization_barrier((summed, *tie))
    shared = jnp.broadcast_to(summed.astype(BF16)[None], blocks.shape)
    return lax.all_to_all(shared, "tiles", 0, 0).reshape(packed.shape), tie


def per_device(
    fields,
    cotangent,
    ocean_mask,
    neighbours,
    kernel,
    conv_bias,
    ln_gain,
    ln_bias,
    weight_in,
    bias_in,
    weight_out,
    bias_out,
    layer_scale,
):
    peers = lax.axis_size("tiles")
    device = lax.axis_index("tiles").astype(jnp.int32).reshape(1)
    own, mask_strips = run_outgoing(neighbours, fields[0], ocean_mask[0])
    paired, other = swap_groups(own)
    mask, masked, signal = run_mask(ocean_mask[0], fields[0], cotangent[0])
    lists = jnp.stack([paired[-16, :8], other[-16, :8]]).astype(jnp.int32)
    (blocks,) = run_relay(neighbours, device, lists, own, paired, other, False)
    arrived = within_group(blocks)
    vectors = [v.reshape(1, -1) for v in (conv_bias, ln_gain, ln_bias, bias_in, bias_out, layer_scale)]
    updated, d_conv, strips, padded, *gradients = run_core(
        neighbours, device, masked, arrived, signal, mask, tap_rows(kernel), vectors,
        (weight_in, weight_out),
    )
    paired, other = swap_groups(strips)
    flipped = kernel[::-1, ::-1]
    scale = jnp.full((1,), 1.0 / math.sqrt(peers * SIDE * SIDE), F32)
    rows = -(-PACKED_ROWS // (peers * 8)) * (peers * 8)
    packed, partial = run_inner(
        rows, scale, padded, d_conv, signal, mask, tap_rows(flipped), gradients
    )
    packed, paired, other = lax.optimization_barrier((packed, paired, other))
    arrived = swap_within_group(run_relay(neighbours, device, lists, strips, paired, other, True))
    weights = flipped.reshape(TAPS * TAPS, 128)
    total, arrived = sum_over_tiles(packed, arrived)
    d_fields = run_edge(neighbours, device, partial, arrived, mask_strips, weights)
    t_in, t_out, t_bias_in, t_kernel, *t_small = run_unpack(total)
    return (
        updated[None],
        d_fields[None],
        t_kernel,
        t_small[4][0],
        t_small[2][0],
        t_small[3][0],
        t_in,
        t_bias_in[0],
        t_out,
        t_small[1][0],
        t_small[0][0],
    )


def solution(mesh):
    placed = (
        P("tiles", None, None, None),
        P("tiles", None, None, None),
        P("tiles", None, None),
        P("tiles", None),
        P(),
        P(),
        P(),
        P(),
        P(),
        P(),
        P(),
        P(),
        P(),
    )
    return jax.shard_map(
        per_device,
        mesh=mesh,
        in_specs=placed,
        out_specs=(
            P("tiles", None, None, None),
            P("tiles", None, None, None),
            P(),
            P(),
            P(),
            P(),
            P(),
            P(),
            P(),
            P(),
            P(),
        ),
        check_vma=False,
    )
```

```python
import math

import jax
import jax.numpy as jnp
from jax import lax
from jax.experimental import pallas as pl
from jax.experimental.pallas import tpu as pltpu
from jax.sharding import PartitionSpec as P

EPS = 1e-06
GELU_K = 0.7978845608028654
GELU_C = 0.044715
CONTRACT_LAST = (((1,), (1,)), ((), ()))
CONTRACT_ROWS = (((0,), (0,)), ((), ()))
SIDE = 64
RADIUS = 3
STRIP_ROWS = RADIUS * SIDE
GROUP = 8
STRIP_FOR = (1, 0, 3, 2, 1, 1, 0, 0)
OPPOSITE = (1, 0, 3, 2, 7, 6, 5, 4)
TAPS = 7
PITCH = 72
ROWS = SIDE + 2 * RADIUS
PAIRS = ROWS // 2
BLOCK = 16
AT_KERNEL = 1024
AT_BIAS_IN = 1080
AT_SMALL = 1088
PACKED_ROWS = 1096
F32 = jnp.float32
BF16 = jnp.bfloat16


def tap_rows(kernel):
    wide = jnp.pad(kernel, ((1, 1), (0, 0), (0, 0)))
    both = jnp.concatenate([wide[1:9], wide[0:8]], axis=2)
    return jnp.pad(both.transpose(1, 0, 2).reshape(TAPS * 8, 256), ((0, 8), (0, 0)))


def build_taps(rows, taps):
    shape = (128, 256)
    across = lax.broadcasted_iota(jnp.int32, shape, 1)
    down = lax.broadcasted_iota(jnp.int32, shape, 0)
    eye = ((across == down) | (across == down + 128)).astype(F32)

    def body(tap, carry):
        for position in range(8):
            at = tap * 8 + position
            taps[pl.ds(pl.multiple_of(at * 128, 128), 128), :] = (eye * rows[pl.ds(at, 1), :]).astype(BF16)
        return carry

    lax.fori_loop(0, TAPS, body, 0)


def place_strips(pick, padded, stage):
    for r in range(RADIUS):
        padded[r * PITCH + RADIUS : r * PITCH + RADIUS + SIDE, :] = pick(0, r)
        low = (RADIUS + SIDE + r) * PITCH
        padded[low + RADIUS : low + RADIUS + SIDE, :] = pick(1, r)
        padded[pl.ds(RADIUS * PITCH + r, SIDE, stride=PITCH), :] = pick(2, r)
        padded[pl.ds(RADIUS * PITCH + RADIUS + SIDE + r, SIDE, stride=PITCH), :] = pick(3, r)
        stage[0:SIDE, :] = pick(4, r)
        padded[r * PITCH : r * PITCH + RADIUS, :] = stage[SIDE - RADIUS : SIDE, :]
        stage[SIDE : 2 * SIDE, :] = pick(5, r)
        padded[r * PITCH + RADIUS + SIDE : r * PITCH + 2 * RADIUS + SIDE, :] = stage[SIDE : SIDE + RADIUS, :]
        stage[2 * SIDE : 3 * SIDE, :] = pick(6, r)
        padded[low : low + RADIUS, :] = stage[3 * SIDE - RADIUS : 3 * SIDE, :]
        stage[3 * SIDE : 4 * SIDE, :] = pick(7, r)
        padded[low + RADIUS + SIDE : low + 2 * RADIUS + SIDE, :] = stage[3 * SIDE : 3 * SIDE + RADIUS, :]


def shift_copies(padded, shifted):
    def body(pair, carry):
        for half in range(2):
            at = (2 * pair + half) * PITCH
            for tap in range(TAPS):
                row = padded[pl.ds(at + tap, SIDE), :].astype(BF16)
                shifted[tap, pair, :, half * 128 : (half + 1) * 128] = row
        return carry

    lax.fori_loop(0, PAIRS, body, 0)


def conv_block(shifted, taps, first, count):
    total = None
    for tap in range(TAPS):
        rows = [
            shifted[tap, pl.ds(first + move, count)].reshape(count * SIDE, 256) for move in range(4)
        ]
        part = jnp.dot(
            jnp.concatenate(rows, axis=1),
            taps[tap * 1024 : (tap + 1) * 1024, :],
            preferred_element_type=F32,
        )
        total = part if total is None else total + part
    return total


def picker(place, device, arrived, swapped):
    group = lax.div(device[0], GROUP)
    mine = lax.rem(device[0], GROUP)

    def pick(side, r):
        tile = place[0, side]
        owner = jnp.maximum(tile, 0)
        source = lax.rem(owner, GROUP)
        slot = 2 * (source ^ mine if swapped else source) + jnp.where(lax.div(owner, GROUP) != group, 1, 0)
        at = pl.multiple_of(slot * STRIP_ROWS + r * SIDE, SIDE)
        return jnp.where(tile >= 0, arrived[pl.ds(at, SIDE), :].astype(F32), 0.0)

    return pick


def arrivals(blocks, held):
    pairs = []
    for k in range(1, GROUP):
        pairs.append((blocks[k - 1], held.at[pl.ds(2 * k * STRIP_ROWS, 2 * STRIP_ROWS)]))
    return tuple(pairs)


def start_all(pairs, sems):
    copies = [pltpu.make_async_copy(src, dst, sems.at[i]) for i, (src, dst) in enumerate(pairs)]
    for copy in copies:
        copy.start()
    return copies


def mask_body(ocean_mask, fields, cotangent, mask, masked, signal):
    across = ocean_mask[...].astype(F32).T
    for i in range(SIDE):
        live = jnp.broadcast_to(across[:, i : i + 1], (SIDE, 128))
        mask[i] = live.astype(BF16)
        masked[i] = (fields[i].astype(F32) * live).astype(BF16)
        signal[i] = (cotangent[i].astype(F32) * live).astype(BF16)


def outgoing_body(place, fields, ocean_mask, out, mask_strips, near, far):
    def fill(i, carry):
        near[pl.ds(i * 16, 16), :] = fields[i, 0:16, :].astype(F32)
        far[pl.ds(i * 16, 16), :] = fields[i, SIDE - 16 : SIDE, :].astype(F32)
        return carry

    lax.fori_loop(0, SIDE, fill, 0, unroll=4)
    live = ocean_mask[...].astype(F32)
    across = live.T
    for r in range(RADIUS):
        back = SIDE - RADIUS + r
        rows = (
            (fields[r].astype(F32), across[:, r : r + 1]),
            (fields[back].astype(F32), across[:, back : back + 1]),
            (near[pl.ds(r, SIDE, stride=16), :], live[:, r : r + 1]),
            (far[pl.ds(16 - RADIUS + r, SIDE, stride=16), :], live[:, back : back + 1]),
        )
        for side, (values, column) in enumerate(rows):
            at = side * STRIP_ROWS + r * SIDE
            wide = jnp.broadcast_to(column, (SIDE, 128))
            mask_strips[side, r] = wide
            out[at : at + SIDE, :] = (values * wide).astype(BF16)
    lane = lax.broadcasted_iota(jnp.int32, (16, 128), 1)
    listing = jnp.zeros((16, 128), F32)
    for side in range(8):
        listing = jnp.where(lane == side, place[0, side].astype(F32), listing)
    out[4 * STRIP_ROWS :, :] = listing.astype(BF16)


def strip_for(read, tile):
    strip = jnp.int32(0)
    for side in range(8):
        strip = jnp.where(read(side) == tile, STRIP_FOR[OPPOSITE[side]], strip)
    return pl.ds(pl.multiple_of(strip * STRIP_ROWS, STRIP_ROWS), STRIP_ROWS)


def relayed_strip(device, lists, paired, other, dest):
    group = lax.div(device[0], GROUP)
    use_pair = (dest < lax.rem(device[0], GROUP)) == (lax.rem(group, 2) == 1)
    rows = strip_for(lambda side: jnp.where(use_pair, lists[0, side], lists[1, side]), group * GROUP + dest)
    return jnp.where(use_pair, paired[rows, :], other[rows, :])


def relay_body(place, device, lists, own, paired, other, *out):
    group = lax.div(device[0], GROUP)
    mine = lax.rem(device[0], GROUP)
    for k in range(GROUP):
        if len(out) == 1:
            block, at, dest = out[0], 2 * k * STRIP_ROWS, k
        elif k:
            block, at, dest = out[k - 1], 0, mine ^ k
        else:
            continue
        rows = strip_for(lambda side: place[0, side], group * GROUP + dest)
        block[at : at + STRIP_ROWS, :] = own[rows, :]
        block[at + STRIP_ROWS : at + 2 * STRIP_ROWS, :] = relayed_strip(device, lists, paired, other, dest)


def core_body(
    place, device, fields, arrived, cotangent, mask, tap_table, conv_bias, ln_gain, ln_bias, weight_in,
    bias_in, weight_out, bias_out, layer_scale,
    updated_out, d_conv_out, strips, padded_out, d_weight_in, d_weight_out, d_bias_in, small,
    shifted, stage, taps, fields_in, arrived_in, cotangent_in, mask_in, updated, d_conv, padded,
    in_sems, out_sems, row_sems,
):
    loads = start_all(
        ((fields, fields_in), (arrived, arrived_in), (mask, mask_in), (cotangent, cotangent_in)), in_sems
    )
    mask, fields, arrived, cotangent = mask_in, fields_in, arrived_in, cotangent_in
    build_taps(tap_table, taps)
    for load in loads[:2]:
        load.wait()
    place_strips(picker(place, device, arrived, False), padded, stage)

    def fill(i, carry):
        padded[pl.ds((i + RADIUS) * PITCH + RADIUS, SIDE), :] = fields[i].astype(F32)
        return carry

    lax.fori_loop(0, SIDE, fill, 0)
    stores = start_all(((padded.at[pl.ds(0, ROWS * PITCH)], padded_out),), out_sems)
    shift_copies(padded, shifted)
    for load in loads[2:]:
        load.wait()
    d_weight_in[...] = jnp.zeros_like(d_weight_in)
    d_weight_out[...] = jnp.zeros_like(d_weight_out)
    d_bias_in[...] = jnp.zeros_like(d_bias_in)
    small[...] = jnp.zeros_like(small)
    d_conv[...] = jnp.zeros_like(d_conv)
    half_in = weight_in[...] * jnp.bfloat16(0.5)
    half_bias = bias_in[...] * 0.5
    count = BLOCK // 2
    points = BLOCK * SIDE

    def by_half(ref, at):
        part = ref[pl.ds(at, BLOCK)].astype(F32).reshape(count, 2, SIDE, 128)
        return jnp.concatenate([part[:, 0], part[:, 1]], axis=0).reshape(points, 128)

    def by_row(value):
        part = value.reshape(2, count, SIDE, 128)
        return jnp.stack([part[0], part[1]], axis=1).reshape(BLOCK, SIDE, 128)

    def fold(value):
        return jnp.sum(value.reshape(-1, 8, value.shape[-1]), axis=0)

    def step(index, both, last=False):
        at = index * BLOCK
        conv = jnp.concatenate([both[:, :128], both[:, 128:]], axis=0) + conv_bias[...]
        following = both if last else conv_block(shifted, taps, (index + 1) * count, count)
        live = by_half(mask, at)
        signal = by_half(cotangent, at)
        centred = conv - jnp.mean(conv, axis=-1, keepdims=True)
        inv_std = lax.rsqrt(jnp.mean(centred * centred, axis=-1, keepdims=True) + EPS)
        normed = centred * inv_std
        lifted = (normed * ln_gain[...] + ln_bias[...]).astype(BF16)
        half = jnp.dot(lifted, half_in, preferred_element_type=F32) + half_bias
        square = half * half
        tanh_part = jnp.tanh(half * (2.0 * GELU_K + 8.0 * GELU_K * GELU_C * square))
        above = 1.0 + tanh_part
        activated = (half * above).astype(BF16)
        slope = above * (
            0.5 + (half * (GELU_K + 12.0 * GELU_K * GELU_C * square)) * (1.0 - tanh_part)
        )
        branch = jnp.dot(activated, weight_out[...], preferred_element_type=F32) + bias_out[...]
        d_branch = signal * layer_scale[...]
        branch_low = d_branch.astype(BF16)
        d_hidden = slope * lax.dot_general(
            branch_low, weight_out[...], CONTRACT_LAST, preferred_element_type=F32
        )
        hidden_low = d_hidden.astype(BF16)
        d_lifted = lax.dot_general(
            hidden_low, weight_in[...], CONTRACT_LAST, preferred_element_type=F32
        )
        d_normed = d_lifted * ln_gain[...]
        d_out = inv_std * (
            d_normed
            - jnp.mean(d_normed, axis=-1, keepdims=True)
            - normed * jnp.mean(d_normed * normed, axis=-1, keepdims=True)
        )
        masked = by_half(fields, at)
        updated[pl.ds(at, BLOCK)] = by_row(live * (masked + layer_scale[...] * branch)).astype(BF16)
        rows = by_row(d_out)
        for i in range(BLOCK):
            d_conv[pl.ds((at + i + RADIUS) * PITCH + RADIUS, SIDE), :] = rows[i]
        d_weight_out[...] += lax.dot_general(
            branch_low, activated, CONTRACT_ROWS, preferred_element_type=F32
        )
        d_weight_in[...] += lax.dot_general(
            lifted, hidden_low, CONTRACT_ROWS, preferred_element_type=F32
        )
        d_bias_in[...] += fold(d_hidden)
        small[0:8] += fold(signal * branch)
        small[8:16] += fold(d_branch)
        small[16:24] += fold(d_lifted * normed)
        small[24:32] += fold(d_lifted)
        small[32:40] += fold(d_out)
        for store in rows_out(index):
            store.start()
        return following

    def rows_out(index):
        rows = pl.ds(index * BLOCK, BLOCK)
        wide = pl.ds(pl.multiple_of((index * BLOCK + RADIUS) * PITCH, 8), BLOCK * PITCH)
        return (
            pltpu.make_async_copy(updated.at[rows], updated_out.at[rows], row_sems.at[0, index]),
            pltpu.make_async_copy(d_conv.at[wide], d_conv_out.at[wide], row_sems.at[1, index]),
        )

    both = conv_block(shifted, taps, 0, count)
    both = lax.fori_loop(0, SIDE // BLOCK - 1, step, both)
    step(SIDE // BLOCK - 1, both, last=True)
    edge = RADIUS * PITCH
    for i, rows in enumerate((pl.ds(0, edge), pl.ds(edge + SIDE * PITCH, edge))):
        store = pltpu.make_async_copy(d_conv.at[rows], d_conv_out.at[rows], out_sems.at[1 + i])
        store.start()
        stores.append(store)
    for r in range(RADIUS):
        corner = RADIUS * PITCH + RADIUS
        far = SIDE - RADIUS + r
        rows = (
            d_conv[corner + r * PITCH : corner + r * PITCH + SIDE, :],
            d_conv[corner + far * PITCH : corner + far * PITCH + SIDE, :],
            d_conv[pl.ds(corner + r, SIDE, stride=PITCH), :],
            d_conv[pl.ds(corner + far, SIDE, stride=PITCH), :],
        )
        for side in range(4):
            at = side * STRIP_ROWS + r * SIDE
            strips[at : at + SIDE, :] = rows[side].astype(BF16)
    for index in range(SIDE // BLOCK):
        stores += rows_out(index)
    for store in stores:
        store.wait()


def inner_body(
    scale, padded, d_conv, cotangent, mask, tap_table, d_weight_in, d_weight_out, d_bias_in, small,
    packed, d_fields_out, sums, shifted, taps, held, padded_in, d_conv_in, cotangent_in, mask_in, d_fields,
    in_sems, row_sems,
):
    loads = start_all(
        ((d_conv, d_conv_in), (padded, padded_in), (mask, mask_in), (cotangent, cotangent_in)), in_sems
    )
    d_conv, padded, mask, cotangent = d_conv_in, padded_in, mask_in, cotangent_in
    build_taps(tap_table, taps)
    loads[0].wait()
    shift_copies(d_conv, shifted)
    sums[...] = jnp.zeros_like(sums)
    for load in loads[1:]:
        load.wait()
    count = BLOCK // 2

    def step(index, carry):
        at = index * BLOCK
        both = conv_block(shifted, taps, index * count, count).reshape(count, SIDE, 256)
        for b in range(TAPS):
            part = [None] * TAPS
            for left in range(0, SIDE, 8):
                near = [
                    d_conv[pl.ds((at + i + RADIUS) * PITCH + RADIUS + left, 8), :] for i in range(BLOCK)
                ]
                for row in range(BLOCK + TAPS - 1):
                    piece = padded[pl.ds((at + row) * PITCH + left + b, 8), :]
                    for a in range(TAPS):
                        if 0 <= row - a < BLOCK:
                            term = piece * near[row - a]
                            part[a] = term if part[a] is None else part[a] + term
            for a in range(TAPS):
                sums[a * TAPS + b] += part[a]
        back = jnp.stack([both[:, :, :128], both[:, :, 128:]], axis=1).reshape(BLOCK, SIDE, 128)
        live = mask[pl.ds(at, BLOCK)].astype(F32)
        d_fields[pl.ds(at, BLOCK)] = live * (cotangent[pl.ds(at, BLOCK)].astype(F32) + back)
        rows_out(index).start()
        return carry

    def rows_out(index):
        rows = pl.ds(index * BLOCK, BLOCK)
        return pltpu.make_async_copy(d_fields.at[rows], d_fields_out.at[rows], row_sems.at[index])

    lax.fori_loop(0, SIDE // BLOCK, step, 0)
    for tile in range(4):
        across = slice(tile * 128, (tile + 1) * 128)
        held[tile * 128 : (tile + 1) * 128, :] = d_weight_in[:, across] * scale[0]
        held[512 + tile * 128 : 512 + (tile + 1) * 128, :] = d_weight_out[:, across].T * scale[0]
        at = AT_BIAS_IN + tile
        held[at : at + 1, :] = jnp.sum(d_bias_in[:, across], axis=0, keepdims=True) * scale[0]
    held[AT_KERNEL : AT_KERNEL + TAPS * TAPS, :] = jnp.sum(sums[...], axis=1) * scale[0]
    for i in range(5):
        at = AT_SMALL + i
        held[at : at + 1, :] = jnp.sum(small[8 * i : 8 * i + 8, :], axis=0, keepdims=True) * scale[0]
    held[AT_SMALL + 5 :, :] = jnp.zeros((held.shape[0] - AT_SMALL - 5, 128), F32)
    packed[...] = held[0 : packed.shape[0], :].astype(packed.dtype)
    for index in range(SIDE // BLOCK):
        rows_out(index).wait()


def unpack_body(total, d_weight_in, d_weight_out, d_bias_in, d_kernel, *rest):
    small, held = rest[:5], rest[5]
    held[...] = total[...].astype(F32)
    for tile in range(4):
        across = slice(tile * 128, (tile + 1) * 128)
        d_weight_in[:, across] = held[tile * 128 : (tile + 1) * 128, :]
        at = AT_BIAS_IN + tile
        d_bias_in[:, across] = held[at : at + 1, :]
    d_weight_out[...] = held[512:1024, :]
    for a in range(TAPS):
        d_kernel[a] = held[AT_KERNEL + a * TAPS : AT_KERNEL + (a + 1) * TAPS, :]
    for i in range(5):
        small[i][...] = held[AT_SMALL + i : AT_SMALL + i + 1, :]


def edge_body(place, device, partial, a1, a2, a3, a4, a5, a6, a7, mask_strips, weights, d_fields,
              frame, columns, beside, top, bottom, left, right, sems, arrived, in_sems):
    waits = start_all(arrivals((a1, a2, a3, a4, a5, a6, a7), arrived), in_sems)
    arrived[0 : 2 * STRIP_ROWS, :] = jnp.zeros((2 * STRIP_ROWS, 128), BF16)
    inner = SIDE - 2 * RADIUS
    parts = (
        (top.at[pl.ds(0, RADIUS)], (pl.ds(0, RADIUS),)),
        (bottom.at[pl.ds(0, RADIUS)], (pl.ds(SIDE - RADIUS, RADIUS),)),
        (left.at[pl.ds(0, inner)], (pl.ds(RADIUS, inner), pl.ds(0, 8))),
        (right.at[pl.ds(0, inner)], (pl.ds(RADIUS, inner), pl.ds(SIDE - 8, 8))),
    )
    loads = [
        pltpu.make_async_copy(partial.at[where], held, sems.at[i])
        for i, (held, where) in enumerate(parts)
    ]
    for load in loads:
        load.start()
    pick = picker(place, device, arrived, True)
    frame[...] = jnp.zeros_like(frame)
    columns[...] = jnp.zeros_like(columns)
    for wait in waits:
        wait.wait()
    for r in range(RADIUS):
        frame[0, r, RADIUS : RADIUS + SIDE, :] = pick(0, r)
        frame[1, r, RADIUS : RADIUS + SIDE, :] = pick(1, r)
        columns[0, r, RADIUS : RADIUS + SIDE, :] = pick(2, r)
        columns[1, r, RADIUS : RADIUS + SIDE, :] = pick(3, r)
        frame[0, r, 0:RADIUS, :] = pick(4, r)[SIDE - RADIUS :]
        frame[0, r, RADIUS + SIDE : 2 * RADIUS + SIDE, :] = pick(5, r)[:RADIUS]
        frame[1, r, 0:RADIUS, :] = pick(6, r)[SIDE - RADIUS :]
        frame[1, r, RADIUS + SIDE : 2 * RADIUS + SIDE, :] = pick(7, r)[:RADIUS]

    def rim(source, far, line, at, tap):
        total = None
        for r in range(RADIUS):
            across = r + 6 - line if far else r - line
            if 0 <= across < TAPS:
                for along in range(TAPS):
                    term = source[far, r, pl.ds(at + along, 8), :] * tap(across, along)
                    total = term if total is None else total + term
        return total

    def weight_row(a, b):
        return weights[a * TAPS + b : a * TAPS + b + 1, :]

    for load in loads:
        load.wait()

    def along(step, carry):
        at = pl.multiple_of(step * 8, 8)
        for line in range(RADIUS):
            for far, held in ((0, top), (1, bottom)):
                live = mask_strips[far, line, pl.ds(at, 8), :]
                add = rim(frame, far, line, at, weight_row)
                held[line, pl.ds(at, 8), :] += live * add
            for far in range(2):
                live = mask_strips[2 + far, line, pl.ds(at, 8), :]
                add = rim(columns, far, line, at, lambda across, along: weight_row(along, across))
                beside[far, line, pl.ds(at, 8), :] = live * add
        return carry

    lax.fori_loop(0, SIDE // 8, along, 0)
    for far, held in ((0, left), (1, right)):
        flat = held.reshape(SIDE * 8, 128)
        for line in range(RADIUS):
            column = 5 + line if far else line
            flat[pl.ds(column, inner, stride=8), :] += beside[far, line, RADIUS : SIDE - RADIUS, :]
            place = SIDE - RADIUS + line if far else line
            for i in range(RADIUS):
                top[i, place : place + 1, :] += beside[far, line, i : i + 1, :]
                low = SIDE - RADIUS + i
                bottom[i, place : place + 1, :] += beside[far, line, low : low + 1, :]
    stores = [
        pltpu.make_async_copy(held, d_fields.at[where], sems.at[i])
        for i, (held, where) in enumerate(parts)
    ]
    for store in stores:
        store.start()
    for store in stores:
        store.wait()


MIB = 1024 * 1024
IN_VMEM = pl.BlockSpec(memory_space=pltpu.VMEM)
IN_SMEM = pl.BlockSpec(memory_space=pltpu.SMEM)
ANYWHERE = pl.BlockSpec(memory_space=pl.ANY)


def params(mib):
    return pltpu.CompilerParams(vmem_limit_bytes=mib * MIB)


def run_outgoing(place, fields, ocean_mask):
    return pl.pallas_call(
        outgoing_body,
        out_shape=(
            jax.ShapeDtypeStruct((4 * STRIP_ROWS + 16, 128), BF16),
            jax.ShapeDtypeStruct((4, RADIUS, SIDE, 128), F32),
        ),
        in_specs=[IN_SMEM] + [IN_VMEM] * 2,
        out_specs=(IN_VMEM,) * 2,
        scratch_shapes=[pltpu.VMEM((SIDE * 16, 128), F32)] * 2,
        compiler_params=params(64),
        name="outgoing",
    )(place, fields, ocean_mask)


def run_mask(ocean_mask, fields, cotangent):
    return pl.pallas_call(
        mask_body,
        out_shape=(jax.ShapeDtypeStruct((SIDE, SIDE, 128), BF16),) * 3,
        in_specs=[IN_VMEM] * 3,
        out_specs=(IN_VMEM,) * 3,
        compiler_params=params(64),
        cost_estimate=pl.CostEstimate(flops=4_000_000_000, bytes_accessed=1_000_000, transcendentals=0),
        name="mask",
    )(ocean_mask, fields, cotangent)


def run_relay(place, device, lists, own, paired, other, swapped):
    pair = 2 * STRIP_ROWS
    shapes = [(pair, 128)] * (GROUP - 1) if swapped else [(GROUP * pair, 128)]
    return pl.pallas_call(
        relay_body,
        out_shape=tuple(jax.ShapeDtypeStruct(shape, BF16) for shape in shapes),
        in_specs=[IN_SMEM] * 3 + [IN_VMEM] * 3,
        out_specs=(IN_VMEM,) * len(shapes),
        compiler_params=params(64),
        cost_estimate=pl.CostEstimate(flops=2_000_000_000, bytes_accessed=1_000_000, transcendentals=0),
        name="relay",
    )(place, device, lists, own, paired, other)


def run_core(place, device, fields, arrived, cotangent, mask, tap_table, vectors, weights):
    conv_bias, ln_gain, ln_bias, bias_in, bias_out, layer_scale = vectors
    weight_in, weight_out = weights
    shape = jax.ShapeDtypeStruct
    return pl.pallas_call(
        core_body,
        out_shape=(
            shape((SIDE, SIDE, 128), BF16),
            shape((ROWS * PITCH, 128), F32),
            shape((4 * STRIP_ROWS, 128), BF16),
            shape((ROWS * PITCH, 128), F32),
            shape((128, 512), F32),
            shape((128, 512), F32),
            shape((8, 512), F32),
            shape((40, 128), F32),
        ),
        in_specs=[IN_SMEM] * 2 + [ANYWHERE] * 4 + [IN_VMEM] * 9,
        out_specs=(ANYWHERE, ANYWHERE, IN_VMEM, ANYWHERE) + (IN_VMEM,) * 4,
        scratch_shapes=[
            pltpu.VMEM((TAPS, PAIRS, SIDE, 256), BF16),
            pltpu.VMEM((4 * SIDE, 128), F32),
            pltpu.VMEM((TAPS * 1024, 256), BF16),
            pltpu.VMEM((SIDE, SIDE, 128), BF16),
            pltpu.VMEM((2 * GROUP * STRIP_ROWS, 128), BF16),
            pltpu.VMEM((SIDE, SIDE, 128), BF16),
            pltpu.VMEM((SIDE, SIDE, 128), BF16),
            pltpu.VMEM((SIDE, SIDE, 128), BF16),
            pltpu.VMEM((ROWS * PITCH + 8, 128), F32),
            pltpu.VMEM((ROWS * PITCH + 8, 128), F32),
            pltpu.SemaphoreType.DMA((4,)),
            pltpu.SemaphoreType.DMA((3,)),
            pltpu.SemaphoreType.DMA((2, SIDE // BLOCK)),
        ],
        compiler_params=params(64),
        cost_estimate=pl.CostEstimate(flops=22_000_000_000, bytes_accessed=8_000_000, transcendentals=0),
        name="core",
    )(place, device, fields, arrived, cotangent, mask, tap_table, conv_bias, ln_gain, ln_bias,
      weight_in, bias_in, weight_out, bias_out, layer_scale)


def run_inner(rows, scale, padded, d_conv, cotangent, mask, tap_table, gradients):
    return pl.pallas_call(
        inner_body,
        out_shape=(
            jax.ShapeDtypeStruct((rows, 128), BF16),
            jax.ShapeDtypeStruct((SIDE, SIDE, 128), F32),
        ),
        in_specs=[IN_SMEM] + [ANYWHERE] * 4 + [IN_VMEM] * 5,
        out_specs=(IN_VMEM, ANYWHERE),
        scratch_shapes=[
            pltpu.VMEM((TAPS * TAPS, 8, 128), F32),
            pltpu.VMEM((TAPS, PAIRS, SIDE, 256), BF16),
            pltpu.VMEM((TAPS * 1024, 256), BF16),
            pltpu.VMEM((rows + 8, 128), F32),
            pltpu.VMEM((ROWS * PITCH, 128), F32),
            pltpu.VMEM((ROWS * PITCH, 128), F32),
            pltpu.VMEM((SIDE, SIDE, 128), BF16),
            pltpu.VMEM((SIDE, SIDE, 128), BF16),
            pltpu.VMEM((SIDE, SIDE, 128), F32),
            pltpu.SemaphoreType.DMA((4,)),
            pltpu.SemaphoreType.DMA((SIDE // BLOCK,)),
        ],
        compiler_params=params(64),
        cost_estimate=pl.CostEstimate(flops=16_000_000_000, bytes_accessed=8_000_000, transcendentals=0),
        name="inner",
    )(scale, padded, d_conv, cotangent, mask, tap_table, *gradients)


def run_unpack(total):
    shape = jax.ShapeDtypeStruct
    return pl.pallas_call(
        unpack_body,
        out_shape=(
            shape((128, 512), F32),
            shape((512, 128), F32),
            shape((1, 512), F32),
            shape((TAPS, TAPS, 128), F32),
        )
        + (shape((1, 128), F32),) * 5,
        in_specs=[IN_VMEM],
        out_specs=(IN_VMEM,) * 9,
        scratch_shapes=[pltpu.VMEM(total.shape, F32)],
        compiler_params=params(6),
        name="unpack",
    )(total)


def run_edge(place, device, partial, arrived, mask_strips, weights):
    rim = pltpu.VMEM((RADIUS + 1, SIDE, 128), F32)
    side = pltpu.VMEM((SIDE, 8, 128), F32)
    return pl.pallas_call(
        edge_body,
        out_shape=jax.ShapeDtypeStruct((SIDE, SIDE, 128), F32),
        in_specs=[IN_SMEM, IN_SMEM, ANYWHERE] + [ANYWHERE] * 7 + [IN_VMEM] * 2,
        out_specs=ANYWHERE,
        scratch_shapes=[
            pltpu.VMEM((2, RADIUS, PITCH + 8, 128), F32),
            pltpu.VMEM((2, RADIUS, PITCH + 8, 128), F32),
            pltpu.VMEM((2, RADIUS, SIDE + 8, 128), F32),
            rim, rim, side, side,
            pltpu.SemaphoreType.DMA((4,)),
            pltpu.VMEM((2 * GROUP * STRIP_ROWS, 128), BF16),
            pltpu.SemaphoreType.DMA((GROUP - 1,)),
        ],
        input_output_aliases={2: 0},
        compiler_params=params(6),
        cost_estimate=pl.CostEstimate(flops=4_000_000_000, bytes_accessed=1_000_000, transcendentals=0),
        name="edge",
    )(place, device, partial, *arrived, mask_strips, weights)


def swap_groups(value):
    groups = lax.axis_size("tiles") // GROUP

    def swap(first):
        pairs = []
        for low in range(first, groups - 1, 2):
            for i in range(low * GROUP, (low + 1) * GROUP):
                pairs += [(i, i + GROUP), (i + GROUP, i)]
        return lax.ppermute(value, "tiles", pairs)

    return swap(0), swap(1)


def within_group(blocks):
    peers = lax.axis_size("tiles")
    groups = [list(range(g, g + GROUP)) for g in range(0, peers, GROUP)]
    blocks = blocks.reshape(GROUP, -1, 128)
    return lax.all_to_all(blocks, "tiles", 0, 0, axis_index_groups=groups).reshape(-1, 128)


def swap_within_group(blocks):
    peers = lax.axis_size("tiles")
    return [
        lax.ppermute(block, "tiles", [(i, i ^ k) for i in range(peers)])
        for k, block in enumerate(blocks, start=1)
    ]


def sum_over_tiles(packed, tie):
    peers = lax.axis_size("tiles")
    blocks = packed.reshape(peers, -1, 128)
    summed = jnp.sum(lax.all_to_all(blocks, "tiles", 0, 0).astype(F32), axis=0)
    summed, *tie = lax.optimization_barrier((summed, *tie))
    shared = jnp.broadcast_to(summed.astype(BF16)[None], blocks.shape)
    return lax.all_to_all(shared, "tiles", 0, 0).reshape(packed.shape), tie


def per_device(
    fields,
    cotangent,
    ocean_mask,
    neighbours,
    kernel,
    conv_bias,
    ln_gain,
    ln_bias,
    weight_in,
    bias_in,
    weight_out,
    bias_out,
    layer_scale,
):
    peers = lax.axis_size("tiles")
    device = lax.axis_index("tiles").astype(jnp.int32).reshape(1)
    own, mask_strips = run_outgoing(neighbours, fields[0], ocean_mask[0])
    paired, other = swap_groups(own)
    mask, masked, signal = run_mask(ocean_mask[0], fields[0], cotangent[0])
    lists = jnp.stack([paired[-16, :8], other[-16, :8]]).astype(jnp.int32)
    (blocks,) = run_relay(neighbours, device, lists, own, paired, other, False)
    arrived = within_group(blocks)
    vectors = [v.reshape(1, -1) for v in (conv_bias, ln_gain, ln_bias, bias_in, bias_out, layer_scale)]
    updated, d_conv, strips, padded, *gradients = run_core(
        neighbours, device, masked, arrived, signal, mask, tap_rows(kernel), vectors,
        (weight_in, weight_out),
    )
    paired, other = swap_groups(strips)
    flipped = kernel[::-1, ::-1]
    scale = jnp.full((1,), 1.0 / math.sqrt(peers * SIDE * SIDE), F32)
    rows = -(-PACKED_ROWS // (peers * 8)) * (peers * 8)
    packed, partial = run_inner(
        rows, scale, padded, d_conv, signal, mask, tap_rows(flipped), gradients
    )
    packed, paired, other = lax.optimization_barrier((packed, paired, other))
    arrived = swap_within_group(run_relay(neighbours, device, lists, strips, paired, other, True))
    weights = jnp.pad(flipped.reshape(TAPS * TAPS, 128), ((0, 15), (0, 0)))
    total, arrived = sum_over_tiles(packed, arrived)
    d_fields = run_edge(neighbours, device, partial, arrived, mask_strips, weights)
    t_in, t_out, t_bias_in, t_kernel, *t_small = run_unpack(total)
    return (
        updated[None],
        d_fields[None],
        t_kernel,
        t_small[4][0],
        t_small[2][0],
        t_small[3][0],
        t_in,
        t_bias_in[0],
        t_out,
        t_small[1][0],
        t_small[0][0],
    )


def solution(mesh):
    placed = (
        P("tiles", None, None, None),
        P("tiles", None, None, None),
        P("tiles", None, None),
        P("tiles", None),
        P(),
        P(),
        P(),
        P(),
        P(),
        P(),
        P(),
        P(),
        P(),
    )
    return jax.shard_map(
        per_device,
        mesh=mesh,
        in_specs=placed,
        out_specs=(
            P("tiles", None, None, None),
            P("tiles", None, None, None),
            P(),
            P(),
            P(),
            P(),
            P(),
            P(),
            P(),
            P(),
            P(),
        ),
        check_vma=False,
    )
```
